32 devices in a mesh: seq: 16 (over z, y, x), tp: 2 (over core).
Axes of the slice: x: 2, y: 2, z: 4, core: 2. Of those that a mesh axis runs over, the one named last changes fastest.
Arguments:
- tokens: bfloat16 [2048, 2048], P('seq'), may hold values from -6 to 6
- attn_gain: bfloat16 [2048], P('seq'), may hold values from 0.099609375 to 1.8984375
- q_gain: bfloat16 [1024], P('seq'), may hold values from 0.099609375 to 1.8984375
- w_qdown: bfloat16 [2048, 1024], P('seq'), may hold values from -0.125 to 0.125
- w_qup: bfloat16 [1024, 4096], P('seq', 'tp'), may hold values from -0.1875 to 0.1875
- w_kv: bfloat16 [2048, 512], P('seq'), may hold values from -0.125 to 0.125
- w_out: bfloat16 [4096, 2048], P('tp', 'seq'), may hold values from -2 to 2
- mlp_gain: bfloat16 [2048], P('seq'), may hold values from 0.099609375 to 1.8984375
- w_gate: bfloat16 [2048, 5632], P('seq', 'tp'), may hold values from -0.125 to 0.125
- w_up: bfloat16 [2048, 5632], P('seq', 'tp'), may hold values from -0.125 to 0.125
- w_down: bfloat16 [5632, 2048], P('tp', 'seq'), may hold values from -0.078125 to 0.078125
- cotangent: bfloat16 [2048, 2048], P('seq'), may hold values from -6 to 6
- seq_lengths: int32 [4], replicated, may hold values from 64 to 1152, as said below
- block_slots: int32 [32], replicated, may hold values from 0 to 31, as said below
Outputs:
- layer_out: bfloat16 [2048, 2048], P('seq')
- token_grad: bfloat16 [2048, 2048], P('seq')
- attn_gain_grad: float32 [2048], P('seq')
- q_gain_grad: float32 [1024], P('seq')
- w_qdown_grad: float32 [2048, 1024], P('seq')
- w_qup_grad: float32 [1024, 4096], P('seq', 'tp')
- w_kv_grad: float32 [2048, 512], P('seq')
- w_out_grad: float32 [4096, 2048], P('tp', 'seq')
- mlp_gain_grad: float32 [2048], P('seq')
- w_gate_grad: float32 [2048, 5632], P('seq', 'tp')
- w_up_grad: float32 [2048, 5632], P('seq', 'tp')
- w_down_grad: float32 [5632, 2048], P('tp', 'seq')
The draws below stay inside these ranges and needn't reach their ends.
Inputs may be any that keep to these rules, and one draw needn't show every extreme that they name: `seq_lengths`: the 4 lengths sum to 2048; either the first or the last sequence has exactly 1152 tokens, and the other lengths are shorter. `block_slots`: every block appears once; the slots 2 i and 2 i + 1 hold blocks c and 31 - c for some c below 16.
All inputs are finite; a program needn't handle non-finite values.
Results may differ from the reference program's by a relative error of at most 0.023.
Values may be sent and summed in bfloat16 or wider, within the bound.
No kernel may reach another device: no remote copies, remote signals or barrier semaphores. Data moves between devices by JAX's collectives and lax.ppermute only.
A program may use at most 256 MiB of HBM per device.

```python
import math
import jax
import jax.numpy as jnp
from jax import lax

D = 2048
RQ = 1024
H = 16
HD = 256
FF = 5632
BLOCK_ROWS = 64
SLOTS = 32
TOKENS = 2048


def draw_seq_lengths(key, part):
    key = jax.random.fold_in(key, 11)
    place_key, second_key, third_key = jax.random.split(key, 3)
    longest = 9 * TOKENS // 16
    remainder = TOKENS - longest
    spread = remainder // 8
    share_each = remainder // 3
    second_len = share_each + jax.random.randint(second_key, (), -spread, spread + 1)
    third_len = share_each + jax.random.randint(third_key, (), -spread, spread + 1)
    fourth_len = remainder - second_len - third_len
    at_end = jax.random.randint(place_key, (), 0, 2)
    leading = jnp.stack([jnp.int32(longest), second_len, third_len, fourth_len])
    trailing = jnp.stack([second_len, third_len, fourth_len, jnp.int32(longest)])
    return jnp.where(at_end == 1, trailing, leading).astype(jnp.int32)


def draw_block_slots(key, part):
    key = jax.random.fold_in(key, 23)
    shuffled = jax.random.permutation(key, SLOTS // 2).astype(jnp.int32)
    return jnp.stack([shuffled, SLOTS - 1 - shuffled], axis=1).reshape(SLOTS).astype(jnp.int32)


def level_of(own_key, dims, cuts, low, largest):
    factor_of = 1.0
    for axis_at, parts in cuts:
        heights = jax.random.uniform(jax.random.fold_in(jax.random.fold_in(own_key, 6), axis_at), (parts,), jnp.float32, low / len(cuts), largest / len(cuts))
        factor_of = factor_of * jnp.repeat(jnp.exp(heights), dims[axis_at] // parts).reshape((-1,) + (1,) * (len(dims) - 1 - axis_at))
    return factor_of


def noise(stream_key, dims, deviation, reach, shards=(), held_as=jnp.bfloat16):
    loudness = level_of(stream_key, dims, shards, -0.22, 0.18) if shards else 1.0
    values = jax.random.normal(stream_key, dims, jnp.float32) * deviation * loudness
    return jnp.minimum(jnp.maximum(values, -reach), reach).astype(held_as)


def setup_inputs(seed: int = 0) -> dict:
    splits = jax.random.split(jax.random.key(seed), 15)
    return {
        "tokens": noise(splits[0], (TOKENS, D), 1.0, 6.0, ((0, 16),)),
        "attn_gain": jnp.clip(1.0 + 0.18 * jax.random.normal(splits[1], (D,), jnp.float32), 0.099609375, 1.8984375).astype(jnp.bfloat16),
        "q_gain": jnp.clip(1.0 + 0.18 * jax.random.normal(splits[2], (RQ,), jnp.float32), 0.099609375, 1.8984375).astype(jnp.bfloat16),
        "w_qdown": noise(splits[3], (D, RQ), D ** -0.5, 0.125, ((0, 16),)),
        "w_qup": noise(splits[4], (RQ, H * HD), RQ ** -0.5, 0.1875, ((0, 16), (1, 2))),
        "w_kv": noise(splits[5], (D, 2 * HD), D ** -0.5, 0.125, ((0, 16),)),
        "w_out": noise(splits[6], (H * HD, D), (max(1, H * HD // 512)) ** -0.5, 2.0, ((0, 2), (1, 16))),
        "mlp_gain": jnp.clip(1.0 + 0.18 * jax.random.normal(splits[7], (D,), jnp.float32), 0.099609375, 1.8984375).astype(jnp.bfloat16),
        "w_gate": noise(splits[8], (D, FF), D ** -0.5, 0.125, ((0, 16), (1, 2))),
        "w_up": noise(splits[9], (D, FF), D ** -0.5, 0.125, ((0, 16), (1, 2))),
        "w_down": noise(splits[10], (FF, D), FF ** -0.5, 0.078125, ((0, 2), (1, 16))),
        "cotangent": noise(splits[11], (TOKENS, D), 1.0, 6.0, ((0, 16),)),
        "seq_lengths": draw_seq_lengths(jax.random.fold_in(splits[14], 71), 0),
        "block_slots": draw_block_slots(jax.random.fold_in(splits[14], 71), 0),
    }


EPSILON = 1e-06
ROPE_BASE = 10000.0
MASKED = -1e+30
HIGHEST_PRECISION = lax.Precision.HIGHEST

@jax.custom_vjp
def low(v):
    return lax.optimization_barrier(v.astype(jnp.bfloat16)).astype(jnp.float32)

@jax.custom_vjp
def low_back(v):
    return v

def low_keep(v):
    return (low(v), None)

def low_pass(kept, grad):
    return (grad,)

def back_keep(v):
    return (v, None)

def back_low(kept, grad):
    return (low(grad),)
low.defvjp(low_keep, low_pass)
low_back.defvjp(back_keep, back_low)

def layout(seq_lengths, block_slots, block_rows):
    slot_count = block_slots.shape[0]
    natural = jnp.repeat(block_slots, block_rows) * block_rows + jnp.tile(jnp.arange(block_rows, dtype=jnp.int32), slot_count)
    natural = natural.astype(jnp.int32)
    bounds = jnp.cumsum(seq_lengths).astype(jnp.int32)
    starts = (bounds - seq_lengths).astype(jnp.int32)
    member = (natural[:, None] >= starts[None, :]) & (natural[:, None] < bounds[None, :])
    numbers = jnp.arange(seq_lengths.shape[0], dtype=jnp.int32)
    doc_ids = lax.optimization_barrier(jnp.sum(jnp.where(member, numbers[None, :], 0), axis=1)).astype(jnp.int32)
    offset = lax.optimization_barrier(jnp.sum(jnp.where(member, starts[None, :], 0), axis=1)).astype(jnp.int32)
    return (natural, doc_ids, (natural - offset).astype(jnp.int32))

def angles(position, width):
    half_width = width // 2
    frequency = jnp.exp(jnp.arange(half_width, dtype=jnp.float32) * (-math.log(ROPE_BASE) / half_width))
    phase_angle = position.astype(jnp.float32)[:, None] * frequency[None, :]
    return (jnp.cos(phase_angle), jnp.sin(phase_angle))

def rotate(vector, cosine, sine_table):
    half_width = vector.shape[-1] // 2
    front_half = vector[..., :half_width]
    back_half = vector[..., half_width:]
    return jnp.concatenate([front_half * cosine - back_half * sine_table, back_half * cosine + front_half * sine_table], axis=-1)

def product(left, right):
    return jnp.dot(left, right, precision=HIGHEST_PRECISION, preferred_element_type=jnp.float32)

def inverse_rms(vector):
    return lax.rsqrt(lax.optimization_barrier(jnp.mean(vector * vector, axis=-1, keepdims=True)) + EPSILON)

def reference(tokens, attn_gain, q_gain, w_qdown, w_qup, w_kv, w_out, mlp_gain, w_gate, w_up, w_down, cotangent, seq_lengths, block_slots):
    natural, doc_ids, position = layout(seq_lengths, block_slots, BLOCK_ROWS)
    cosine, sine_table = angles(position, HD)
    query_rows = math.gcd(TOKENS, 256)
    blocks = TOKENS // query_rows
    score_scale = HD ** (-0.5)

    def layer(inputs, gain_attn, gain_query, down_query, up_query, key_value, out_proj, gain_mlp, gate_proj, up_weight, down_weight):
        x_hat = inputs * inverse_rms(inputs)
        x_norm = low(x_hat * gain_attn)
        q_lat = low_back(product(x_norm, down_query))
        q_norm = low(q_lat * inverse_rms(q_lat) * gain_query)
        q_pre = low_back(product(q_norm, up_query)).reshape(TOKENS, H, HD)
        queries = low(rotate(q_pre, cosine[:, None, :], sine_table[:, None, :]))
        kv_pre = low_back(product(x_norm, key_value))
        keys_rot = low(rotate(kv_pre[:, :HD], cosine, sine_table))
        values = low(kv_pre[:, HD:])

        def attend(query_block):
            q_rows, q_natural, q_doc = query_block
            allowed = (q_doc[:, None] == doc_ids[None, :]) & (natural[None, :] <= q_natural[:, None])
            scores = low_back(jnp.einsum('qhd,kd->hqk', q_rows, keys_rot, precision=HIGHEST_PRECISION) * score_scale)
            masked = jnp.where(allowed[None], scores, MASKED)
            row_max = lax.optimization_barrier(jnp.max(masked, axis=-1, keepdims=True))
            exp_terms = jnp.where(allowed[None], jnp.exp(masked - row_max), 0.0)
            probs = exp_terms / lax.optimization_barrier(jnp.sum(exp_terms, axis=-1, keepdims=True))
            return jnp.einsum('hqk,kd->qhd', low(probs), values, precision=HIGHEST_PRECISION)
        attn_mix = lax.map(jax.checkpoint(attend), (queries.reshape(blocks, query_rows, H, HD), natural.reshape(blocks, query_rows), doc_ids.reshape(blocks, query_rows)))
        o_low = low(low_back(attn_mix.reshape(TOKENS, H * HD)))
        hidden = inputs + low_back(product(o_low, out_proj))
        h_norm = low(hidden * inverse_rms(hidden) * gain_mlp)
        gate_act = low_back(product(h_norm, gate_proj))
        up_proj = low_back(product(h_norm, up_weight))
        hidden_act = low(jax.nn.silu(gate_act) * up_proj)
        return hidden + low_back(product(hidden_act, down_weight))
    primals = tuple((arg.astype(jnp.float32) for arg in (tokens, attn_gain, q_gain, w_qdown, w_qup, w_kv, w_out, mlp_gain, w_gate, w_up, w_down)))
    result, pullback = jax.vjp(layer, *primals)
    grads = pullback(cotangent.astype(jnp.float32))
    return (result.astype(jnp.bfloat16), grads[0].astype(jnp.bfloat16), grads[1], grads[2], grads[3], grads[4], grads[5], grads[6], grads[7], grads[8], grads[9], grads[10])
```

```python
import functools
import math

import jax
import jax.numpy as jnp
from jax import lax
from jax.experimental import pallas as pl
from jax.experimental.pallas import tpu as pltpu
from jax.sharding import PartitionSpec as P

EPSILON = 1e-06
ROPE_BASE = 10000.0
MASKED = -1e30
HEAD = 256
SQUARE = 4
VMEM_LIMIT = 56 * 1024 * 1024
BF16 = jnp.bfloat16
F32 = jnp.float32


def matmul(left, right):
    return jnp.dot(left, right, preferred_element_type=F32)


def contract_rows(left, right):
    return lax.dot_general(left, right, (((0,), (0,)), ((), ())), preferred_element_type=F32)


def times_transposed(left, right):
    return lax.dot_general(left, right, (((1,), (1,)), ((), ())), preferred_element_type=F32)


def inverse_rms(vector):
    return lax.rsqrt(jnp.mean(vector * vector, axis=-1, keepdims=True) + EPSILON)


def norm_back(scaled_grad, normed, inverse):
    return inverse * (scaled_grad - normed * jnp.mean(scaled_grad * normed, axis=-1, keepdims=True))


def angles(position):
    half = HEAD // 2
    frequency = jnp.exp(jnp.arange(half, dtype=F32) * (-math.log(ROPE_BASE) / half))
    phase = position.astype(F32)[:, None] * frequency[None, :]
    return jnp.cos(phase), jnp.sin(phase)


def rotate(vector, cosine, sine):
    half = HEAD // 2
    front, back = vector[:, :half], vector[:, half:]
    return jnp.concatenate([front * cosine - back * sine, back * cosine + front * sine], axis=1)


def unrotate(vector, cosine, sine):
    return rotate(vector, cosine, -sine)


def masked_scores(q, k, row_natural, row_start, key_natural):
    scores = times_transposed(q, k)
    allowed = (key_natural <= row_natural) & (key_natural >= row_start)
    return scores, allowed


def attend_kernel(q_ref, natural_ref, start_ref, kv_ref, keys_ref, o_ref, lse_ref):
    scores, allowed = masked_scores(
        q_ref[...], kv_ref[:, :HEAD], natural_ref[...], start_ref[...], keys_ref[...]
    )
    scores = jnp.where(allowed, scores, MASKED)
    top = jnp.max(scores, axis=-1, keepdims=True)
    terms = jnp.exp(scores - top)
    total = jnp.sum(terms, axis=-1, keepdims=True)
    o_ref[...] = matmul(terms.astype(BF16), kv_ref[:, HEAD:]) / total
    lse_ref[...] = top + jnp.log(total)


def attend(q, natural, start, kv, keys, block):
    rows, count = q.shape[0], kv.shape[0]
    row = lambda width: pl.BlockSpec((block, width), lambda i: (i, 0))
    whole = lambda shape: pl.BlockSpec(shape, lambda i: (0, 0))
    return pl.pallas_call(
        attend_kernel,
        grid=(rows // block,),
        in_specs=[row(HEAD), row(1), row(1), whole((count, 2 * HEAD)), whole((1, count))],
        out_specs=[row(HEAD), row(1)],
        out_shape=[
            jax.ShapeDtypeStruct((rows, HEAD), F32),
            jax.ShapeDtypeStruct((rows, 1), F32),
        ],
        compiler_params=pltpu.CompilerParams(vmem_limit_bytes=VMEM_LIMIT),
        cost_estimate=pl.CostEstimate(
            flops=4 * rows * count * HEAD, bytes_accessed=4 * count * HEAD, transcendentals=rows * count
        ),
        name="attend",
    )(q, natural, start, kv, keys)


def attend_back_kernel(
    q_ref, natural_ref, start_ref, kv_ref, keys_ref, o_ref, lse_ref, do_ref, dq_ref, dkv_ref
):
    scores, allowed = masked_scores(
        q_ref[...], kv_ref[:, :HEAD], natural_ref[...], start_ref[...], keys_ref[...]
    )
    probs = jnp.exp(jnp.where(allowed, scores - lse_ref[...], MASKED))
    d_o = do_ref[...]
    delta = jnp.sum(d_o.astype(F32) * o_ref[...], axis=-1, keepdims=True)
    d_probs = times_transposed(d_o, kv_ref[:, HEAD:])
    d_scores = (probs * (d_probs - delta)).astype(BF16)
    dq_ref[...] = matmul(d_scores, kv_ref[:, :HEAD]) * HEAD**-0.5

    @pl.when(pl.program_id(0) == 0)
    def _():
        dkv_ref[...] = jnp.zeros_like(dkv_ref)

    dkv_ref[:, :HEAD] += contract_rows(d_scores, q_ref[...])
    dkv_ref[:, HEAD:] += contract_rows(probs.astype(BF16), d_o)


def attend_back(q, natural, start, kv, keys, o, lse, d_o, block):
    rows, count = q.shape[0], kv.shape[0]
    row = lambda width: pl.BlockSpec((block, width), lambda i: (i, 0))
    whole = lambda shape: pl.BlockSpec(shape, lambda i: (0, 0))
    return pl.pallas_call(
        attend_back_kernel,
        grid=(rows // block,),
        in_specs=[
            row(HEAD),
            row(1),
            row(1),
            whole((count, 2 * HEAD)),
            whole((1, count)),
            row(HEAD),
            row(1),
            row(HEAD),
        ],
        out_specs=[row(HEAD), whole((count, 2 * HEAD))],
        out_shape=[
            jax.ShapeDtypeStruct((rows, HEAD), F32),
            jax.ShapeDtypeStruct((count, 2 * HEAD), F32),
        ],
        compiler_params=pltpu.CompilerParams(vmem_limit_bytes=VMEM_LIMIT),
        cost_estimate=pl.CostEstimate(
            flops=10 * rows * count * HEAD, bytes_accessed=12 * count * HEAD, transcendentals=rows * count
        ),
        name="attend_back",
    )(q, natural, start, kv, keys, o, lse, d_o)


def local(
    chips,
    tokens,
    attn_gain,
    q_gain,
    w_qdown,
    w_qup,
    w_kv,
    w_out,
    mlp_gain,
    w_gate,
    w_up,
    w_down,
    cotangent,
    seq_lengths,
    block_slots,
):
    layers = chips // SQUARE
    rows, width = tokens.shape[0] // 2, tokens.shape[1]
    lanes = width // chips
    rank = w_qdown.shape[1]
    rank_rows = w_qup.shape[0]
    heads_half = w_qup.shape[1] // HEAD
    heads = 2 * heads_half
    sharing = chips // heads
    units = w_gate.shape[1] // chips
    squares = range(SQUARE // sharing)
    half = HEAD // 2
    place = lax.axis_index("seq")
    core = lax.axis_index("tp")
    layer, corner = place // SQUARE, place % SQUARE
    first = core == 0

    def across(value):
        return lax.ppermute(value, "tp", [(0, 1), (1, 0)])

    def along(value, step):
        pairs = [
            (z * SQUARE + c, (z + step) % layers * SQUARE + c)
            for z in range(layers)
            for c in range(SQUARE)
        ]
        return lax.ppermute(value, "seq", pairs)

    def within(value, flip):
        return lax.ppermute(value, "seq", [(i, i ^ flip) for i in range(chips)])

    def gather(value, flips=range(SQUARE)):
        column = jnp.stack([value] + [along(value, k) for k in range(1, layers)])
        return [column if m == 0 else within(column, m) for m in flips]

    def scatter(pieces):
        total = sum(
            (piece if m == 0 else within(piece, m)).astype(F32) for m, piece in enumerate(pieces)
        )
        low = total.astype(BF16)
        return total[0] + sum(along(low[k], -k).astype(F32) for k in range(1, layers))

    def own(pair_value):
        return lax.dynamic_slice_in_dim(pair_value, core * rows, rows, 0)

    def others(pair_value):
        return lax.dynamic_slice_in_dim(pair_value, (1 - core) * rows, rows, 0)

    def both(mine, theirs, axis=0):
        return jnp.concatenate(
            [jnp.where(first, mine, theirs), jnp.where(first, theirs, mine)], axis=axis
        )

    def half_of(value, which, axis):
        size = value.shape[axis] // 2
        low_half = lax.slice_in_dim(value, 0, size, axis=axis)
        high_half = lax.slice_in_dim(value, size, 2 * size, axis=axis)
        return jnp.where(which == 0, low_half, high_half)

    bounds = jnp.cumsum(seq_lengths)
    starts = bounds - seq_lengths

    def layout(blocks):
        natural = (blocks[:, None] * rows + jnp.arange(rows, dtype=jnp.int32)[None, :]).reshape(-1)
        member = (natural[:, None] >= starts[None, :]) & (natural[:, None] < bounds[None, :])
        return natural, jnp.sum(jnp.where(member, starts[None, :], 0), axis=1)

    back_steps = jnp.arange(layers, dtype=jnp.int32)
    owners = jnp.concatenate(
        [((layer - back_steps) % layers) * SQUARE + (corner ^ m) for m in range(SQUARE)]
    )
    row_natural, row_start = layout(block_slots[2 * owners + core])
    far_natural, _ = layout(block_slots[2 * owners + 1 - core])
    key_natural = jnp.concatenate([row_natural, far_natural])[None, :]
    row_cos, row_sin = angles(row_natural - row_start)
    own_cos, own_sin = row_cos[:rows], row_sin[:rows]
    live = len(squares) * layers * rows
    q_cos, q_sin = row_cos[:live], row_sin[:live]
    q_natural, q_start = row_natural[:live, None], row_start[:live, None]

    gain_rows = attn_gain.astype(F32)[:, None]
    down = jnp.concatenate([w_qdown, w_kv], axis=1)
    down_scaled = (down.astype(F32) * gain_rows).astype(BF16)
    columns = down.shape[1] // 2
    down_own = half_of(down_scaled, core, 1)

    def put(parts, indices):
        stacked = jnp.zeros((len(parts),) + parts[0].shape, parts[0].dtype)
        for part, index in zip(parts, indices):
            stacked = lax.dynamic_update_index_in_dim(stacked, part, index, 0)
        return stacked

    down_line = put(
        [down_own] + [along(down_own, k) for k in range(1, layers)],
        [(layer - k) % layers for k in range(layers)],
    )
    down_full = put(
        [down_line] + [within(down_line, m) for m in range(1, SQUARE)],
        [corner ^ m for m in range(SQUARE)],
    ).reshape(width, columns)

    def to_placed(value):
        shaped = value.reshape(value.shape[0], layers, SQUARE, lanes)
        return jnp.swapaxes(shaped, 1, 2).reshape(value.shape[0], width)

    def from_placed(value):
        shaped = value.reshape(value.shape[0], SQUARE, layers, lanes)
        return jnp.swapaxes(shaped, 1, 2).reshape(value.shape[0], width)

    inputs = tokens.astype(F32)
    x_inverse = inverse_rms(inputs)
    x_hat = inputs * x_inverse
    x_low = to_placed(x_hat.astype(BF16))

    q_gain_rows = q_gain.astype(F32)[:, None]
    mlp_gain_rows = mlp_gain.astype(F32)[:, None]
    gate_up = jnp.concatenate([w_gate, w_up], axis=1)
    gate_up_scaled = (gate_up.astype(F32) * mlp_gain_rows).astype(BF16).T
    mlp_out = jnp.concatenate([gate_up_scaled, w_down]).reshape(3, chips, units, lanes)
    mlp_out = jnp.swapaxes(mlp_out, 0, 1).reshape(chips, 3 * units, lanes)

    qup_scaled = (w_qup.astype(F32) * q_gain_rows).astype(BF16)
    qup_heads = qup_scaled.reshape(rank_rows, heads_half, 2, half)
    qup_heads = jnp.transpose(qup_heads, (2, 1, 0, 3))
    out_heads = jnp.swapaxes(w_out.reshape(heads_half, 2, half, lanes), 0, 1)

    def of_core(value, which):
        return lax.dynamic_index_in_dim(value, which, 0, keepdims=False)

    qup_mine = both(of_core(qup_heads, core), across(of_core(qup_heads, 1 - core)))
    out_mine = both(of_core(out_heads, core), across(of_core(out_heads, 1 - core)))
    attn_out = jnp.concatenate(
        [qup_mine.reshape(heads, -1, lanes), out_mine.reshape(heads, -1, lanes)], axis=1
    )
    attn_out = jnp.repeat(attn_out, sharing, axis=0)

    def exchange(value):
        return lax.all_to_all(value, "seq", 0, 0, tiled=True)

    attn_in = exchange(attn_out)
    qup_size = rank_rows * half // lanes
    qup_half = attn_in[:, :qup_size].reshape(rank, half)
    out_half = jnp.swapaxes(attn_in[:, qup_size:], 0, 1).reshape(half, width)
    qup_head = both(qup_half, across(qup_half), axis=1)
    out_head = both(out_half, across(out_half), axis=0)

    mlp_in = jnp.swapaxes(exchange(mlp_out), 0, 1).reshape(3, units, width)
    mlp_far = across(mlp_in)
    gate_up_units = jnp.concatenate([mlp_in[0], mlp_far[0], mlp_in[1], mlp_far[1]])
    down_units = jnp.concatenate([mlp_in[2], mlp_far[2]])

    cot_own = own(cotangent)
    cot_pieces = gather(cot_own)

    part = matmul(x_low, down_full)
    mine, theirs = own(part), across(others(part))
    projected = both(mine, theirs, axis=1)
    q_lat, kv_pre = projected[:, :rank], projected[:, rank:]
    lat_inverse = inverse_rms(q_lat)
    lat_hat = q_lat * lat_inverse
    kv_own = jnp.concatenate([rotate(kv_pre[:, :HEAD], own_cos, own_sin), kv_pre[:, HEAD:]], axis=1)
    latent_pieces = gather(jnp.concatenate([lat_hat, kv_own], axis=1).astype(BF16))
    lat_all = jnp.concatenate([latent_pieces[m][..., :rank] for m in squares]).reshape(live, rank)
    kv_near = jnp.concatenate([piece[..., rank:] for piece in latent_pieces])
    kv_near = kv_near.reshape(-1, 2 * HEAD)
    kv_all = jnp.concatenate([kv_near, across(kv_near)])

    queries = rotate(matmul(lat_all, qup_head), q_cos, q_sin).astype(BF16)
    queries = queries * jnp.asarray(HEAD**-0.5, BF16)
    block = max(64, min(256, 256 * 2048 // kv_all.shape[0]))
    attn_mix, log_total = attend(queries, q_natural, q_start, kv_all, key_natural, block)
    o_low = attn_mix.astype(BF16)

    def cut(value):
        return value.reshape(len(squares), layers, rows, value.shape[-1])

    attn_pieces = cut(matmul(o_low, out_head).astype(BF16))
    hidden = own(inputs) + scatter([attn_pieces[m] for m in squares])
    h_inverse = inverse_rms(hidden)
    h_hat = hidden * h_inverse

    piece_rows = layers * rows
    h_pieces = [piece.reshape(piece_rows, width) for piece in gather(h_hat.astype(BF16))]
    cot_pieces = [piece.reshape(piece_rows, width) for piece in cot_pieces]
    chip_units = 2 * units
    mlp_parts, d_h_parts, act_parts, d_gate_up_parts = [], [], [], []
    for h_piece, cot_piece in zip(h_pieces, cot_pieces):
        d_act = times_transposed(cot_piece, down_units)
        both_act = times_transposed(h_piece, gate_up_units)
        gate_act, up_proj = both_act[:, :chip_units], both_act[:, chip_units:]
        sigmoid_gate = jax.nn.sigmoid(gate_act)
        silu_gate = gate_act * sigmoid_gate
        act = (silu_gate * up_proj).astype(BF16)
        d_gate = d_act * up_proj * sigmoid_gate * (1.0 + gate_act * (1.0 - sigmoid_gate))
        d_up = d_act * silu_gate
        d_gate_up = jnp.concatenate([d_gate, d_up], axis=1).astype(BF16)
        d_h_parts.append(matmul(d_gate_up, gate_up_units).astype(BF16).reshape(layers, rows, width))
        mlp_parts.append(matmul(act, down_units).astype(BF16).reshape(layers, rows, width))
        act_parts.append(act)
        d_gate_up_parts.append(d_gate_up)
    d_hscaled = scatter(d_h_parts)
    layer_own = (hidden + scatter(mlp_parts)).astype(BF16)
    layer_out = both(layer_own, across(layer_own))

    out_grad = cot_own.astype(F32)
    d_hidden = out_grad + norm_back(d_hscaled, h_hat, h_inverse)
    d_attn = d_hidden.astype(BF16)
    d_attn_pieces = gather(d_attn, squares)

    h_all, cot_all = jnp.concatenate(h_pieces), jnp.concatenate(cot_pieces)
    grad_gate_up = contract_rows(jnp.concatenate(d_gate_up_parts), h_all)
    grad_down = contract_rows(jnp.concatenate(act_parts), cot_all)
    mlp_grads = jnp.concatenate([grad_gate_up, grad_down]).reshape(3, 2, units, width)
    mlp_sum = mlp_grads[:, 0] + across(mlp_grads[:, 1].astype(BF16)).astype(F32)
    mlp_sum = mlp_sum.astype(BF16).reshape(3 * units, chips, lanes)
    mlp_back = exchange(jnp.swapaxes(mlp_sum, 0, 1))
    mlp_back = jnp.swapaxes(mlp_back.reshape(chips, 3, units, lanes), 0, 1).astype(F32)
    mlp_back = mlp_back.reshape(3, chips * units, lanes)
    gate_up_back = mlp_back[:2].reshape(2 * chips * units, lanes).T
    gate_up_grad = gate_up_back * mlp_gain_rows
    mlp_gain_part = jnp.sum(gate_up_back * gate_up.astype(F32), axis=1)
    gate_part = gate_up_grad[:, : chips * units]
    up_part = gate_up_grad[:, chips * units :]
    down_part = mlp_back[2]

    d_attn_all = jnp.concatenate(d_attn_pieces).reshape(live, width)
    grad_out = contract_rows(o_low, d_attn_all)
    d_o = times_transposed(d_attn_all, out_head).astype(BF16)
    d_query, d_kv = attend_back(
        queries, q_natural, q_start, kv_all, key_natural, attn_mix, log_total, d_o, block
    )
    d_qpre = unrotate(d_query, q_cos, q_sin).astype(BF16)
    grad_qup = contract_rows(lat_all, d_qpre)
    d_lat_pieces = cut(times_transposed(d_qpre, qup_head).astype(BF16))
    near = SQUARE * layers * rows
    d_kv_near = d_kv[:near] + across(d_kv[near:].astype(BF16)).astype(F32)
    d_kv_pieces = d_kv_near.astype(BF16).reshape(SQUARE, layers, rows, 2 * HEAD)
    if len(squares) == SQUARE:
        d_latent = scatter(
            [jnp.concatenate([d_lat_pieces[m], d_kv_pieces[m]], axis=-1) for m in squares]
        )
        d_lat_scaled, d_kv_own = d_latent[:, :rank], d_latent[:, rank:]
    else:
        d_lat_scaled = scatter([d_lat_pieces[m] for m in squares])
        d_kv_own = scatter([d_kv_pieces[m] for m in range(SQUARE)])
    d_lat = norm_back(d_lat_scaled, lat_hat, lat_inverse)
    d_kvpre = jnp.concatenate([unrotate(d_kv_own[:, :HEAD], own_cos, own_sin), d_kv_own[:, HEAD:]], axis=1)
    d_down = jnp.concatenate([d_lat, d_kvpre], axis=1).astype(BF16)

    d_columns = both(half_of(d_down, core, 1), across(half_of(d_down, 1 - core, 1)))
    d_x_part = times_transposed(d_columns, down_full)
    d_xscaled = from_placed(own(d_x_part) + across(others(d_x_part)))
    x_hat_own, x_inverse_own = own(x_hat), own(x_inverse)
    token_own = (d_hidden + norm_back(d_xscaled, x_hat_own, x_inverse_own)).astype(BF16)
    token_grad = both(token_own, across(token_own))

    grad_down_in = contract_rows(x_low, d_columns).astype(BF16)
    grad_down_in = grad_down_in.reshape(SQUARE, layers, lanes, columns)
    down_pieces = [lax.dynamic_index_in_dim(grad_down_in, corner ^ m, 0, keepdims=False) for m in range(SQUARE)]
    total = sum(
        (piece if m == 0 else within(piece, m)).astype(F32) for m, piece in enumerate(down_pieces)
    )
    low = total.astype(BF16)

    def level(value, k):
        return lax.dynamic_index_in_dim(value, (layer - k) % layers, 0, keepdims=False)

    down_half = level(total, 0) + sum(along(level(low, k), -k).astype(F32) for k in range(1, layers))
    down_sum = both(down_half, across(down_half), axis=1)
    attn_gain_part = jnp.sum(down_sum * down.astype(F32), axis=1)
    down_grad = down_sum * gain_rows
    qdown_part, kv_part = down_grad[:, :rank], down_grad[:, rank:]

    qup_sum = half_of(grad_qup, core, 1) + across(half_of(grad_qup, 1 - core, 1).astype(BF16)).astype(F32)
    out_sum = half_of(grad_out, core, 0) + across(half_of(grad_out, 1 - core, 0).astype(BF16)).astype(F32)
    qup_send = qup_sum.astype(BF16).reshape(chips, -1, lanes)
    out_send = jnp.swapaxes(out_sum.astype(BF16).reshape(half, chips, lanes), 0, 1)
    attn_back = exchange(jnp.concatenate([qup_send, out_send], axis=1))
    attn_back = attn_back.reshape(heads, sharing, -1, lanes)
    if sharing > 1:
        attn_back = jnp.sum(attn_back.astype(F32), axis=1).astype(BF16)
    attn_back = attn_back.reshape(2, heads_half, -1, lanes)
    attn_near, attn_far = of_core(attn_back, core), across(of_core(attn_back, 1 - core))
    attn_grads = jnp.stack([jnp.where(first, attn_near, attn_far), jnp.where(first, attn_far, attn_near)])
    attn_grads = attn_grads.astype(F32)
    qup_back = attn_grads[:, :, :qup_size].reshape(2, heads_half, rank_rows, half)
    qup_back = jnp.transpose(qup_back, (2, 1, 0, 3)).reshape(rank_rows, heads_half * HEAD)
    out_part = jnp.swapaxes(attn_grads[:, :, qup_size:], 0, 1).reshape(heads_half * HEAD, lanes)
    qup_part = qup_back * q_gain_rows
    q_gain_half = jnp.sum(qup_back * w_qup.astype(F32), axis=1)
    gain_parts = jnp.concatenate([q_gain_half, mlp_gain_part])
    gain_parts = gain_parts + across(gain_parts)
    q_gain_part, mlp_gain_part = gain_parts[:rank_rows], gain_parts[rank_rows:]
    return (
        layer_out,
        token_grad,
        attn_gain_part,
        q_gain_part,
        qdown_part,
        qup_part,
        kv_part,
        out_part,
        mlp_gain_part,
        gate_part,
        up_part,
        down_part,
    )


def solution(mesh):
    in_specs = (
        P("seq", None),
        P("seq"),
        P("seq"),
        P("seq", None),
        P("seq", "tp"),
        P("seq", None),
        P("tp", "seq"),
        P("seq"),
        P("seq", "tp"),
        P("seq", "tp"),
        P("tp", "seq"),
        P("seq", None),
        P(),
        P(),
    )
    out_specs = (
        P("seq", None),
        P("seq", None),
        P("seq"),
        P("seq"),
        P("seq", None),
        P("seq", "tp"),
        P("seq", None),
        P("tp", "seq"),
        P("seq"),
        P("seq", "tp"),
        P("seq", "tp"),
        P("tp", "seq"),
    )
    body = functools.partial(local, mesh.shape["seq"])
    return jax.shard_map(body, mesh=mesh, in_specs=in_specs, out_specs=out_specs, check_vma=False)
```

```python
import functools
import math

import jax
import jax.numpy as jnp
from jax import lax
from jax.experimental import pallas as pl
from jax.experimental.pallas import tpu as pltpu
from jax.sharding import PartitionSpec as P

EPSILON = 1e-06
ROPE_BASE = 10000.0
MASKED = -1e30
HEAD = 256
SQUARE = 4
VMEM_LIMIT = 56 * 1024 * 1024
BF16 = jnp.bfloat16
F32 = jnp.float32


def matmul(left, right):
    return jnp.dot(left, right, preferred_element_type=F32)


def contract_rows(left, right):
    return lax.dot_general(left, right, (((0,), (0,)), ((), ())), preferred_element_type=F32)


def times_transposed(left, right):
    return lax.dot_general(left, right, (((1,), (1,)), ((), ())), preferred_element_type=F32)


def inverse_rms(vector):
    return lax.rsqrt(jnp.mean(vector * vector, axis=-1, keepdims=True) + EPSILON)


def norm_back(scaled_grad, normed, inverse):
    return inverse * (scaled_grad - normed * jnp.mean(scaled_grad * normed, axis=-1, keepdims=True))


def angles(position):
    half = HEAD // 2
    frequency = jnp.exp(jnp.arange(half, dtype=F32) * (-math.log(ROPE_BASE) / half))
    phase = position.astype(F32)[:, None] * frequency[None, :]
    return jnp.cos(phase), jnp.sin(phase)


def rotate(vector, cosine, sine):
    half = HEAD // 2
    front, back = vector[:, :half], vector[:, half:]
    return jnp.concatenate([front * cosine - back * sine, back * cosine + front * sine], axis=1)


def unrotate(vector, cosine, sine):
    return rotate(vector, cosine, -sine)


def attend_kernel(
    lat_ref,
    wq_ref,
    cos_ref,
    sin_ref,
    natural_ref,
    start_ref,
    kv_ref,
    keys_ref,
    out_ref,
    q_ref,
    o_ref,
    lse_ref,
    part_ref,
    part_sum,
):
    head, heads = pl.program_id(1), pl.num_programs(1)
    q_pre = matmul(lat_ref[...], wq_ref[...])
    q = (rotate(q_pre, cos_ref[...], sin_ref[...]).astype(BF16).astype(F32) * HEAD**-0.5).astype(BF16)
    q_ref[...] = q
    scores = times_transposed(q, kv_ref[:, :HEAD])
    keys = keys_ref[...]
    allowed = (keys <= natural_ref[...]) & (keys >= start_ref[...])
    scores = jnp.where(allowed, scores, MASKED)
    top = jnp.max(scores, axis=-1, keepdims=True)
    terms = jnp.exp(scores - top)
    total = jnp.sum(terms, axis=-1, keepdims=True)
    mix = matmul(terms.astype(BF16), kv_ref[:, HEAD:]) / total
    o_ref[...] = mix
    lse_ref[0] = top + jnp.log(total)
    share = matmul(mix.astype(BF16), out_ref[...])

    @pl.when(head == 0)
    def _():
        part_sum[...] = share

    @pl.when(head > 0)
    def _():
        part_sum[...] += share

    @pl.when(head == heads - 1)
    def _():
        part_ref[...] = part_sum[...].astype(BF16)


def attend(lat, wq, cosine, sine, natural, start, kv, keys, out_proj, block):
    rows, rank = lat.shape
    count, width = kv.shape[0], out_proj.shape[1]
    heads = wq.shape[1] // HEAD
    row = lambda size: pl.BlockSpec((block, size), lambda i, h: (i, 0))
    whole = lambda shape: pl.BlockSpec(shape, lambda i, h: (0, 0))
    row_head = pl.BlockSpec((block, HEAD), lambda i, h: (i, h))
    half = HEAD // 2
    return pl.pallas_call(
        attend_kernel,
        grid=(rows // block, heads),
        in_specs=[
            row(rank),
            pl.BlockSpec((rank, HEAD), lambda i, h: (0, h)),
            row(half),
            row(half),
            row(1),
            row(1),
            whole((count, 2 * HEAD)),
            whole((1, count)),
            pl.BlockSpec((HEAD, width), lambda i, h: (h, 0)),
        ],
        out_specs=[
            row_head,
            row_head,
            pl.BlockSpec((1, block, 1), lambda i, h: (h, i, 0)),
            row(width),
        ],
        out_shape=[
            jax.ShapeDtypeStruct((rows, heads * HEAD), BF16),
            jax.ShapeDtypeStruct((rows, heads * HEAD), F32),
            jax.ShapeDtypeStruct((heads, rows, 1), F32),
            jax.ShapeDtypeStruct((rows, width), BF16),
        ],
        scratch_shapes=[pltpu.VMEM((block, width), F32)],
        compiler_params=pltpu.CompilerParams(vmem_limit_bytes=VMEM_LIMIT),
        cost_estimate=pl.CostEstimate(
            flops=2 * rows * heads * HEAD * (2 * count + rank + width),
            bytes_accessed=4 * count * HEAD + 2 * heads * HEAD * (rank + width),
            transcendentals=rows * heads * count,
        ),
        name="attend",
    )(lat, wq, cosine, sine, natural, start, kv, keys, out_proj)


def attend_back_kernel(
    lat_ref,
    wq_ref,
    cos_ref,
    sin_ref,
    natural_ref,
    start_ref,
    kv_ref,
    keys_ref,
    out_ref,
    q_ref,
    o_ref,
    lse_ref,
    d_attn_ref,
    grad_q_ref,
    grad_out_ref,
    d_lat_ref,
    dot_ref,
    near_ref,
    far_ref,
    grad_q_sum,
    grad_out_sum,
    d_lat_sum,
    d_kv_sum,
):
    step, steps = pl.program_id(0), pl.num_programs(0)
    head, heads = pl.program_id(1), pl.num_programs(1)
    d_attn, mix, q = d_attn_ref[...], o_ref[...], q_ref[...]
    keys = keys_ref[...]
    allowed = (keys <= natural_ref[...]) & (keys >= start_ref[...])

    @pl.when(step == 0)
    def _():
        grad_q_sum[...] = jnp.zeros_like(grad_q_sum)
        grad_out_sum[...] = jnp.zeros_like(grad_out_sum)

    @pl.when(head == 0)
    def _():
        d_lat_sum[...] = jnp.zeros_like(d_lat_sum)

    @pl.when((step == 0) & (head == 0))
    def _():
        d_kv_sum[...] = jnp.zeros_like(d_kv_sum)

    grad_out_sum[...] += contract_rows(mix.astype(BF16), d_attn)
    d_o = times_transposed(d_attn, out_ref[...]).astype(BF16)
    delta = jnp.sum(d_o.astype(F32) * mix, axis=-1, keepdims=True)
    scores = times_transposed(q, kv_ref[:, :HEAD])
    probs = jnp.exp(jnp.where(allowed, scores - lse_ref[0], MASKED))
    d_probs = times_transposed(d_o, kv_ref[:, HEAD:])
    d_scores = (probs * (d_probs - delta)).astype(BF16)
    d_query = matmul(d_scores, kv_ref[:, :HEAD]) * HEAD**-0.5
    d_kv_sum[:, :HEAD] += contract_rows(d_scores, q)
    d_kv_sum[:, HEAD:] += contract_rows(probs.astype(BF16), d_o)
    d_qpre = unrotate(d_query, cos_ref[...], sin_ref[...]).astype(BF16)
    grad_q_sum[...] += contract_rows(lat_ref[...], d_qpre)
    d_lat_sum[...] += times_transposed(d_qpre, wq_ref[...])

    @pl.when(step == steps - 1)
    def _():
        grad_q_ref[...] = grad_q_sum[...].astype(BF16)
        grad_out_ref[...] = grad_out_sum[...].astype(BF16)

    @pl.when(head == heads - 1)
    def _():
        d_lat = d_lat_sum[...]
        d_lat_ref[...] = d_lat.astype(BF16)
        dot = jnp.sum(d_lat * lat_ref[...].astype(F32), axis=-1, keepdims=True)
        dot_ref[...] = jnp.broadcast_to(dot, dot_ref.shape).astype(BF16)

    @pl.when((step == steps - 1) & (head == heads - 1))
    def _():
        size = near_ref.shape[0]
        near_ref[...] = d_kv_sum[:size, :]
        far_ref[...] = d_kv_sum[size:, :].astype(BF16)


def attend_back(lat, wq, cosine, sine, natural, start, kv, keys, out_proj, q, o, lse, d_attn, block):
    rows, rank = lat.shape
    count, width = kv.shape[0], out_proj.shape[1]
    heads = wq.shape[1] // HEAD
    row = lambda size: pl.BlockSpec((block, size), lambda i, h: (i, 0))
    whole = lambda shape: pl.BlockSpec(shape, lambda i, h: (0, 0))
    row_head = pl.BlockSpec((block, HEAD), lambda i, h: (i, h))
    half = HEAD // 2
    wq_spec = pl.BlockSpec((rank, HEAD), lambda i, h: (0, h))
    out_spec = pl.BlockSpec((HEAD, width), lambda i, h: (h, 0))
    return pl.pallas_call(
        attend_back_kernel,
        grid=(rows // block, heads),
        in_specs=[
            row(rank),
            wq_spec,
            row(half),
            row(half),
            row(1),
            row(1),
            whole((count, 2 * HEAD)),
            whole((1, count)),
            out_spec,
            row_head,
            row_head,
            pl.BlockSpec((1, block, 1), lambda i, h: (h, i, 0)),
            row(width),
        ],
        out_specs=[
            wq_spec,
            out_spec,
            row(rank),
            row(128),
            whole((count // 2, 2 * HEAD)),
            whole((count // 2, 2 * HEAD)),
        ],
        out_shape=[
            jax.ShapeDtypeStruct((rank, heads * HEAD), BF16),
            jax.ShapeDtypeStruct((heads * HEAD, width), BF16),
            jax.ShapeDtypeStruct((rows, rank), BF16),
            jax.ShapeDtypeStruct((rows, 128), BF16),
            jax.ShapeDtypeStruct((count // 2, 2 * HEAD), F32),
            jax.ShapeDtypeStruct((count // 2, 2 * HEAD), BF16),
        ],
        scratch_shapes=[
            pltpu.VMEM((rank, HEAD), F32),
            pltpu.VMEM((HEAD, width), F32),
            pltpu.VMEM((block, rank), F32),
            pltpu.VMEM((count, 2 * HEAD), F32),
        ],
        compiler_params=pltpu.CompilerParams(vmem_limit_bytes=VMEM_LIMIT),
        cost_estimate=pl.CostEstimate(
            flops=2 * rows * heads * HEAD * (5 * count + 2 * rank + 2 * width),
            bytes_accessed=12 * count * HEAD + 4 * heads * HEAD * (rank + width),
            transcendentals=rows * heads * count,
        ),
        name="attend_back",
    )(lat, wq, cosine, sine, natural, start, kv, keys, out_proj, q, o, lse, d_attn)


def mlp_kernel(
    h_ref, cot_ref, near_ref, far_ref, d_h_ref, out_ref, act_near_ref, act_far_ref, weights, d_h_sum, out_sum, sems
):
    copies = [
        pltpu.make_async_copy(source, weights.at[i], sems.at[i])
        for i, source in enumerate((near_ref, far_ref))
    ]
    for copy in copies:
        copy.start()
    size = weights.shape[-1]
    for i, acts in enumerate((act_near_ref, act_far_ref)):
        copies[i].wait()

        def product(value_ref, kind):
            return sum(
                times_transposed(value_ref[:, q * size : (q + 1) * size], weights[i, q, kind])
                for q in range(SQUARE)
            )

        gate_act, up_proj, d_act = product(h_ref, 0), product(h_ref, 1), product(cot_ref, 2)
        sigmoid_gate = 1.0 / (1.0 + jnp.exp(-gate_act))
        silu_gate = gate_act * sigmoid_gate
        d_gate = d_act * up_proj * sigmoid_gate * (1.0 + gate_act * (1.0 - sigmoid_gate))
        acts[0] = d_gate.astype(BF16)
        acts[1] = (d_act * silu_gate).astype(BF16)
        acts[2] = (silu_gate * up_proj).astype(BF16)
        for q in range(SQUARE):
            here = slice(q * size, (q + 1) * size)
            d_h = matmul(acts[0], weights[i, q, 0]) + matmul(acts[1], weights[i, q, 1])
            out = matmul(acts[2], weights[i, q, 2])
            if i == 0:
                d_h_sum[:, here] = d_h
                out_sum[:, here] = out
            else:
                d_h_ref[:, here] = (d_h_sum[:, here] + d_h).astype(BF16)
                out_ref[:, here] = (out_sum[:, here] + out).astype(BF16)


def mlp(h, cot, near, far):
    rows, width = h.shape
    units = near.shape[2]
    vmem = pl.BlockSpec(memory_space=pltpu.VMEM)
    hbm = pl.BlockSpec(memory_space=pl.ANY)
    low = jax.ShapeDtypeStruct((rows, width), BF16)
    acts = jax.ShapeDtypeStruct((3, rows, units), BF16)
    return pl.pallas_call(
        mlp_kernel,
        in_specs=[vmem, vmem, hbm, hbm],
        out_specs=[vmem] * 4,
        out_shape=[low, low, acts, acts],
        scratch_shapes=[
            pltpu.VMEM((2,) + near.shape, BF16),
            pltpu.VMEM((rows, width), F32),
            pltpu.VMEM((rows, width), F32),
            pltpu.SemaphoreType.DMA((2,)),
        ],
        compiler_params=pltpu.CompilerParams(vmem_limit_bytes=VMEM_LIMIT),
        cost_estimate=pl.CostEstimate(
            flops=24 * rows * width * units,
            bytes_accessed=4 * near.size + 8 * rows * width,
            transcendentals=2 * rows * units,
        ),
        name="mlp",
    )(h, cot, near, far)


def unit_grads_kernel(acts_ref, h_ref, cot_ref, *refs):
    grads_ref = refs[-1]

    def store(value):
        grad = contract_rows(acts_ref[0], value)
        if len(refs) > 1:
            grad = grad + refs[0][0, 0].astype(F32)
        grads_ref[0, 0] = grad.astype(BF16)

    @pl.when(pl.program_id(1) < 2)
    def _():
        store(h_ref[...])

    @pl.when(pl.program_id(1) == 2)
    def _():
        store(cot_ref[...])


def unit_grads(acts, h, cot, *more):
    rows, width = h.shape
    units, size = acts.shape[2], width // SQUARE
    column = pl.BlockSpec((rows, size), lambda q, kind: (0, q))
    grads = pl.BlockSpec((1, 1, units, size), lambda q, kind: (q, kind, 0, 0))
    return pl.pallas_call(
        unit_grads_kernel,
        grid=(SQUARE, 3),
        in_specs=[pl.BlockSpec((1, rows, units), lambda q, kind: (kind, 0, 0)), column, column]
        + [grads] * len(more),
        out_specs=grads,
        out_shape=jax.ShapeDtypeStruct((SQUARE, 3, units, size), BF16),
        compiler_params=pltpu.CompilerParams(vmem_limit_bytes=VMEM_LIMIT),
        cost_estimate=pl.CostEstimate(
            flops=6 * rows * width * units, bytes_accessed=6 * width * units, transcendentals=0
        ),
        name="unit_grads",
    )(acts, h, cot, *more)


def local(
    chips,
    tokens,
    attn_gain,
    q_gain,
    w_qdown,
    w_qup,
    w_kv,
    w_out,
    mlp_gain,
    w_gate,
    w_up,
    w_down,
    cotangent,
    seq_lengths,
    block_slots,
):
    layers = chips // SQUARE
    rows, width = tokens.shape[0] // 2, tokens.shape[1]
    line_rows = layers * rows
    lanes = width // chips
    rank = w_qdown.shape[1]
    rank_rows = w_qup.shape[0]
    heads_half = w_qup.shape[1] // HEAD
    heads = 2 * heads_half
    heads_here = heads // layers
    units = w_gate.shape[1] // layers
    half = HEAD // 2
    place = lax.axis_index("seq")
    core = lax.axis_index("tp")
    layer, corner = place // SQUARE, place % SQUARE
    first = core == 0
    lines = [[z * SQUARE + c for z in range(layers)] for c in range(SQUARE)]
    square_groups = [[z * SQUARE + c for c in range(SQUARE)] for z in range(layers)]

    def across(value):
        return lax.ppermute(value, "tp", [(0, 1), (1, 0)])

    def along(value, step):
        pairs = [
            (z * SQUARE + c, (z + step) % layers * SQUARE + c)
            for z in range(layers)
            for c in range(SQUARE)
        ]
        return lax.ppermute(value, "seq", pairs)

    def within(value, flip):
        return lax.ppermute(value, "seq", [(i, i ^ flip) for i in range(chips)])

    def exchange(value):
        return lax.all_to_all(value, "seq", 0, 0, axis_index_groups=lines, tiled=True)

    def line_gather(value):
        return jnp.concatenate([value] + [along(value, k) for k in range(1, layers)])

    def line_scatter(value):
        blocks = value.reshape(layers, rows, value.shape[1])
        return blocks[0].astype(F32) + sum(
            along(blocks[k], -k).astype(F32) for k in range(1, layers)
        )

    def put(parts, indices):
        stacked = jnp.zeros((len(parts),) + parts[0].shape, parts[0].dtype)
        for part, index in zip(parts, indices):
            stacked = lax.dynamic_update_index_in_dim(stacked, part, index, 0)
        return stacked

    def square_gather(value):
        size = value.shape[0] // 2
        one, two = within(value, 1), within(value, 2)
        three = jnp.concatenate([within(one[:size], 2), within(two[size:], 1)])
        return put([value, one, two, three], [corner ^ m for m in range(SQUARE)])

    def square_scatter(value):
        size = value.shape[1] // 2
        piece = lambda m: lax.dynamic_index_in_dim(value, corner ^ m, 0, keepdims=False)
        pieces = [piece(m) for m in range(SQUARE)]
        sums = []
        for here, near, next_one in ((slice(0, size), 1, 2), (slice(size, None), 2, 1)):
            sent = jnp.stack([pieces[near][here], pieces[3][here]])
            got = within(sent, near)
            mine = pieces[0][here].astype(F32) + got[0].astype(F32)
            other = pieces[next_one][here].astype(F32) + got[1].astype(F32)
            sums.append(mine + within(other.astype(BF16), next_one).astype(F32))
        return jnp.concatenate(sums)

    def own(pair_value):
        return lax.dynamic_slice_in_dim(pair_value, core * rows, rows, 0)

    def both(mine, theirs, axis=0):
        return jnp.concatenate(
            [jnp.where(first, mine, theirs), jnp.where(first, theirs, mine)], axis=axis
        )

    def of_core(value, which):
        return lax.dynamic_index_in_dim(value, which, 0, keepdims=False)

    def block_of(value, index, size):
        return lax.dynamic_slice_in_dim(value, index * size, size, 1)

    def to_placed(value):
        shaped = value.reshape(value.shape[0], layers, SQUARE, lanes)
        return jnp.swapaxes(shaped, 1, 2).reshape(value.shape[0], width)

    def from_placed(value):
        shaped = value.reshape(value.shape[0], SQUARE, layers, lanes)
        return jnp.swapaxes(shaped, 1, 2).reshape(value.shape[0], width)

    inputs = to_placed(own(tokens).astype(F32))
    x_inverse = inverse_rms(inputs)
    x_hat = inputs * x_inverse
    x_all = line_gather(x_hat.astype(BF16))

    gain_rows = attn_gain.astype(F32)[:, None]
    down = jnp.concatenate([w_qdown, w_kv], axis=1)
    rank_share, kv_share = rank // layers, 2 * HEAD // layers
    share = rank_share + kv_share

    def shares(value):
        lat = value[:, :rank].reshape(-1, layers, rank_share)
        kv = value[:, rank:].reshape(-1, layers, kv_share)
        return jnp.swapaxes(jnp.concatenate([lat, kv], axis=2), 0, 1)

    def unshares(value):
        value = jnp.swapaxes(value, 0, 1)
        count = value.shape[0]
        lat = value[:, :, :rank_share].reshape(count, rank)
        return jnp.concatenate([lat, value[:, :, rank_share:].reshape(count, 2 * HEAD)], axis=1)

    down_scaled = (down.astype(F32) * gain_rows).astype(BF16)
    down_half = lax.dynamic_slice_in_dim(down_scaled, core * (lanes // 2), lanes // 2, 0)
    down_near = square_gather(exchange(shares(down_half))).reshape(SQUARE, layers, lanes // 2, share)
    down_here = both(down_near, across(down_near), axis=2).reshape(width, share)

    q_gain_rows = q_gain.astype(F32)[:, None]
    qup_scaled = (w_qup.astype(F32) * q_gain_rows).astype(BF16)
    qup_heads = qup_scaled.reshape(rank_rows, heads_half, 2, half)
    qup_heads = jnp.transpose(qup_heads, (2, 1, 0, 3))
    out_heads = jnp.swapaxes(w_out.reshape(heads_half, 2, half, lanes), 0, 1)
    qup_mine = both(of_core(qup_heads, core), across(of_core(qup_heads, 1 - core)))
    out_mine = both(of_core(out_heads, core), across(of_core(out_heads, 1 - core)))
    attn_send = jnp.concatenate(
        [qup_mine.reshape(layers, -1, lanes), out_mine.reshape(layers, -1, lanes)], axis=1
    )
    qup_size = heads_here * rank_rows * half // lanes
    attn_in = square_gather(exchange(attn_send))
    qup_half = attn_in[:, :, :qup_size].reshape(SQUARE, layers, heads_here, rank_rows, half)
    qup_half = jnp.transpose(qup_half, (1, 0, 3, 2, 4)).reshape(rank, heads_here, half)
    out_half = attn_in[:, :, qup_size:].reshape(SQUARE, layers, heads_here, half, lanes)
    out_half = jnp.transpose(out_half, (2, 3, 0, 1, 4)).reshape(heads_here, half, width)
    qup_here = both(qup_half, across(qup_half), axis=2).reshape(rank, heads_here * HEAD)
    out_here = both(out_half, across(out_half), axis=1).reshape(heads_here * HEAD, width)

    mlp_gain_rows = mlp_gain.astype(F32)[:, None]
    gate_up = jnp.concatenate([w_gate, w_up], axis=1)
    gate_up_scaled = (gate_up.astype(F32) * mlp_gain_rows).astype(BF16).T
    mlp_send = jnp.concatenate([gate_up_scaled, w_down]).reshape(3, layers, units, lanes)
    mlp_send = jnp.swapaxes(mlp_send, 0, 1).reshape(layers, 3 * units, lanes)
    mlp_block = jnp.swapaxes(exchange(mlp_send), 0, 1).reshape(3 * units, layers * lanes)
    mlp_near = lax.all_gather(mlp_block, "seq", axis_index_groups=square_groups)
    mlp_near = mlp_near.reshape(SQUARE, 3, units, layers * lanes)
    mlp_far = across(mlp_near)
    cot_own = to_placed(own(cotangent))
    cot_all = line_gather(cot_own)

    bounds = jnp.cumsum(seq_lengths)
    starts = bounds - seq_lengths

    def layout(blocks):
        natural = (blocks[:, None] * rows + jnp.arange(rows, dtype=jnp.int32)[None, :]).reshape(-1)
        member = (natural[:, None] >= starts[None, :]) & (natural[:, None] < bounds[None, :])
        return natural, jnp.sum(jnp.where(member, starts[None, :], 0), axis=1)

    back_steps = jnp.arange(layers, dtype=jnp.int32)
    owners = jnp.concatenate(
        [((layer - back_steps) % layers) * SQUARE + (corner ^ m) for m in range(SQUARE)]
    )
    near_natural, near_start = layout(block_slots[2 * owners + core])
    far_natural, _ = layout(block_slots[2 * owners + 1 - core])
    key_natural = jnp.concatenate([near_natural, far_natural])[None, :]
    row_natural, row_start = near_natural[:line_rows], near_start[:line_rows]
    cosine, sine = angles(row_natural - row_start)
    row_natural, row_start = row_natural[:, None], row_start[:, None]

    part = matmul(x_all, down_here).astype(BF16)

    def rolled(value, step):
        return jnp.roll(value.reshape(layers, rows, value.shape[1]), step, axis=0).reshape(value.shape)

    parts = jnp.stack([part] + [rolled(along(part, k), k) for k in range(1, layers)])
    parts = jnp.stack([of_core(parts, (layer - z) % layers) for z in range(layers)])
    projected = unshares(parts).astype(F32)
    q_lat, kv_pre = projected[:, :rank], projected[:, rank:]
    lat_inverse = inverse_rms(q_lat)
    lat_hat = q_lat * lat_inverse
    lat_low = lat_hat.astype(BF16)
    kv_line = jnp.concatenate([rotate(kv_pre[:, :HEAD], cosine, sine), kv_pre[:, HEAD:]], axis=1)
    kv_line = kv_line.astype(BF16)
    kv_near = jnp.concatenate([kv_line] + [within(kv_line, m) for m in range(1, SQUARE)])
    kv_all = jnp.concatenate([kv_near, across(kv_near)])

    block = max(64, min(line_rows, 256 * 2048 // kv_all.shape[0]))
    queries, attn_mix, log_total, attn_part = attend(
        lat_low, qup_here, cosine, sine, row_natural, row_start, kv_all, key_natural, out_here, block
    )
    hidden = inputs + line_scatter(attn_part)
    h_inverse = inverse_rms(hidden)
    h_hat = hidden * h_inverse
    h_all = line_gather(h_hat.astype(BF16))

    d_h_part, mlp_part, acts_near, acts_far = mlp(h_all, cot_all, mlp_near, mlp_far)
    d_hscaled = line_scatter(d_h_part)
    d_hidden = cot_own.astype(F32) + norm_back(d_hscaled, h_hat, h_inverse)
    d_attn_all = line_gather(d_hidden.astype(BF16))
    layer_own = from_placed((hidden + line_scatter(mlp_part)).astype(BF16))
    layer_out = both(layer_own, across(layer_own))

    grads_far = unit_grads(acts_far, h_all, cot_all)
    grads_near = unit_grads(acts_near, h_all, cot_all, across(grads_far))
    mlp_back = lax.psum_scatter(
        grads_near.reshape(SQUARE, 3 * units, layers * lanes), "seq", axis_index_groups=square_groups
    )
    mlp_back = jnp.swapaxes(mlp_back.reshape(3 * units, layers, lanes), 0, 1)
    mlp_back = exchange(mlp_back).reshape(layers, 3, units, lanes)
    mlp_back = jnp.swapaxes(mlp_back, 0, 1).astype(F32).reshape(3, layers * units, lanes)
    gate_up_back = mlp_back[:2].reshape(2 * layers * units, lanes).T
    gate_up_grad = gate_up_back * mlp_gain_rows
    mlp_gain_part = jnp.sum(gate_up_back * gate_up.astype(F32), axis=1)
    gate_part = gate_up_grad[:, : layers * units]
    up_part = gate_up_grad[:, layers * units :]
    down_part = mlp_back[2]

    grad_qup, grad_out, d_lat_part, dot_part, d_kv_near, d_kv_far = attend_back(
        lat_low,
        qup_here,
        cosine,
        sine,
        row_natural,
        row_start,
        kv_all,
        key_natural,
        out_here,
        queries,
        attn_mix,
        log_total,
        d_attn_all,
        block,
    )
    d_kv_low = (d_kv_near + across(d_kv_far).astype(F32)).astype(BF16)
    d_kv_low = d_kv_low.reshape(SQUARE, line_rows, 2 * HEAD)
    d_kv_line = d_kv_low[0].astype(F32) + sum(
        within(d_kv_low[m], m).astype(F32) for m in range(1, SQUARE)
    )
    d_kv_line = jnp.concatenate(
        [unrotate(d_kv_line[:, :HEAD], cosine, sine), d_kv_line[:, HEAD:]], axis=1
    ).astype(BF16)

    def columns_for(where):
        return jnp.concatenate(
            [block_of(d_lat_part, where, rank_share), block_of(d_kv_line, where, kv_share), dot_part],
            axis=1,
        )

    d_share = columns_for(layer).astype(F32) + sum(
        rolled(along(columns_for((layer - k) % layers), -k), -k).astype(F32)
        for k in range(1, layers)
    )
    dot = d_share[:, share : share + 1] / rank
    d_lat = lat_inverse * (d_share[:, :rank_share] - block_of(lat_hat, layer, rank_share) * dot)
    d_down = jnp.concatenate([d_lat, d_share[:, rank_share:share]], axis=1).astype(BF16)

    d_xscaled = line_scatter(times_transposed(d_down, down_here).astype(BF16))
    token_own = from_placed((d_hidden + norm_back(d_xscaled, x_hat, x_inverse)).astype(BF16))
    token_grad = both(token_own, across(token_own))
    grad_down = contract_rows(x_all, d_down).reshape(SQUARE, layers, 2, lanes // 2, share)
    grad_down = jnp.transpose(grad_down, (2, 0, 1, 3, 4))
    grad_down = of_core(grad_down, core) + across(of_core(grad_down, 1 - core).astype(BF16)).astype(F32)
    down_back = square_scatter(grad_down.astype(BF16)).astype(BF16)
    down_back = unshares(exchange(down_back)).astype(F32)
    down_sum = both(down_back, across(down_back))
    attn_gain_part = jnp.sum(down_sum * down.astype(F32), axis=1)
    down_grad = down_sum * gain_rows
    qdown_part, kv_part = down_grad[:, :rank], down_grad[:, rank:]

    grad_qup = grad_qup.reshape(layers, SQUARE, rank_rows, heads_here, 2, half)
    grad_qup = jnp.transpose(grad_qup, (4, 1, 0, 3, 2, 5)).reshape(2, SQUARE, layers, -1, lanes)
    grad_out = grad_out.reshape(heads_here, 2, half, SQUARE, layers, lanes)
    grad_out = jnp.transpose(grad_out, (1, 3, 4, 0, 2, 5)).reshape(2, SQUARE, layers, -1, lanes)
    attn_grads = jnp.concatenate([grad_qup, grad_out], axis=3)
    attn_sum = of_core(attn_grads, core).astype(F32) + across(of_core(attn_grads, 1 - core)).astype(F32)
    attn_back = exchange(square_scatter(attn_sum.astype(BF16)).astype(BF16))
    qup_back = attn_back[:, :qup_size].reshape(2, heads_half, rank_rows, half)
    out_back = attn_back[:, qup_size:].reshape(2, heads_half, half, lanes)
    qup_back = both(of_core(qup_back, core)[None], across(of_core(qup_back, 1 - core))[None])
    out_back = both(of_core(out_back, core)[None], across(of_core(out_back, 1 - core))[None])
    qup_back = jnp.transpose(qup_back, (2, 1, 0, 3)).reshape(rank_rows, heads_half * HEAD).astype(F32)
    out_part = jnp.swapaxes(out_back, 0, 1).reshape(heads_half * HEAD, lanes).astype(F32)
    qup_part = qup_back * q_gain_rows
    q_gain_half = jnp.sum(qup_back * w_qup.astype(F32), axis=1)
    gain_parts = jnp.concatenate([q_gain_half, mlp_gain_part])
    gain_parts = gain_parts + across(gain_parts)
    q_gain_part, mlp_gain_part = gain_parts[:rank_rows], gain_parts[rank_rows:]
    return (
        layer_out,
        token_grad,
        attn_gain_part,
        q_gain_part,
        qdown_part,
        qup_part,
        kv_part,
        out_part,
        mlp_gain_part,
        gate_part,
        up_part,
        down_part,
    )


def solution(mesh):
    in_specs = (
        P("seq", None),
        P("seq"),
        P("seq"),
        P("seq", None),
        P("seq", "tp"),
        P("seq", None),
        P("tp", "seq"),
        P("seq"),
        P("seq", "tp"),
        P("seq", "tp"),
        P("tp", "seq"),
        P("seq", None),
        P(),
        P(),
    )
    out_specs = (
        P("seq", None),
        P("seq", None),
        P("seq"),
        P("seq"),
        P("seq", None),
        P("seq", "tp"),
        P("seq", None),
        P("tp", "seq"),
        P("seq"),
        P("seq", "tp"),
        P("seq", "tp"),
        P("tp", "seq"),
    )
    body = functools.partial(local, mesh.shape["seq"])
    return jax.shard_map(body, mesh=mesh, in_specs=in_specs, out_specs=out_specs, check_vma=False)
```

```python
import functools
import math

import jax
import jax.numpy as jnp
from jax import lax
from jax.experimental import pallas as pl
from jax.experimental.pallas import tpu as pltpu
from jax.sharding import PartitionSpec as P

EPSILON = 1e-06
ROPE_BASE = 10000.0
MASKED = -1e30
HEAD = 256
SQUARE = 4
VMEM_LIMIT = 56 * 1024 * 1024
BF16 = jnp.bfloat16
F32 = jnp.float32


def matmul(left, right):
    return jnp.dot(left, right, preferred_element_type=F32)


def contract_rows(left, right):
    return lax.dot_general(left, right, (((0,), (0,)), ((), ())), preferred_element_type=F32)


def times_transposed(left, right):
    return lax.dot_general(left, right, (((1,), (1,)), ((), ())), preferred_element_type=F32)


def inverse_rms(vector):
    return lax.rsqrt(jnp.mean(vector * vector, axis=-1, keepdims=True) + EPSILON)


def norm_back(scaled_grad, normed, inverse):
    return inverse * (scaled_grad - normed * jnp.mean(scaled_grad * normed, axis=-1, keepdims=True))


def angles(position):
    half = HEAD // 2
    frequency = jnp.exp(jnp.arange(half, dtype=F32) * (-math.log(ROPE_BASE) / half))
    phase = position.astype(F32)[:, None] * frequency[None, :]
    return jnp.cos(phase), jnp.sin(phase)


def rotate(vector, cosine, sine):
    half = HEAD // 2
    front, back = vector[:, :half], vector[:, half:]
    return jnp.concatenate([front * cosine - back * sine, back * cosine + front * sine], axis=1)


def unrotate(vector, cosine, sine):
    return rotate(vector, cosine, -sine)


def params(limit=VMEM_LIMIT):
    return pltpu.CompilerParams(vmem_limit_bytes=limit)


VMEM = pl.BlockSpec(memory_space=pltpu.VMEM)
SMEM = pl.BlockSpec(memory_space=pltpu.SMEM)
HBM = pl.BlockSpec(memory_space=pl.ANY)


def shape(dims, dtype=BF16):
    return jax.ShapeDtypeStruct(tuple(dims), dtype)


def project_kernel(layers, at_ref, x_ref, *refs):
    near, far = refs[:layers], refs[layers : 2 * layers]
    part_ref, w_ref, sems = refs[2 * layers :]
    layer, core = at_ref[0], at_ref[2]
    copies = []
    for c, pieces in enumerate((near, far)):
        side = core if c == 0 else 1 - core
        for k, piece in enumerate(pieces):
            first = lax.rem(layer + layers - k, layers) * SQUARE
            target = w_ref.at[pl.ds(first, SQUARE), side]
            copies.append(pltpu.make_async_copy(piece, target, sems.at[c, k]))
    for copy in copies:
        copy.start()
    for copy in copies:
        copy.wait()
    width, share = x_ref.shape[1], w_ref.shape[-1]
    part_ref[...] = matmul(x_ref[...], w_ref[...].reshape(width, share)).astype(BF16)


def project(at, x, near, far):
    layers = len(near)
    rows, width = x.shape
    _, lane_rows, share = near[0].shape
    return pl.pallas_call(
        functools.partial(project_kernel, layers),
        in_specs=[SMEM, VMEM] + [HBM] * (2 * layers),
        out_specs=[VMEM, VMEM],
        out_shape=[
            shape((rows, share)),
            shape((layers * SQUARE, 2, lane_rows, share)),
        ],
        scratch_shapes=[pltpu.SemaphoreType.DMA((2, layers))],
        compiler_params=params(),
        cost_estimate=pl.CostEstimate(
            flops=2 * rows * width * share, bytes_accessed=4 * width * share, transcendentals=0
        ),
        name="project",
    )(at, x, *near, *far)


def latent_kernel(at_ref, cos_ref, sin_ref, *refs):
    parts = refs[:SQUARE]
    hat_ref, low_ref, inverse_ref, kv_ref, kv_sum = refs[SQUARE:]
    corner = at_ref[1]
    rows = kv_ref.shape[0]
    rank_share, kv_share = hat_ref.shape[1] // SQUARE, 2 * HEAD // SQUARE
    for m, part in enumerate(parts):
        b = corner ^ m
        columns = pl.ds(pl.multiple_of(b * rank_share, rank_share), rank_share)
        for i in range(SQUARE):
            source = slice((i ^ m) * rows, (i ^ m) * rows + rows)
            hat_ref[i * rows : (i + 1) * rows, columns] = part[source, :rank_share].astype(F32)
        columns = pl.ds(pl.multiple_of(b * kv_share, kv_share), kv_share)
        kv_sum[:, columns] = part[m * rows : (m + 1) * rows, rank_share:].astype(F32)
    q_lat = hat_ref[...]
    inverse = inverse_rms(q_lat)
    hat = q_lat * inverse
    hat_ref[...] = hat
    low_ref[...] = hat.astype(BF16)
    inverse_ref[...] = inverse
    kv_ref[:, :HEAD] = rotate(kv_sum[:, :HEAD], cos_ref[:rows], sin_ref[:rows]).astype(BF16)
    kv_ref[:, HEAD:] = kv_sum[:, HEAD:].astype(BF16)


def latent(at, cosine, sine, parts, rank):
    count = parts[0].shape[0]
    rows = count // SQUARE
    return pl.pallas_call(
        latent_kernel,
        in_specs=[SMEM] + [VMEM] * (2 + SQUARE),
        out_specs=[VMEM] * 4,
        out_shape=[
            shape((count, rank), F32),
            shape((count, rank)),
            shape((count, 1), F32),
            shape((rows, 2 * HEAD)),
        ],
        scratch_shapes=[pltpu.VMEM((rows, 2 * HEAD), F32)],
        compiler_params=params(),
        cost_estimate=pl.CostEstimate(flops=8 * count * rank, bytes_accessed=10 * count * rank, transcendentals=0),
        name="latent",
    )(at, cosine, sine, *parts)


def head_copies(layers, layer, refs, wq, wo, sems):
    per_layer = wo.shape[1] // layers
    copies = []
    for i, (target, count) in enumerate(((wq, SQUARE), (wo, per_layer))):
        for c in range(2):
            for k in range(layers):
                source = refs[(2 * i + c) * layers + k]
                first = lax.rem(layer + layers - k, layers) * count
                copies.append(
                    pltpu.make_async_copy(source, target.at[c, pl.ds(first, count)], sems.at[i, c, k])
                )
    return copies


def head_q(wq, c, h):
    rank = wq.shape[1] * wq.shape[3]
    half = HEAD // 2
    return jnp.concatenate([wq[c, :, 2 * h + i].reshape(rank, half) for i in range(2)], axis=1)


def head_out(wo, c, h):
    return jnp.concatenate(
        [wo[c, tile, h * HEAD : (h + 1) * HEAD, :] for tile in range(wo.shape[1])], axis=1
    )


def attend_kernel(
    layers, at_ref, lat_ref, cos_ref, sin_ref, natural_ref, start_ref, kv_ref, keys_ref, *refs
):
    weights, (q_ref, o_ref, lse_ref, part_ref, wq, wo, sems) = refs[: 4 * layers], refs[4 * layers :]

    @pl.when(pl.program_id(0) == 0)
    def _():
        copies = head_copies(layers, at_ref[0], weights, wq, wo, sems)
        for copy in copies:
            copy.start()
        for copy in copies:
            copy.wait()

    keys = keys_ref[...]
    allowed = (keys <= natural_ref[...]) & (keys >= start_ref[...])
    pair = wq.shape[2] // 2
    part = None
    for c in range(2):
        for h in range(pair):
            q_pre = matmul(lat_ref[...], head_q(wq, c, h))
            q = rotate(q_pre, cos_ref[...], sin_ref[...]).astype(BF16)
            q = (q.astype(F32) * HEAD**-0.5).astype(BF16)
            scores = jnp.where(allowed, times_transposed(q, kv_ref[:, :HEAD]), MASKED)
            top = jnp.max(scores, axis=-1, keepdims=True)
            terms = jnp.exp(scores - top)
            total = jnp.sum(terms, axis=-1, keepdims=True)
            mix = matmul(terms.astype(BF16), kv_ref[:, HEAD:]) / total
            q_ref[c * pair + h] = q
            o_ref[c * pair + h] = mix
            lse_ref[c * pair + h] = top + jnp.log(total)
            share = matmul(mix.astype(BF16), head_out(wo, c, h))
            part = share if part is None else part + share
    part_ref[...] = part.astype(BF16)


def attend_specs(layers, block, rank, count):
    row = lambda size: pl.BlockSpec((block, size), lambda i: (i, 0))
    whole = lambda dims: pl.BlockSpec(dims, lambda i: (0,) * len(dims))
    half = HEAD // 2
    return [
        SMEM,
        row(rank),
        row(half),
        row(half),
        row(1),
        row(1),
        whole((count, 2 * HEAD)),
        whole((1, count)),
    ] + [HBM] * (4 * layers)


def attend(at, lat, tables, kv, keys, weights, block):
    near_q, far_q, near_out, far_out = weights
    layers = len(near_q)
    rows, rank = lat.shape
    count = kv.shape[0]
    _, tiles_q, rank_rows, half = near_q[0].shape
    per_layer, pair_rows, lanes = near_out[0].shape
    heads, width = tiles_q, per_layer * layers * lanes
    by_head = lambda size: pl.BlockSpec((heads, block, size), lambda i: (0, i, 0))
    return pl.pallas_call(
        functools.partial(attend_kernel, layers),
        grid=(rows // block,),
        in_specs=attend_specs(layers, block, rank, count),
        out_specs=[
            by_head(HEAD),
            by_head(HEAD),
            by_head(1),
            pl.BlockSpec((block, width), lambda i: (i, 0)),
        ],
        out_shape=[
            shape((heads, rows, HEAD)),
            shape((heads, rows, HEAD), F32),
            shape((heads, rows, 1), F32),
            shape((rows, width)),
        ],
        scratch_shapes=[
            pltpu.VMEM((2, layers * SQUARE, tiles_q, rank_rows, half), BF16),
            pltpu.VMEM((2, layers * per_layer, pair_rows, lanes), BF16),
            pltpu.SemaphoreType.DMA((2, 2, layers)),
        ],
        compiler_params=params(),
        cost_estimate=pl.CostEstimate(
            flops=2 * rows * heads * HEAD * (2 * count + rank + width),
            bytes_accessed=4 * count * HEAD + 2 * heads * HEAD * (rank + width),
            transcendentals=rows * heads * count,
        ),
        name="attend",
    )(at, lat, *tables, kv, keys, *near_q, *far_q, *near_out, *far_out)


def attend_back_kernel(
    layers, at_ref, lat_ref, cos_ref, sin_ref, natural_ref, start_ref, kv_ref, keys_ref, *refs
):
    weights, refs = refs[: 4 * layers], refs[4 * layers :]
    q_ref, o_ref, lse_ref, d_attn_ref = refs[:4]
    grads_q, grads_out, d_lat_ref, near_ref, far_ref = refs[4:6], refs[6:8], refs[8], refs[9], refs[10]
    wq, wo, sems, d_kv_sum, d_lat_sum = refs[11:16]
    sums = refs[16:]
    step, steps = pl.program_id(0), pl.num_programs(0)
    layer, corner = at_ref[0], at_ref[1]
    per_layer = wo.shape[1] // layers

    @pl.when(step == 0)
    def _():
        copies = head_copies(layers, layer, weights, wq, wo, sems)
        for copy in copies:
            copy.start()
        d_kv_sum[...] = jnp.zeros_like(d_kv_sum)
        for total in sums:
            total[...] = jnp.zeros_like(total)
        for copy in copies:
            copy.wait()

    def store(c, h, grad_q, grad_out):
        for z in range(layers):
            k = lax.rem(layer + layers - z, layers)
            ranks = grad_q.shape[0] // layers
            rows_here = grad_q[z * ranks : (z + 1) * ranks].astype(BF16)
            for i in range(2):
                tile = rows_here[:, i * 128 : (i + 1) * 128]
                grads_q[c][k, :, 2 * h + i] = tile.reshape(SQUARE, ranks // SQUARE, 128)
            for i in range(per_layer):
                tile = z * per_layer + i
                grads_out[c][k, i, h * HEAD : (h + 1) * HEAD, :] = grad_out[
                    :, tile * 128 : (tile + 1) * 128
                ].astype(BF16)

    keys = keys_ref[...]
    allowed = (keys <= natural_ref[...]) & (keys >= start_ref[...])
    d_attn, lat = d_attn_ref[...], lat_ref[...]
    pair = wq.shape[2] // 2
    d_lat = None
    for c in range(2):
        for h in range(pair):
            q, mix, lse = q_ref[c * pair + h], o_ref[c * pair + h], lse_ref[c * pair + h]
            w_q, w_out = head_q(wq, c, h), head_out(wo, c, h)
            grad_out = contract_rows(mix.astype(BF16), d_attn)
            d_o = times_transposed(d_attn, w_out).astype(BF16)
            delta = jnp.sum(d_o.astype(F32) * mix, axis=-1, keepdims=True)
            scores = times_transposed(q, kv_ref[:, :HEAD])
            probs = jnp.exp(jnp.where(allowed, scores - lse, MASKED))
            d_probs = times_transposed(d_o, kv_ref[:, HEAD:])
            d_scores = (probs * (d_probs - delta)).astype(BF16)
            d_query = matmul(d_scores, kv_ref[:, :HEAD]) * HEAD**-0.5
            probs_low = probs.astype(BF16)
            for some in range(0, d_kv_sum.shape[0], 2048):
                these = slice(some, some + 2048)
                d_kv_sum[these, :HEAD] += contract_rows(d_scores[:, these], q)
                d_kv_sum[these, HEAD:] += contract_rows(probs_low[:, these], d_o)
            d_qpre = unrotate(d_query, cos_ref[...], sin_ref[...]).astype(BF16)
            grad_q = contract_rows(lat, d_qpre)
            share = times_transposed(d_qpre, w_q)
            d_lat = share if d_lat is None else d_lat + share
            if sums:
                sums[0][c, h] += grad_q
                sums[1][c, h] = (sums[1][c, h].astype(F32) + grad_out).astype(BF16)
            else:
                store(c, h, grad_q, grad_out)
    if sums:

        @pl.when(step == steps - 1)
        def _():
            for c in range(2):
                for h in range(pair):
                    store(c, h, sums[0][c, h], sums[1][c, h])

    d_lat_sum[...] = d_lat
    share = d_lat.shape[1] // SQUARE
    dot = jnp.sum(d_lat * lat.astype(F32), axis=-1, keepdims=True)
    for m in range(SQUARE):
        b = corner ^ m
        columns = pl.ds(pl.multiple_of(b * share, share), share)
        d_lat_ref[m, :, :share] = d_lat_sum[:, columns].astype(BF16)
        d_lat_ref[m, :, share:] = jnp.broadcast_to(dot, (d_lat.shape[0], 128)).astype(BF16)

    @pl.when(step == steps - 1)
    def _():
        size = near_ref.shape[0]
        near_ref[...] = d_kv_sum[:size, :].astype(near_ref.dtype)
        far_ref[...] = d_kv_sum[size:, :].astype(BF16)


def attend_back(at, lat, tables, kv, keys, weights, q, o, lse, d_attn, block):
    near_q, far_q, near_out, far_out = weights
    layers = len(near_q)
    rows, rank = lat.shape
    count = kv.shape[0]
    _, tiles_q, rank_rows, half = near_q[0].shape
    per_layer, pair_rows, lanes = near_out[0].shape
    heads, width = tiles_q, per_layer * layers * lanes
    by_head = lambda size: pl.BlockSpec((heads, block, size), lambda i: (0, i, 0))
    whole = lambda dims: pl.BlockSpec(dims, lambda i: (0,) * len(dims))
    q_dims = (layers, SQUARE, tiles_q, rank_rows, half)
    out_dims = (layers, per_layer, pair_rows, lanes)
    d_lat_dims = (SQUARE, rows, rank // SQUARE + 128)
    pair = tiles_q // 2
    sums = []
    if rows != block:
        sums = [pltpu.VMEM((2, pair, rank, HEAD), F32), pltpu.VMEM((2, pair, HEAD, width), BF16)]
    return pl.pallas_call(
        functools.partial(attend_back_kernel, layers),
        grid=(rows // block,),
        in_specs=attend_specs(layers, block, rank, count)
        + [by_head(HEAD), by_head(HEAD), by_head(1), pl.BlockSpec((block, width), lambda i: (i, 0))],
        out_specs=[
            whole(q_dims),
            whole(q_dims),
            whole(out_dims),
            whole(out_dims),
            pl.BlockSpec((SQUARE, block, d_lat_dims[2]), lambda i: (0, i, 0)),
            whole((count // 2, 2 * HEAD)),
            whole((count // 2, 2 * HEAD)),
        ],
        out_shape=[
            shape(q_dims),
            shape(q_dims),
            shape(out_dims),
            shape(out_dims),
            shape(d_lat_dims),
            shape((count // 2, 2 * HEAD), BF16 if sums else F32),
            shape((count // 2, 2 * HEAD)),
        ],
        scratch_shapes=[
            pltpu.VMEM((2, layers * SQUARE, tiles_q, rank_rows, half), BF16),
            pltpu.VMEM((2, layers * per_layer, pair_rows, lanes), BF16),
            pltpu.SemaphoreType.DMA((2, 2, layers)),
            pltpu.VMEM((count, 2 * HEAD), F32),
            pltpu.VMEM((block, rank), F32),
        ]
        + sums,
        compiler_params=params(VMEM_LIMIT + len(sums) * 2**21),
        cost_estimate=pl.CostEstimate(
            flops=2 * rows * heads * HEAD * (5 * count + 2 * rank + 2 * width),
            bytes_accessed=12 * count * HEAD + 4 * heads * HEAD * (rank + width),
            transcendentals=rows * heads * count,
        ),
        name="attend_back",
    )(at, lat, *tables, kv, keys, *near_q, *far_q, *near_out, *far_out, q, o, lse, d_attn)


def latent_back_kernel(layers, at_ref, hat_ref, inverse_ref, d_kv_ref, x_ref, w_ref, *refs):
    parts = refs[:SQUARE]
    d_x_ref, near_ref, far_ref, d_sum = refs[SQUARE:]
    layer, corner, core = at_ref[0], at_ref[1], at_ref[2]
    count, width = x_ref.shape
    rows = count // SQUARE
    share = w_ref.shape[-1]
    rank_share = hat_ref.shape[1] // SQUARE
    for i in range(SQUARE):
        d_sum[i * rows : (i + 1) * rows] = sum(
            part[(i ^ m) * rows : (i ^ m) * rows + rows].astype(F32) for m, part in enumerate(parts)
        )
    columns = pl.ds(pl.multiple_of(corner * rank_share, rank_share), rank_share)
    dot = d_sum[:, rank_share : rank_share + 1] * (1.0 / hat_ref.shape[1])
    d_lat = inverse_ref[...] * (d_sum[:, :rank_share] - hat_ref[:, columns] * dot)
    d_down = jnp.concatenate([d_lat.astype(BF16), d_kv_ref[...]], axis=1)
    weight = w_ref[...].reshape(width, share)
    d_x_ref[...] = times_transposed(d_down, weight).astype(BF16)
    grad = contract_rows(x_ref[...], d_down)
    grad = grad.reshape(layers, SQUARE, 2, near_ref.shape[2], share)
    low, high = grad[:, :, 0], grad[:, :, 1]
    near = jnp.where(core == 0, low, high)
    far = jnp.where(core == 0, high, low).astype(BF16)
    for z in range(layers):
        k = lax.rem(layer + layers - z, layers)
        near_ref[k] = near[z]
        far_ref[k] = far[z]


def latent_back(at, hat, inverse, d_kv, x, weight, parts):
    count, width = x.shape
    places, _, lane_rows, share = weight.shape
    layers = places // SQUARE
    dims = (layers, SQUARE, lane_rows, share)
    return pl.pallas_call(
        functools.partial(latent_back_kernel, layers),
        in_specs=[SMEM] + [VMEM] * (5 + SQUARE),
        out_specs=[VMEM] * 3,
        out_shape=[shape((count, width)), shape(dims, F32), shape(dims)],
        scratch_shapes=[pltpu.VMEM(parts[0].shape, F32)],
        compiler_params=params(),
        cost_estimate=pl.CostEstimate(
            flops=4 * count * width * share, bytes_accessed=10 * width * share, transcendentals=0
        ),
        name="latent_back",
    )(at, hat, inverse, d_kv, x, weight, *parts)


def chunk(ref, corner, m, size):
    tiles = size // 128
    columns = [(t * SQUARE + (corner ^ m)) * 128 for t in range(tiles)]
    return jnp.concatenate([ref[:, pl.ds(pl.multiple_of(c, 128), 128)] for c in columns], axis=1)


def mlp_kernel(at_ref, h_ref, cot_ref, *refs):
    pieces = refs[: 2 * 3 * 5]
    d_h_ref, out_ref, act_near_ref, act_far_ref, weights, sems = refs[2 * 3 * 5 :]
    corner = at_ref[1]
    tiles, units = weights.shape[3], weights.shape[4]
    half = tiles // 2
    copies = []
    for c in range(2):
        for kind in range(3):
            one = []
            for i in range(5):
                target = weights.at[c, kind, min(i, 3)]
                if i >= 3:
                    target = target.at[pl.ds((i - 3) * half, half)]
                source = pieces[(c * 3 + kind) * 5 + i]
                one.append(pltpu.make_async_copy(source, target, sems.at[c, kind, i]))
            copies.append(one)
    for one in copies:
        for copy in one:
            copy.start()
    size = tiles * 128

    def weight(c, kind, m):
        return jnp.concatenate([weights[c, kind, m, t] for t in range(tiles)], axis=1)

    for c, acts in enumerate((act_near_ref, act_far_ref)):

        def product(value_ref, kind):
            for copy in copies[c * 3 + kind]:
                copy.wait()
            return sum(
                times_transposed(chunk(value_ref, corner, m, size), weight(c, kind, m))
                for m in range(SQUARE)
            )

        gate_act, up_proj, d_act = product(h_ref, 0), product(h_ref, 1), product(cot_ref, 2)
        sigmoid_gate = 1.0 / (1.0 + jnp.exp(-gate_act))
        silu_gate = gate_act * sigmoid_gate
        d_gate = d_act * up_proj * sigmoid_gate * (1.0 + gate_act * (1.0 - sigmoid_gate))
        acts[0] = d_gate.astype(BF16)
        acts[1] = (d_act * silu_gate).astype(BF16)
        acts[2] = (silu_gate * up_proj).astype(BF16)
    accumulators = (act_near_ref, act_far_ref)
    for m in range(SQUARE):
        d_h = sum(
            matmul(acts[kind], weight(c, kind, m))
            for c, acts in enumerate(accumulators)
            for kind in range(2)
        )
        out = sum(matmul(acts[2], weight(c, 2, m)) for c, acts in enumerate(accumulators))
        for t in range(tiles):
            here = pl.ds(pl.multiple_of((t * SQUARE + (corner ^ m)) * 128, 128), 128)
            d_h_ref[:, here] = d_h[:, t * 128 : (t + 1) * 128].astype(BF16)
            out_ref[:, here] = out[:, t * 128 : (t + 1) * 128].astype(BF16)


def mlp(at, h, cot, near, far):
    rows, width = h.shape
    tiles, units, lanes = near[0][0].shape
    low = shape((rows, width))
    acts = shape((3, rows, units))
    return pl.pallas_call(
        mlp_kernel,
        in_specs=[SMEM, VMEM, VMEM] + [HBM] * 30,
        out_specs=[VMEM] * 4,
        out_shape=[low, low, acts, acts],
        scratch_shapes=[
            pltpu.VMEM((2, 3, SQUARE, tiles, units, lanes), BF16),
            pltpu.SemaphoreType.DMA((2, 3, 5)),
        ],
        compiler_params=params(),
        cost_estimate=pl.CostEstimate(
            flops=24 * rows * width * units,
            bytes_accessed=12 * width * units + 8 * rows * width,
            transcendentals=2 * rows * units,
        ),
        name="mlp",
    )(at, h, cot, *[piece for side in (near, far) for kind in side for piece in kind])


ROUTES = (((1, 3), 0), ((0, 2), 0), ((2, 3), 1), ((0, 1), 1))


def unit_grads_kernel(at_ref, acts_ref, value_ref, *refs):
    more, outs = refs[: len(refs) - 4], refs[len(refs) - 4 :]
    corner = at_ref[1]
    half = outs[0].shape[1]
    acts = acts_ref[...]
    size = 2 * half * 128
    for m in range(SQUARE):
        grad = contract_rows(acts, chunk(value_ref, corner, m, size))
        for i, (flips, side) in enumerate(ROUTES):
            if m in flips:
                j = flips.index(m)
                for t in range(half):
                    column = (side * half + t) * 128
                    tile = grad[:, column : column + 128]
                    if more:
                        tile = tile + more[i][j, t].astype(F32)
                    outs[i][j, t] = tile.astype(BF16)


def unit_grads(at, acts, value, *more):
    rows, width = value.shape
    units = acts.shape[1]
    dims = (2, width // SQUARE // 256, units, 128)
    return pl.pallas_call(
        unit_grads_kernel,
        in_specs=[SMEM] + [VMEM] * (2 + len(more)),
        out_specs=[VMEM] * 4,
        out_shape=[shape(dims)] * 4,
        compiler_params=params(),
        cost_estimate=pl.CostEstimate(
            flops=2 * rows * width * units, bytes_accessed=2 * width * units * (1 + bool(more)), transcendentals=0
        ),
        name="unit_grads",
    )(at, acts, value, *more)


def local(
    chips,
    tokens,
    attn_gain,
    q_gain,
    w_qdown,
    w_qup,
    w_kv,
    w_out,
    mlp_gain,
    w_gate,
    w_up,
    w_down,
    cotangent,
    seq_lengths,
    block_slots,
):
    layers = chips // SQUARE
    rows, width = tokens.shape[0] // 2, tokens.shape[1]
    lanes = width // chips
    rank = w_qdown.shape[1]
    rank_rows = w_qup.shape[0]
    pair = w_qup.shape[1] // HEAD // SQUARE
    units = w_gate.shape[1] // layers
    half = HEAD // 2
    place = lax.axis_index("seq")
    core = lax.axis_index("tp")
    layer, corner = place // SQUARE, place % SQUARE
    at = jnp.stack([layer, corner, core]).astype(jnp.int32)
    first = core == 0
    lines = [[z * SQUARE + c for z in range(layers)] for c in range(SQUARE)]
    square_groups = [[z * SQUARE + c for c in range(SQUARE)] for z in range(layers)]

    def across(value):
        return lax.ppermute(value, "tp", [(0, 1), (1, 0)])

    def along(value, step):
        pairs = [
            (z * SQUARE + c, (z + step) % layers * SQUARE + c)
            for z in range(layers)
            for c in range(SQUARE)
        ]
        return lax.ppermute(value, "seq", pairs)

    def within(value, flip):
        return lax.ppermute(value, "seq", [(i, i ^ flip) for i in range(chips)])

    def line_exchange(value):
        return lax.all_to_all(value, "seq", 0, 0, axis_index_groups=lines, tiled=True)

    def square_exchange(value):
        return lax.all_to_all(value, "seq", 0, 0, axis_index_groups=square_groups, tiled=True)

    def line_pieces(value):
        return [value] + [along(value, k) for k in range(1, layers)]

    def line_sum(blocks):
        return blocks[0].astype(F32) + sum(
            along(blocks[k], -k).astype(F32) for k in range(1, layers)
        )

    def square_pieces(value):
        return [value] + [within(value, m) for m in range(1, SQUARE)]

    def square_sum(blocks):
        return blocks[0].astype(F32) + sum(
            within(blocks[m], m).astype(F32) for m in range(1, SQUARE)
        )

    def after(value, *earlier):
        return lax.optimization_barrier((value,) + earlier)[0]

    def own(pair_value):
        return lax.dynamic_slice_in_dim(pair_value, core * rows, rows, 0)

    def both(mine, theirs, axis=0):
        return jnp.concatenate(
            [jnp.where(first, mine, theirs), jnp.where(first, theirs, mine)], axis=axis
        )

    def tiled(value):
        if lanes == 128:
            return value
        count, size, _ = value.shape
        value = jnp.swapaxes(value, 0, 1).reshape(size, count * lanes // 128, 128)
        return jnp.swapaxes(value, 0, 1)

    def untiled(value):
        if lanes == 128:
            return value
        count, size, _ = value.shape
        value = jnp.swapaxes(value, 0, 1).reshape(size, count * 128 // lanes, lanes)
        return jnp.swapaxes(value, 0, 1)

    def arranged(value):
        if lanes == 128:
            return value
        shaped = value.reshape(value.shape[0], -1, 128 // lanes, SQUARE, lanes)
        return jnp.swapaxes(shaped, 2, 3).reshape(value.shape)

    def unarranged(value):
        if lanes == 128:
            return value
        shaped = value.reshape(value.shape[0], -1, SQUARE, 128 // lanes, lanes)
        return jnp.swapaxes(shaped, 2, 3).reshape(value.shape)

    inputs = own(tokens).astype(F32)
    x_inverse = inverse_rms(inputs)
    x_hat = inputs * x_inverse
    x_all = jnp.concatenate(square_pieces(x_hat.astype(BF16)))

    gain_rows = attn_gain.astype(F32)[:, None]
    down = jnp.concatenate([w_qdown, w_kv], axis=1)
    rank_share, kv_share = rank // SQUARE, 2 * HEAD // SQUARE

    def shares(value):
        return jnp.stack(
            [
                jnp.concatenate(
                    [
                        value[:, b * rank_share : (b + 1) * rank_share],
                        value[:, rank + b * kv_share : rank + (b + 1) * kv_share],
                    ],
                    axis=1,
                )
                for b in range(SQUARE)
            ]
        )

    def unshares(value):
        return jnp.concatenate(
            [value[b, :, :rank_share] for b in range(SQUARE)]
            + [value[b, :, rank_share:] for b in range(SQUARE)],
            axis=1,
        )

    down_scaled = (down.astype(F32) * gain_rows).astype(BF16)
    down_half = lax.dynamic_slice_in_dim(down_scaled, core * (lanes // 2), lanes // 2, 0)
    down_near = line_pieces(square_exchange(shares(down_half)))
    down_far = [across(piece) for piece in down_near]

    q_gain_rows = q_gain.astype(F32)[:, None]
    qup_scaled = (w_qup.astype(F32) * q_gain_rows).astype(BF16)
    qup_send = qup_scaled.reshape(rank_rows, SQUARE, 2 * pair, half)
    qup_send = jnp.transpose(qup_send, (1, 2, 0, 3))
    qup_own = square_exchange(after(qup_send, down_near[0]))
    out_own = square_exchange(w_out.reshape(SQUARE, pair * HEAD, lanes))
    qup_near = line_pieces(qup_own)
    qup_far = [across(piece) for piece in qup_near]
    out_near = line_pieces(tiled(after(out_own, qup_near[1])))
    out_far = [across(piece) for piece in out_near]
    head_weights = (qup_near, qup_far, out_near, out_far)

    mlp_gain_rows = mlp_gain.astype(F32)[:, None]
    gate_send = (w_gate.astype(F32) * mlp_gain_rows).astype(BF16).T
    up_send = (w_up.astype(F32) * mlp_gain_rows).astype(BF16).T
    mlp_near, mlp_far = [], []
    earlier = out_near[1]
    for sent in (gate_send, up_send, w_down):
        mine = line_exchange(after(sent, earlier).reshape(layers, units, lanes))
        earlier = mine
        mine = tiled(mine)
        size = mine.shape[0] // 2
        one, two = within(mine, 1), within(mine, 2)
        pieces = [mine, one, two, within(one[:size], 2), within(two[size:], 1)]
        mlp_near.append(pieces)
        mlp_far.append([across(piece) for piece in pieces])
    cot_own = own(cotangent)
    cot_all = jnp.concatenate(line_pieces(after(arranged(cot_own), earlier)))

    bounds = jnp.cumsum(seq_lengths)
    starts = bounds - seq_lengths

    def layout(blocks):
        natural = (blocks[:, None] * rows + jnp.arange(rows, dtype=jnp.int32)[None, :]).reshape(-1)
        member = (natural[:, None] >= starts[None, :]) & (natural[:, None] < bounds[None, :])
        return natural, jnp.sum(jnp.where(member, starts[None, :], 0), axis=1)

    back_steps = jnp.arange(layers, dtype=jnp.int32)
    flips = jnp.arange(SQUARE, dtype=jnp.int32)
    owners = (((layer - back_steps) % layers) * SQUARE)[None, :] + (corner ^ flips)[:, None]
    square_slots = block_slots[2 * owners[:, 0] + core]
    row_natural, row_start = layout(square_slots)
    owners = owners.reshape(-1)
    near_natural, _ = layout(block_slots[2 * owners + core])
    far_natural, _ = layout(block_slots[2 * owners + 1 - core])
    key_natural = jnp.concatenate([near_natural, far_natural])[None, :]
    cosine, sine = angles(row_natural - row_start)
    tables = (cosine, sine, row_natural[:, None], row_start[:, None])

    part, down_here = project(at, x_all, down_near, down_far)
    lat_hat, lat_low, lat_inverse, kv_own = latent(at, cosine, sine, square_pieces(part), rank)
    kv_line = jnp.concatenate(line_pieces(kv_own))
    kv_near = jnp.concatenate(square_pieces(kv_line))
    kv_all = jnp.concatenate([kv_near, across(kv_near)])

    block = max(32, min(SQUARE * rows, 2**30 // kv_all.shape[0] ** 2))
    queries, attn_mix, log_total, attn_part = attend(
        at, lat_low, tables, kv_all, key_natural, head_weights, block
    )
    hidden = inputs + square_sum(attn_part.reshape(SQUARE, rows, width))
    h_inverse = inverse_rms(hidden)
    h_hat = hidden * h_inverse
    h_all = jnp.concatenate(line_pieces(arranged(h_hat.astype(BF16))))

    d_h_part, mlp_part, acts_near, acts_far = mlp(at, h_all, cot_all, mlp_near, mlp_far)
    d_hscaled = unarranged(line_sum(d_h_part.reshape(layers, rows, width)))
    d_hidden = cot_own.astype(F32) + norm_back(d_hscaled, h_hat, h_inverse)
    d_attn_all = jnp.concatenate(square_pieces(d_hidden.astype(BF16)))
    mlp_own = unarranged(line_sum(mlp_part.reshape(layers, rows, width)))
    layer_own = (hidden + mlp_own).astype(BF16)
    layer_out = both(layer_own, across(layer_own))

    mlp_back = []
    for kind, value in ((0, h_all), (1, h_all), (2, cot_all)):
        far_grads = unit_grads(at, acts_far[kind], value)
        sent_a, kept_a, sent_b, kept_b = unit_grads(
            at, acts_near[kind], value, *[across(grad) for grad in far_grads]
        )
        sums = []
        for sent, kept, flip, next_flip in ((sent_a, kept_a, 1, 2), (sent_b, kept_b, 2, 1)):
            total = kept.astype(F32) + within(sent, flip).astype(F32)
            sums.append(total[0] + within(total[1].astype(BF16), next_flip).astype(F32))
        back = line_exchange(untiled(jnp.concatenate(sums).astype(BF16)))
        mlp_back.append(back.reshape(layers * units, lanes).astype(F32))
    gate_back, up_back, down_part = mlp_back[0].T, mlp_back[1].T, mlp_back[2]
    gate_part, up_part = gate_back * mlp_gain_rows, up_back * mlp_gain_rows
    mlp_gain_part = jnp.sum(gate_back * w_gate.astype(F32) + up_back * w_up.astype(F32), axis=1)

    grad_q_near, grad_q_far, grad_out_near, grad_out_far, d_lat_parts, d_kv_near, d_kv_far = attend_back(
        at, lat_low, tables, kv_all, key_natural, head_weights, queries, attn_mix, log_total, d_attn_all, block
    )
    d_kv_low = (d_kv_near.astype(F32) + across(d_kv_far).astype(F32)).astype(BF16)
    d_kv_line = square_sum(d_kv_low.reshape(SQUARE, layers * rows, 2 * HEAD)).astype(BF16)
    d_kv_own = line_sum(d_kv_line.reshape(layers, rows, 2 * HEAD))
    d_kv_own = jnp.concatenate(
        [unrotate(d_kv_own[:, :HEAD], cosine[:rows], sine[:rows]), d_kv_own[:, HEAD:]], axis=1
    ).astype(BF16)
    kv_share_of = lambda m: lax.dynamic_slice_in_dim(d_kv_own, (corner ^ m) * kv_share, kv_share, 1)
    d_kv_share = jnp.concatenate(
        [kv_share_of(0)] + [within(kv_share_of(m), m) for m in range(1, SQUARE)]
    )
    d_lat_received = [d_lat_parts[0]] + [within(d_lat_parts[m], m) for m in range(1, SQUARE)]

    d_x_part, down_grad_near, down_grad_far = latent_back(
        at, lat_hat, lat_inverse, d_kv_share, x_all, down_here, d_lat_received
    )
    d_xscaled = square_sum(d_x_part.reshape(SQUARE, rows, width))
    token_own = (d_hidden + norm_back(d_xscaled, x_hat, x_inverse)).astype(BF16)
    token_grad = both(token_own, across(token_own))
    down_sum = (down_grad_near + across(down_grad_far).astype(F32)).astype(BF16)
    down_back = unshares(square_exchange(line_sum(down_sum).astype(BF16))).astype(F32)
    down_back = both(down_back, across(down_back))
    attn_gain_part = jnp.sum(down_back * down.astype(F32), axis=1)
    down_grad = down_back * gain_rows
    qdown_part, kv_part = down_grad[:, :rank], down_grad[:, rank:]

    def head_back(near, far):
        total = (near.astype(F32) + across(far).astype(F32)).astype(BF16)
        return line_sum(total).astype(BF16)

    qup_back = square_exchange(head_back(grad_q_near, grad_q_far))
    qup_back = jnp.transpose(qup_back, (2, 0, 1, 3)).reshape(rank_rows, -1).astype(F32)
    out_back = square_exchange(untiled(head_back(grad_out_near, grad_out_far)))
    out_part = out_back.reshape(-1, lanes).astype(F32)
    qup_part = qup_back * q_gain_rows
    q_gain_half = jnp.sum(qup_back * w_qup.astype(F32), axis=1)
    gain_parts = jnp.concatenate([q_gain_half, mlp_gain_part])
    gain_parts = gain_parts + across(gain_parts)
    q_gain_part, mlp_gain_part = gain_parts[:rank_rows], gain_parts[rank_rows:]
    return (
        layer_out,
        token_grad,
        attn_gain_part,
        q_gain_part,
        qdown_part,
        qup_part,
        kv_part,
        out_part,
        mlp_gain_part,
        gate_part,
        up_part,
        down_part,
    )


def solution(mesh):
    in_specs = (
        P("seq", None),
        P("seq"),
        P("seq"),
        P("seq", None),
        P("seq", "tp"),
        P("seq", None),
        P("tp", "seq"),
        P("seq"),
        P("seq", "tp"),
        P("seq", "tp"),
        P("tp", "seq"),
        P("seq", None),
        P(),
        P(),
    )
    out_specs = (
        P("seq", None),
        P("seq", None),
        P("seq"),
        P("seq"),
        P("seq", None),
        P("seq", "tp"),
        P("seq", None),
        P("tp", "seq"),
        P("seq"),
        P("seq", "tp"),
        P("seq", "tp"),
        P("tp", "seq"),
    )
    body = functools.partial(local, mesh.shape["seq"])
    return jax.shard_map(body, mesh=mesh, in_specs=in_specs, out_specs=out_specs, check_vma=False)
```

```python
import functools
import math

import jax
import jax.numpy as jnp
from jax import lax
from jax.experimental import pallas as pl
from jax.experimental.pallas import tpu as pltpu
from jax.sharding import PartitionSpec as P

EPSILON = 1e-06
ROPE_BASE = 10000.0
MASKED = -1e30
HEAD = 256
SQUARE = 4
VMEM_LIMIT = 56 * 1024 * 1024
BF16 = jnp.bfloat16
F32 = jnp.float32


def matmul(left, right):
    return jnp.dot(left, right, preferred_element_type=F32)


def contract_rows(left, right):
    return lax.dot_general(left, right, (((0,), (0,)), ((), ())), preferred_element_type=F32)


def times_transposed(left, right):
    return lax.dot_general(left, right, (((1,), (1,)), ((), ())), preferred_element_type=F32)


def inverse_rms(vector):
    return lax.rsqrt(jnp.mean(vector * vector, axis=-1, keepdims=True) + EPSILON)


def norm_back(scaled_grad, normed, inverse):
    return inverse * (scaled_grad - normed * jnp.mean(scaled_grad * normed, axis=-1, keepdims=True))


def angles(position):
    half = HEAD // 2
    frequency = jnp.exp(jnp.arange(half, dtype=F32) * (-math.log(ROPE_BASE) / half))
    phase = position.astype(F32)[:, None] * frequency[None, :]
    return jnp.cos(phase), jnp.sin(phase)


def rotate(vector, cosine, sine):
    half = HEAD // 2
    front, back = vector[:, :half], vector[:, half:]
    return jnp.concatenate([front * cosine - back * sine, back * cosine + front * sine], axis=1)


def unrotate(vector, cosine, sine):
    return rotate(vector, cosine, -sine)


def params(limit=VMEM_LIMIT):
    return pltpu.CompilerParams(vmem_limit_bytes=limit)


VMEM = pl.BlockSpec(memory_space=pltpu.VMEM)
SMEM = pl.BlockSpec(memory_space=pltpu.SMEM)
HBM = pl.BlockSpec(memory_space=pl.ANY)


def shape(dims, dtype=BF16):
    return jax.ShapeDtypeStruct(tuple(dims), dtype)


def project_kernel(layers, at_ref, x_ref, *refs):
    near, far = refs[:layers], refs[layers : 2 * layers]
    part_ref, w_ref, sems = refs[2 * layers :]
    layer, core = at_ref[0], at_ref[2]
    copies = []
    for c, pieces in enumerate((near, far)):
        side = core if c == 0 else 1 - core
        for k, piece in enumerate(pieces):
            first = lax.rem(layer + layers - k, layers) * SQUARE
            target = w_ref.at[pl.ds(first, SQUARE), side]
            copies.append(pltpu.make_async_copy(piece, target, sems.at[c, k]))
    for copy in copies:
        copy.start()
    for copy in copies:
        copy.wait()
    width, share = x_ref.shape[1], w_ref.shape[-1]
    part_ref[...] = matmul(x_ref[...], w_ref[...].reshape(width, share)).astype(BF16)


def project(at, x, near, far):
    layers = len(near)
    rows, width = x.shape
    _, lane_rows, share = near[0].shape
    return pl.pallas_call(
        functools.partial(project_kernel, layers),
        in_specs=[SMEM, VMEM] + [HBM] * (2 * layers),
        out_specs=[VMEM, VMEM],
        out_shape=[
            shape((rows, share)),
            shape((layers * SQUARE, 2, lane_rows, share)),
        ],
        scratch_shapes=[pltpu.SemaphoreType.DMA((2, layers))],
        compiler_params=params(),
        cost_estimate=pl.CostEstimate(
            flops=2 * rows * width * share, bytes_accessed=4 * width * share, transcendentals=0
        ),
        name="project",
    )(at, x, *near, *far)


def latent_kernel(at_ref, cos_ref, sin_ref, *refs):
    parts = refs[:SQUARE]
    hat_ref, low_ref, inverse_ref, kv_ref, kv_sum = refs[SQUARE:]
    corner = at_ref[1]
    rows = kv_ref.shape[0]
    rank_share, kv_share = hat_ref.shape[1] // SQUARE, 2 * HEAD // SQUARE
    for m, part in enumerate(parts):
        b = corner ^ m
        columns = pl.ds(pl.multiple_of(b * rank_share, rank_share), rank_share)
        for i in range(SQUARE):
            source = slice((i ^ m) * rows, (i ^ m) * rows + rows)
            hat_ref[i * rows : (i + 1) * rows, columns] = part[source, :rank_share].astype(F32)
        columns = pl.ds(pl.multiple_of(b * kv_share, kv_share), kv_share)
        kv_sum[:, columns] = part[m * rows : (m + 1) * rows, rank_share:].astype(F32)
    q_lat = hat_ref[...]
    inverse = inverse_rms(q_lat)
    hat = q_lat * inverse
    hat_ref[...] = hat
    low_ref[...] = hat.astype(BF16)
    inverse_ref[...] = inverse
    kv_ref[:, :HEAD] = rotate(kv_sum[:, :HEAD], cos_ref[:rows], sin_ref[:rows]).astype(BF16)
    kv_ref[:, HEAD:] = kv_sum[:, HEAD:].astype(BF16)


def latent(at, cosine, sine, parts, rank):
    count = parts[0].shape[0]
    rows = count // SQUARE
    return pl.pallas_call(
        latent_kernel,
        in_specs=[SMEM] + [VMEM] * (2 + SQUARE),
        out_specs=[VMEM] * 4,
        out_shape=[
            shape((count, rank), F32),
            shape((count, rank)),
            shape((count, 1), F32),
            shape((rows, 2 * HEAD)),
        ],
        scratch_shapes=[pltpu.VMEM((rows, 2 * HEAD), F32)],
        compiler_params=params(),
        cost_estimate=pl.CostEstimate(flops=8 * count * rank, bytes_accessed=10 * count * rank, transcendentals=0),
        name="latent",
    )(at, cosine, sine, *parts)


def head_copies(refs, wq, wo, sems):
    copies = []
    for i, target in enumerate((wq, wo)):
        size = target.shape[2]
        for c in range(2):
            source = refs[2 * i + c]
            if source.shape[1] > size:
                skipped = 0 if i == 0 else source.shape[1] - size
                source = source.at[:, pl.ds(skipped, size)]
            copies.append(pltpu.make_async_copy(source, target.at[c], sems.at[i, c]))
    return copies


def head_q(wq, c, h, pair):
    size = wq.shape[2] // (2 * pair)
    halves = [wq[c, :, (2 * h + i) * size : (2 * h + i + 1) * size, :] for i in range(2)]
    return jnp.concatenate([half.reshape(-1, HEAD // 2) for half in halves], axis=1)


def head_out(wo, c, h):
    return jnp.concatenate(
        [wo[c, tile, h * HEAD : (h + 1) * HEAD, :] for tile in range(wo.shape[1])], axis=1
    )


def attend_kernel(
    lat_ref, cos_ref, sin_ref, natural_ref, start_ref, kv_ref, keys_ref, *refs
):
    weights, (q_ref, o_ref, lse_ref, part_ref, wq, wo, sems) = refs[:4], refs[4:]

    @pl.when(pl.program_id(0) == 0)
    def _():
        copies = head_copies(weights, wq, wo, sems)
        for copy in copies:
            copy.start()
        for copy in copies:
            copy.wait()

    keys = keys_ref[...]
    allowed = (keys <= natural_ref[...]) & (keys >= start_ref[...])
    pair = wo.shape[2] // HEAD
    part = None
    for c in range(2):
        for h in range(pair):
            q_pre = matmul(lat_ref[...], head_q(wq, c, h, pair))
            q = rotate(q_pre, cos_ref[...], sin_ref[...]).astype(BF16)
            q = (q.astype(F32) * HEAD**-0.5).astype(BF16)
            scores = jnp.where(allowed, times_transposed(q, kv_ref[:, :HEAD]), MASKED)
            top = jnp.max(scores, axis=-1, keepdims=True)
            terms = jnp.exp(scores - top)
            total = jnp.sum(terms, axis=-1, keepdims=True)
            mix = matmul(terms.astype(BF16), kv_ref[:, HEAD:]) / total
            q_ref[c * pair + h] = q
            o_ref[c * pair + h] = mix
            lse_ref[c * pair + h] = top + jnp.log(total)
            share = matmul(mix.astype(BF16), head_out(wo, c, h))
            part = share if part is None else part + share
    part_ref[...] = part.astype(BF16)


def attend_specs(block, rank, count):
    row = lambda size: pl.BlockSpec((block, size), lambda i: (i, 0))
    whole = lambda dims: pl.BlockSpec(dims, lambda i: (0,) * len(dims))
    half = HEAD // 2
    return [
        row(rank),
        row(half),
        row(half),
        row(1),
        row(1),
        whole((count, 2 * HEAD)),
        whole((1, count)),
    ] + [HBM] * 4


def attend(lat, tables, kv, keys, weights, pair, block):
    places, tiles, lanes = weights[0].shape[0], weights[2].shape[0], 128
    rows, rank = lat.shape
    count = kv.shape[0]
    q_rows = 2 * pair * rank // places
    heads, width = 2 * pair, tiles * lanes
    by_head = lambda size: pl.BlockSpec((heads, block, size), lambda i: (0, i, 0))
    return pl.pallas_call(
        attend_kernel,
        grid=(rows // block,),
        in_specs=attend_specs(block, rank, count),
        out_specs=[
            by_head(HEAD),
            by_head(HEAD),
            by_head(1),
            pl.BlockSpec((block, width), lambda i: (i, 0)),
        ],
        out_shape=[
            shape((heads, rows, HEAD)),
            shape((heads, rows, HEAD), F32),
            shape((heads, rows, 1), F32),
            shape((rows, width)),
        ],
        scratch_shapes=[
            pltpu.VMEM((2, places, q_rows, HEAD // 2), BF16),
            pltpu.VMEM((2, tiles, pair * HEAD, lanes), BF16),
            pltpu.SemaphoreType.DMA((2, 2)),
        ],
        compiler_params=params(),
        cost_estimate=pl.CostEstimate(
            flops=2 * rows * heads * HEAD * (2 * count + rank + width),
            bytes_accessed=4 * count * HEAD + 2 * heads * HEAD * (rank + width),
            transcendentals=rows * heads * count,
        ),
        name="attend",
    )(lat, *tables, kv, keys, *weights)


def attend_back_kernel(
    at_ref, lat_ref, cos_ref, sin_ref, natural_ref, start_ref, kv_ref, keys_ref, *refs
):
    weights, refs = refs[:4], refs[4:]
    q_ref, o_ref, lse_ref, d_attn_ref = refs[:4]
    joined = weights[0].shape[0] == weights[-1].shape[0]
    grads, refs = (refs[4:6], refs[6:]) if joined else (refs[4:8], refs[8:])
    grads_q, grads_out = grads[:2], grads[-2:]
    d_lat_ref, near_ref, far_ref, wq, wo, sems, d_kv_sum, d_lat_sum = refs[:8]
    sums = refs[8:]
    q_rows = wq.shape[2]
    skipped = q_rows if joined else 0
    pair = wo.shape[2] // HEAD
    step, steps = pl.program_id(0), pl.num_programs(0)
    corner = at_ref[1]

    @pl.when(step == 0)
    def _():
        copies = head_copies(weights, wq, wo, sems)
        for copy in copies:
            copy.start()
        d_kv_sum[...] = jnp.zeros_like(d_kv_sum)
        for total in sums:
            total[...] = jnp.zeros_like(total)
        for copy in copies:
            copy.wait()

    def store(c, h, grad_q, grad_out):
        size = q_rows // (2 * pair)
        for i in range(2):
            here = slice((2 * h + i) * size, (2 * h + i + 1) * size)
            tile = grad_q[:, i * 128 : (i + 1) * 128].astype(BF16)
            grads_q[c][:, here, :] = tile.reshape(-1, size, 128)
        here = slice(skipped + h * HEAD, skipped + (h + 1) * HEAD)
        for tile in range(wo.shape[1]):
            grads_out[c][tile, here, :] = grad_out[:, tile * 128 : (tile + 1) * 128].astype(BF16)

    keys = keys_ref[...]
    allowed = (keys <= natural_ref[...]) & (keys >= start_ref[...])
    d_attn, lat = d_attn_ref[...], lat_ref[...]
    d_lat = None
    for c in range(2):
        for h in range(pair):
            q, mix, lse = q_ref[c * pair + h], o_ref[c * pair + h], lse_ref[c * pair + h]
            w_q, w_out = head_q(wq, c, h, pair), head_out(wo, c, h)
            grad_out = contract_rows(mix.astype(BF16), d_attn)
            d_o = times_transposed(d_attn, w_out).astype(BF16)
            delta = jnp.sum(d_o.astype(F32) * mix, axis=-1, keepdims=True)
            scores = times_transposed(q, kv_ref[:, :HEAD])
            probs = jnp.exp(jnp.where(allowed, scores - lse, MASKED))
            d_probs = times_transposed(d_o, kv_ref[:, HEAD:])
            d_scores = (probs * (d_probs - delta)).astype(BF16)
            d_query = matmul(d_scores, kv_ref[:, :HEAD]) * HEAD**-0.5
            probs_low = probs.astype(BF16)
            for some in range(0, d_kv_sum.shape[0], 2048):
                these = slice(some, some + 2048)
                d_kv_sum[these, :HEAD] += contract_rows(d_scores[:, these], q)
                d_kv_sum[these, HEAD:] += contract_rows(probs_low[:, these], d_o)
            d_qpre = unrotate(d_query, cos_ref[...], sin_ref[...]).astype(BF16)
            grad_q = contract_rows(lat, d_qpre)
            share = times_transposed(d_qpre, w_q)
            d_lat = share if d_lat is None else d_lat + share
            if sums:
                sums[0][c, h] += grad_q
                sums[1][c, h] = (sums[1][c, h].astype(F32) + grad_out).astype(BF16)
            else:
                store(c, h, grad_q, grad_out)
    if sums:

        @pl.when(step == steps - 1)
        def _():
            for c in range(2):
                for h in range(pair):
                    store(c, h, sums[0][c, h], sums[1][c, h])

    d_lat_sum[...] = d_lat
    share = d_lat.shape[1] // SQUARE
    dot = jnp.sum(d_lat * lat.astype(F32), axis=-1, keepdims=True)
    for m in range(SQUARE):
        b = corner ^ m
        columns = pl.ds(pl.multiple_of(b * share, share), share)
        d_lat_ref[m, :, :share] = d_lat_sum[:, columns].astype(BF16)
        d_lat_ref[m, :, share:] = jnp.broadcast_to(dot, (d_lat.shape[0], 128)).astype(BF16)

    @pl.when(step == steps - 1)
    def _():
        size = near_ref.shape[0]
        near_ref[...] = d_kv_sum[:size, :].astype(near_ref.dtype)
        far_ref[...] = d_kv_sum[size:, :].astype(BF16)


def attend_back(at, lat, tables, kv, keys, weights, q, o, lse, d_attn, pair, block):
    places, tiles, lanes = weights[0].shape[0], weights[2].shape[0], 128
    rows, rank = lat.shape
    count = kv.shape[0]
    q_rows = 2 * pair * rank // places
    heads, width = 2 * pair, tiles * lanes
    by_head = lambda size: pl.BlockSpec((heads, block, size), lambda i: (0, i, 0))
    whole = lambda dims: pl.BlockSpec(dims, lambda i: (0,) * len(dims))
    grad_dims = [(places, q_rows, HEAD // 2)] * 2 + [(tiles, pair * HEAD, lanes)] * 2
    if places == tiles:
        grad_dims = [(places, q_rows + pair * HEAD, lanes)] * 2
    d_lat_dims = (SQUARE, rows, rank // SQUARE + 128)
    sums = []
    if rows != block:
        sums = [pltpu.VMEM((2, pair, rank, HEAD), F32), pltpu.VMEM((2, pair, HEAD, width), BF16)]
    return pl.pallas_call(
        attend_back_kernel,
        grid=(rows // block,),
        in_specs=[SMEM]
        + attend_specs(block, rank, count)
        + [by_head(HEAD), by_head(HEAD), by_head(1), pl.BlockSpec((block, width), lambda i: (i, 0))],
        out_specs=[
            *[whole(dims) for dims in grad_dims],
            pl.BlockSpec((SQUARE, block, d_lat_dims[2]), lambda i: (0, i, 0)),
            whole((count // 2, 2 * HEAD)),
            whole((count // 2, 2 * HEAD)),
        ],
        out_shape=[
            *[shape(dims) for dims in grad_dims],
            shape(d_lat_dims),
            shape((count // 2, 2 * HEAD), BF16 if sums else F32),
            shape((count // 2, 2 * HEAD)),
        ],
        scratch_shapes=[
            pltpu.VMEM((2, places, q_rows, HEAD // 2), BF16),
            pltpu.VMEM((2, tiles, pair * HEAD, lanes), BF16),
            pltpu.SemaphoreType.DMA((2, 2)),
            pltpu.VMEM((count, 2 * HEAD), F32),
            pltpu.VMEM((block, rank), F32),
        ]
        + sums,
        compiler_params=params(VMEM_LIMIT + len(sums) * 2**21),
        cost_estimate=pl.CostEstimate(
            flops=2 * rows * heads * HEAD * (5 * count + 2 * rank + 2 * width),
            bytes_accessed=12 * count * HEAD + 4 * heads * HEAD * (rank + width),
            transcendentals=rows * heads * count,
        ),
        name="attend_back",
    )(at, lat, *tables, kv, keys, *weights, q, o, lse, d_attn)


def latent_back_kernel(layers, at_ref, hat_ref, inverse_ref, d_kv_ref, x_ref, w_ref, *refs):
    parts = refs[:SQUARE]
    d_x_ref, near_ref, far_ref, d_sum = refs[SQUARE:]
    layer, corner, core = at_ref[0], at_ref[1], at_ref[2]
    count, width = x_ref.shape
    rows = count // SQUARE
    share = w_ref.shape[-1]
    rank_share = hat_ref.shape[1] // SQUARE
    for i in range(SQUARE):
        d_sum[i * rows : (i + 1) * rows] = sum(
            part[(i ^ m) * rows : (i ^ m) * rows + rows].astype(F32) for m, part in enumerate(parts)
        )
    columns = pl.ds(pl.multiple_of(corner * rank_share, rank_share), rank_share)
    dot = d_sum[:, rank_share : rank_share + 1] * (1.0 / hat_ref.shape[1])
    d_lat = inverse_ref[...] * (d_sum[:, :rank_share] - hat_ref[:, columns] * dot)
    d_down = jnp.concatenate([d_lat.astype(BF16), d_kv_ref[...]], axis=1)
    weight = w_ref[...].reshape(width, share)
    d_x_ref[...] = times_transposed(d_down, weight).astype(BF16)
    grad = contract_rows(x_ref[...], d_down)
    grad = grad.reshape(layers, SQUARE, 2, near_ref.shape[2], share)
    low, high = grad[:, :, 0], grad[:, :, 1]
    near = jnp.where(core == 0, low, high)
    far = jnp.where(core == 0, high, low).astype(BF16)
    for z in range(layers):
        k = lax.rem(layer + layers - z, layers)
        near_ref[k] = near[z]
        far_ref[k] = far[z]


def latent_back(at, hat, inverse, d_kv, x, weight, parts):
    count, width = x.shape
    places, _, lane_rows, share = weight.shape
    layers = places // SQUARE
    dims = (layers, SQUARE, lane_rows, share)
    return pl.pallas_call(
        functools.partial(latent_back_kernel, layers),
        in_specs=[SMEM] + [VMEM] * (5 + SQUARE),
        out_specs=[VMEM] * 3,
        out_shape=[shape((count, width)), shape(dims, F32), shape(dims)],
        scratch_shapes=[pltpu.VMEM(parts[0].shape, F32)],
        compiler_params=params(),
        cost_estimate=pl.CostEstimate(
            flops=4 * count * width * share, bytes_accessed=10 * width * share, transcendentals=0
        ),
        name="latent_back",
    )(at, hat, inverse, d_kv, x, weight, *parts)


def chunk(ref, q, tiles):
    columns = [(t * SQUARE + q) * 128 for t in range(tiles)]
    return jnp.concatenate([ref[:, c : c + 128] for c in columns], axis=1)


def mlp_kernel(h_ref, cot_ref, *refs):
    d_h_ref, out_ref, act_near_ref, act_far_ref, weights, sems = refs[2:]
    tiles, units = weights.shape[3:5]
    copies = [
        [
            pltpu.make_async_copy(
                refs[c].at[:, :, pl.ds(kind * units, units)], weights.at[c, kind], sems.at[c, kind]
            )
            for kind in range(3)
        ]
        for c in range(2)
    ]
    for one in copies:
        for copy in one:
            copy.start()

    def weight(c, kind, q):
        return jnp.concatenate([weights[c, kind, q, t] for t in range(tiles)], axis=1)

    sides = (act_near_ref, act_far_ref)
    for c, acts in enumerate(sides):

        def product(value_ref, kind):
            copies[c][kind].wait()
            return sum(
                times_transposed(chunk(value_ref, q, tiles), weight(c, kind, q)) for q in range(SQUARE)
            )

        gate_act, up_proj, d_act = product(h_ref, 0), product(h_ref, 1), product(cot_ref, 2)
        sigmoid_gate = 1.0 / (1.0 + jnp.exp(-gate_act))
        silu_gate = gate_act * sigmoid_gate
        d_gate = d_act * up_proj * sigmoid_gate * (1.0 + gate_act * (1.0 - sigmoid_gate))
        acts[0] = d_gate.astype(BF16)
        acts[1] = (d_act * silu_gate).astype(BF16)
        acts[2] = (silu_gate * up_proj).astype(BF16)
    for q in range(SQUARE):
        d_h = sum(
            matmul(acts[kind], weight(c, kind, q)) for c, acts in enumerate(sides) for kind in range(2)
        )
        out = sum(matmul(acts[2], weight(c, 2, q)) for c, acts in enumerate(sides))
        for t in range(tiles):
            here = slice((t * SQUARE + q) * 128, (t * SQUARE + q + 1) * 128)
            d_h_ref[:, here] = d_h[:, t * 128 : (t + 1) * 128].astype(BF16)
            out_ref[:, here] = out[:, t * 128 : (t + 1) * 128].astype(BF16)


def mlp(h, cot, near, far):
    rows, width = h.shape
    _, tiles, units, lanes = near.shape
    units = units // 3
    low = shape((rows, width))
    acts = shape((3, rows, units))
    return pl.pallas_call(
        mlp_kernel,
        in_specs=[VMEM, VMEM, HBM, HBM],
        out_specs=[VMEM] * 4,
        out_shape=[low, low, acts, acts],
        scratch_shapes=[
            pltpu.VMEM((2, 3, SQUARE, tiles, units, lanes), BF16),
            pltpu.SemaphoreType.DMA((2, 3)),
        ],
        compiler_params=params(),
        cost_estimate=pl.CostEstimate(
            flops=24 * rows * width * units,
            bytes_accessed=12 * width * units + 8 * rows * width,
            transcendentals=2 * rows * units,
        ),
        name="mlp",
    )(h, cot, near, far)


def unit_grads_kernel(acts_ref, value_ref, *refs):
    more, out_ref = refs[:-1], refs[-1]
    acts = acts_ref[0]
    tiles = out_ref.shape[1]
    for q in range(SQUARE):
        grad = contract_rows(acts, chunk(value_ref, q, tiles))
        for t in range(tiles):
            tile = grad[:, t * 128 : (t + 1) * 128]
            if more:
                tile = tile + more[0][q, t].astype(F32)
            out_ref[q, t] = tile.astype(BF16)


def unit_grads(acts, kind, value, received=None, kinds=None):
    rows, width = value.shape
    units = acts.shape[2]
    tiles = width // SQUARE // 128
    whole = lambda dims: pl.BlockSpec(dims, lambda i: (0,) * len(dims))
    dims = (SQUARE, tiles, units, 128)
    in_specs = [pl.BlockSpec((1, rows, units), lambda i: (kind, 0, 0)), whole((rows, width))]
    args, aliases, body = [acts, value], {}, unit_grads_kernel
    out_specs, out_dims = whole(dims), dims
    if received is not None:
        args.append(received)
        in_specs.append(whole(dims))
        out_specs = pl.BlockSpec(dims, lambda i: (0, 0, kind, 0))
        out_dims = (SQUARE, tiles, 3 * units, 128)
    if kinds is not None:
        args.append(kinds)
        in_specs.append(HBM)
        aliases = {3: 0}
        body = lambda a, v, r, k, o: unit_grads_kernel(a, v, r, o)
    return pl.pallas_call(
        body,
        grid=(1,),
        in_specs=in_specs,
        out_specs=out_specs,
        out_shape=shape(out_dims),
        input_output_aliases=aliases,
        compiler_params=params(),
        cost_estimate=pl.CostEstimate(
            flops=2 * rows * width * units, bytes_accessed=4 * width * units, transcendentals=0
        ),
        name="unit_grads",
    )(*args)


def local(
    chips,
    tokens,
    attn_gain,
    q_gain,
    w_qdown,
    w_qup,
    w_kv,
    w_out,
    mlp_gain,
    w_gate,
    w_up,
    w_down,
    cotangent,
    seq_lengths,
    block_slots,
):
    layers = chips // SQUARE
    rows, width = tokens.shape[0] // 2, tokens.shape[1]
    lanes = width // chips
    rank = w_qdown.shape[1]
    rank_rows = w_qup.shape[0]
    pair = w_qup.shape[1] // HEAD // SQUARE
    units = w_gate.shape[1] // layers
    half = HEAD // 2
    place = lax.axis_index("seq")
    core = lax.axis_index("tp")
    layer, corner = place // SQUARE, place % SQUARE
    at = jnp.stack([layer, corner, core]).astype(jnp.int32)
    first = core == 0
    lines = [[z * SQUARE + c for z in range(layers)] for c in range(SQUARE)]
    square_groups = [[z * SQUARE + c for c in range(SQUARE)] for z in range(layers)]

    def across(value):
        return lax.ppermute(value, "tp", [(0, 1), (1, 0)])

    def along(value, step):
        pairs = [
            (z * SQUARE + c, (z + step) % layers * SQUARE + c)
            for z in range(layers)
            for c in range(SQUARE)
        ]
        return lax.ppermute(value, "seq", pairs)

    def within(value, flip):
        return lax.ppermute(value, "seq", [(i, i ^ flip) for i in range(chips)])

    def line_exchange(value):
        return lax.all_to_all(value, "seq", 0, 0, axis_index_groups=lines, tiled=True)

    def square_exchange(value):
        return lax.all_to_all(value, "seq", 0, 0, axis_index_groups=square_groups, tiled=True)

    def line_pieces(value):
        return [value] + [along(value, k) for k in range(1, layers)]

    def line_sum(blocks):
        return blocks[0].astype(F32) + sum(
            along(blocks[k], -k).astype(F32) for k in range(1, layers)
        )

    def by_layer(value):
        blocks = value.reshape(layers, rows, -1)
        return jnp.concatenate(
            [
                lax.dynamic_index_in_dim(blocks, (layer - z) % layers, 0, keepdims=False)
                for z in range(layers)
            ]
        )

    def square_pieces(value):
        return [value] + [within(value, m) for m in range(1, SQUARE)]

    def square_sum(blocks):
        return blocks[0].astype(F32) + sum(
            within(blocks[m], m).astype(F32) for m in range(1, SQUARE)
        )

    def after(value, *earlier):
        return lax.optimization_barrier((value,) + earlier)[0]

    def together(*values):
        return lax.optimization_barrier(values)

    def own(pair_value):
        return lax.dynamic_slice_in_dim(pair_value, core * rows, rows, 0)

    def both(mine, theirs, axis=0):
        return jnp.concatenate(
            [jnp.where(first, mine, theirs), jnp.where(first, theirs, mine)], axis=axis
        )

    def tiled(value):
        if lanes == 128:
            return value
        count, size, _ = value.shape
        value = jnp.swapaxes(value, 0, 1).reshape(size, count * lanes // 128, 128)
        return jnp.swapaxes(value, 0, 1)

    def untiled(value):
        if lanes == 128:
            return value
        count, size, _ = value.shape
        value = jnp.swapaxes(value, 0, 1).reshape(size, count * 128 // lanes, lanes)
        return jnp.swapaxes(value, 0, 1)

    def arranged(value):
        if lanes == 128:
            return value
        shaped = value.reshape(value.shape[0], -1, 128 // lanes, SQUARE, lanes)
        return jnp.swapaxes(shaped, 2, 3).reshape(value.shape)

    def unarranged(value):
        if lanes == 128:
            return value
        shaped = value.reshape(value.shape[0], -1, SQUARE, 128 // lanes, lanes)
        return jnp.swapaxes(shaped, 2, 3).reshape(value.shape)

    inputs = own(tokens).astype(F32)
    x_inverse = inverse_rms(inputs)
    x_hat = inputs * x_inverse
    x_all = jnp.concatenate(square_pieces(x_hat.astype(BF16)))

    gain_rows = attn_gain.astype(F32)[:, None]
    down = jnp.concatenate([w_qdown, w_kv], axis=1)
    rank_share, kv_share = rank // SQUARE, 2 * HEAD // SQUARE

    def shares(value):
        return jnp.stack(
            [
                jnp.concatenate(
                    [
                        value[:, b * rank_share : (b + 1) * rank_share],
                        value[:, rank + b * kv_share : rank + (b + 1) * kv_share],
                    ],
                    axis=1,
                )
                for b in range(SQUARE)
            ]
        )

    def unshares(value):
        return jnp.concatenate(
            [value[b, :, :rank_share] for b in range(SQUARE)]
            + [value[b, :, rank_share:] for b in range(SQUARE)],
            axis=1,
        )

    down_scaled = (down.astype(F32) * gain_rows).astype(BF16)
    down_half = lax.dynamic_slice_in_dim(down_scaled, core * (lanes // 2), lanes // 2, 0)
    cot_own = own(cotangent)
    cot_pieces = line_pieces(arranged(cot_own))
    cot_all = by_layer(jnp.concatenate(cot_pieces))
    down_own = square_exchange(shares(down_half))
    down_near = line_pieces(after(down_own, *cot_pieces[1:]))
    down_far = [across(piece) for piece in down_near]

    q_gain_rows = q_gain.astype(F32)[:, None]
    qup_scaled = (w_qup.astype(F32) * q_gain_rows).astype(BF16)
    qup_send = qup_scaled.reshape(rank_rows, SQUARE, 2 * pair, half)
    qup_send = jnp.transpose(qup_send, (1, 2, 0, 3)).reshape(SQUARE, -1, lanes)
    qup_size = qup_send.shape[1]
    head_send = jnp.concatenate([qup_send, w_out.reshape(SQUARE, pair * HEAD, lanes)], axis=1)
    head_own = square_exchange(after(head_send, down_own))

    mlp_gain_rows = mlp_gain.astype(F32)[:, None]
    gate_send = (w_gate.astype(F32) * mlp_gain_rows).astype(BF16).T
    up_send = (w_up.astype(F32) * mlp_gain_rows).astype(BF16).T
    mlp_send = jnp.concatenate(
        [value.reshape(layers, units, lanes) for value in (gate_send, up_send, w_down)], axis=1
    )

    bounds = jnp.cumsum(seq_lengths)
    starts = bounds - seq_lengths

    def layout(blocks):
        natural = (blocks[:, None] * rows + jnp.arange(rows, dtype=jnp.int32)[None, :]).reshape(-1)
        member = (natural[:, None] >= starts[None, :]) & (natural[:, None] < bounds[None, :])
        return natural, jnp.sum(jnp.where(member, starts[None, :], 0), axis=1)

    back_steps = jnp.arange(layers, dtype=jnp.int32)
    flips = jnp.arange(SQUARE, dtype=jnp.int32)
    owners = (((layer - back_steps) % layers) * SQUARE)[None, :] + (corner ^ flips)[:, None]
    square_slots = block_slots[2 * owners[:, 0] + core]
    row_natural, row_start = layout(square_slots)
    owners = owners.reshape(-1)
    near_natural, _ = layout(block_slots[2 * owners + core])
    far_natural, _ = layout(block_slots[2 * owners + 1 - core])
    key_natural = jnp.concatenate([near_natural, far_natural])[None, :]
    cosine, sine = angles(row_natural - row_start)
    tables = (cosine, sine, row_natural[:, None], row_start[:, None])

    x_all = after(x_all, head_own)
    part, down_here = project(at, x_all, down_near, down_far)
    lat_hat, lat_low, lat_inverse, kv_own = latent(at, cosine, sine, square_pieces(part), rank)
    mlp_layer = line_exchange(after(mlp_send, *down_near[1:]))
    mlp_layer, kv_own = together(mlp_layer, kv_own)
    kv_line = jnp.concatenate(line_pieces(kv_own))
    mlp_near = lax.all_gather(tiled(mlp_layer), "seq", axis_index_groups=square_groups)

    head_near = line_exchange(jnp.tile(after(head_own, mlp_layer, kv_line), (layers, 1, 1)))
    kv_near = jnp.concatenate(square_pieces(kv_line))
    kv_all = jnp.concatenate([kv_near, across(kv_near)])
    head_near, kv_all = together(head_near, kv_all)
    head_far = across(head_near)
    if lanes == 128:
        head_weights = (head_near, head_far, head_near, head_far)
    else:
        head_weights = tuple(
            side[:, :qup_size].reshape(chips, -1, half) for side in (head_near, head_far)
        ) + tuple(tiled(side[:, qup_size:]) for side in (head_near, head_far))

    block = max(32, min(SQUARE * rows, 2**30 // kv_all.shape[0] ** 2))
    queries, attn_mix, log_total, attn_part = attend(
        lat_low, tables, kv_all, key_natural, head_weights, pair, block
    )
    mlp_near, attn_part = together(mlp_near, attn_part)
    mlp_far = across(mlp_near)
    hidden = inputs + square_sum(attn_part.reshape(SQUARE, rows, width))
    h_inverse = inverse_rms(hidden)
    h_hat = hidden * h_inverse
    h_low = h_hat.astype(BF16)
    h_all = jnp.concatenate(line_pieces(arranged(h_low)))
    h_all = by_layer(h_all)

    d_h_part, mlp_part, acts_near, acts_far = mlp(h_all, cot_all, mlp_near, mlp_far)
    def line_blocks(value):
        return line_exchange(value.reshape(layers, rows, width))

    def line_total(blocks):
        return unarranged(jnp.sum(blocks.astype(F32), axis=0))

    mlp_grads = None
    for kind, value in ((0, h_all), (1, h_all), (2, cot_all)):
        received = across(unit_grads(acts_far, kind, value))
        mlp_grads = unit_grads(acts_near, kind, value, received, mlp_grads)
    d_h_lines, mlp_grads = together(line_blocks(d_h_part), mlp_grads)
    d_hscaled = line_total(d_h_lines)
    d_hidden = cot_own.astype(F32) + norm_back(d_hscaled, h_hat, h_inverse)
    mlp_sum = lax.psum_scatter(mlp_grads, "seq", axis_index_groups=square_groups)
    mlp_lines = line_blocks(after(mlp_part, d_hscaled))
    d_attn_all = jnp.concatenate(square_pieces(d_hidden.astype(BF16)))

    *head_grads, d_lat_parts, d_kv_near, d_kv_far = attend_back(
        at,
        lat_low,
        tables,
        kv_all,
        key_natural,
        head_weights,
        queries,
        attn_mix,
        log_total,
        d_attn_all,
        pair,
        block,
    )
    head_grads = list(head_grads)
    side = len(head_grads) // 2
    head_total = [
        (head_grads[2 * i].astype(F32) + across(head_grads[2 * i + 1]).astype(F32)).astype(BF16)
        for i in range(side)
    ]
    if lanes == 128:
        head_total = head_total[0]
    else:
        head_total = jnp.concatenate(
            [head_total[0].reshape(chips, -1, lanes), untiled(head_total[1])], axis=1
        )
    d_kv_near, head_total, mlp_lines = together(d_kv_near, head_total, mlp_lines)
    layer_out_own = (hidden + line_total(mlp_lines)).astype(BF16)
    layer_out = both(layer_out_own, across(layer_out_own))

    head_q = line_exchange(head_total[:, :qup_size])
    d_kv_low = (d_kv_near.astype(F32) + across(d_kv_far).astype(F32)).astype(BF16)
    d_kv_line = square_sum(d_kv_low.reshape(SQUARE, layers * rows, 2 * HEAD)).astype(BF16)
    head_q, d_kv_line = together(head_q, d_kv_line)
    d_kv_own = line_sum(d_kv_line.reshape(layers, rows, 2 * HEAD))
    d_kv_own = jnp.concatenate(
        [unrotate(d_kv_own[:, :HEAD], cosine[:rows], sine[:rows]), d_kv_own[:, HEAD:]], axis=1
    ).astype(BF16)
    head_out_lines = line_exchange(after(head_total[:, qup_size:], d_kv_own))
    kv_share_of = lambda m: lax.dynamic_slice_in_dim(d_kv_own, (corner ^ m) * kv_share, kv_share, 1)
    d_kv_share = jnp.concatenate(
        [kv_share_of(0)] + [within(kv_share_of(m), m) for m in range(1, SQUARE)]
    )
    d_lat_received = [d_lat_parts[0]] + [within(d_lat_parts[m], m) for m in range(1, SQUARE)]

    d_x_part, down_grad_near, down_grad_far = latent_back(
        at, lat_hat, lat_inverse, d_kv_share, x_all, down_here, d_lat_received
    )
    d_xscaled = square_sum(d_x_part.reshape(SQUARE, rows, width))
    head_out_lines, d_xscaled = together(head_out_lines, d_xscaled)
    mlp_back = line_exchange(untiled(after(mlp_sum, head_out_lines)))
    token_own = (d_hidden + norm_back(d_xscaled, x_hat, x_inverse)).astype(BF16)
    token_grad = both(token_own, across(token_own))
    down_sum = (down_grad_near + across(down_grad_far).astype(F32)).astype(BF16)
    down_line, mlp_back = together(line_sum(down_sum).astype(BF16), mlp_back)
    down_back = unshares(square_exchange(down_line)).astype(F32)
    down_back = both(down_back, across(down_back))
    attn_gain_part = jnp.sum(down_back * down.astype(F32), axis=1)
    down_grad = down_back * gain_rows
    qdown_part, kv_part = down_grad[:, :rank], down_grad[:, rank:]

    gate_back, up_back, down_part = (
        mlp_back[:, kind * units : (kind + 1) * units].reshape(layers * units, lanes).astype(F32)
        for kind in range(3)
    )
    gate_back, up_back = gate_back.T, up_back.T
    gate_part, up_part = gate_back * mlp_gain_rows, up_back * mlp_gain_rows
    mlp_gain_part = jnp.sum(gate_back * w_gate.astype(F32) + up_back * w_up.astype(F32), axis=1)

    head_lines = jnp.concatenate([head_q, head_out_lines], axis=1)
    head_lines = head_lines.reshape(layers, SQUARE, -1, lanes).astype(F32)
    head_sum = square_exchange(jnp.sum(head_lines, axis=0).astype(BF16))
    qup_back = head_sum[:, :qup_size].reshape(SQUARE, 2 * pair, rank_rows, half)
    qup_back = jnp.transpose(qup_back, (2, 0, 1, 3)).reshape(rank_rows, -1).astype(F32)
    out_part = head_sum[:, qup_size:].reshape(-1, lanes).astype(F32)
    qup_part = qup_back * q_gain_rows
    q_gain_half = jnp.sum(qup_back * w_qup.astype(F32), axis=1)
    gain_parts = jnp.concatenate([q_gain_half, mlp_gain_part])
    gain_parts = gain_parts + across(gain_parts)
    q_gain_part, mlp_gain_part = gain_parts[:rank_rows], gain_parts[rank_rows:]
    return (
        layer_out,
        token_grad,
        attn_gain_part,
        q_gain_part,
        qdown_part,
        qup_part,
        kv_part,
        out_part,
        mlp_gain_part,
        gate_part,
        up_part,
        down_part,
    )


def solution(mesh):
    in_specs = (
        P("seq", None),
        P("seq"),
        P("seq"),
        P("seq", None),
        P("seq", "tp"),
        P("seq", None),
        P("tp", "seq"),
        P("seq"),
        P("seq", "tp"),
        P("seq", "tp"),
        P("tp", "seq"),
        P("seq", None),
        P(),
        P(),
    )
    out_specs = (
        P("seq", None),
        P("seq", None),
        P("seq"),
        P("seq"),
        P("seq", None),
        P("seq", "tp"),
        P("seq", None),
        P("tp", "seq"),
        P("seq"),
        P("seq", "tp"),
        P("seq", "tp"),
        P("tp", "seq"),
    )
    body = functools.partial(local, mesh.shape["seq"])
    return jax.shard_map(body, mesh=mesh, in_specs=in_specs, out_specs=out_specs, check_vma=False)
```

```python
import functools
import math

import jax
import jax.numpy as jnp
from jax import lax
from jax.experimental import pallas as pl
from jax.experimental.pallas import tpu as pltpu
from jax.sharding import PartitionSpec as P

EPSILON = 1e-06
ROPE_BASE = 10000.0
MASKED = -1e30
HEAD = 256
SQUARE = 4
VMEM_LIMIT = 56 * 1024 * 1024
BF16 = jnp.bfloat16
F32 = jnp.float32


def matmul(left, right):
    return jnp.dot(left, right, preferred_element_type=F32)


def contract_rows(left, right):
    return lax.dot_general(left, right, (((0,), (0,)), ((), ())), preferred_element_type=F32)


def times_transposed(left, right):
    return lax.dot_general(left, right, (((1,), (1,)), ((), ())), preferred_element_type=F32)


def inverse_rms(vector):
    return lax.rsqrt(jnp.mean(vector * vector, axis=-1, keepdims=True) + EPSILON)


def norm_back(scaled_grad, normed, inverse):
    return inverse * (scaled_grad - normed * jnp.mean(scaled_grad * normed, axis=-1, keepdims=True))


def angles(position):
    half = HEAD // 2
    frequency = jnp.exp(jnp.arange(half, dtype=F32) * (-math.log(ROPE_BASE) / half))
    phase = position.astype(F32)[:, None] * frequency[None, :]
    return jnp.cos(phase), jnp.sin(phase)


def rotate(vector, cosine, sine):
    half = HEAD // 2
    front, back = vector[:, :half], vector[:, half:]
    return jnp.concatenate([front * cosine - back * sine, back * cosine + front * sine], axis=1)


def unrotate(vector, cosine, sine):
    return rotate(vector, cosine, -sine)


def params(limit=VMEM_LIMIT):
    return pltpu.CompilerParams(vmem_limit_bytes=limit)


VMEM = pl.BlockSpec(memory_space=pltpu.VMEM)
SMEM = pl.BlockSpec(memory_space=pltpu.SMEM)
HBM = pl.BlockSpec(memory_space=pl.ANY)


def shape(dims, dtype=BF16):
    return jax.ShapeDtypeStruct(tuple(dims), dtype)


def project_kernel(layers, at_ref, x_ref, *refs):
    near, far = refs[:layers], refs[layers : 2 * layers]
    part_ref, w_ref, sems = refs[2 * layers :]
    layer, core = at_ref[0], at_ref[2]
    copies = []
    for c, pieces in enumerate((near, far)):
        side = core if c == 0 else 1 - core
        for k, piece in enumerate(pieces):
            first = lax.rem(layer + layers - k, layers) * SQUARE
            target = w_ref.at[pl.ds(first, SQUARE), side]
            copies.append(pltpu.make_async_copy(piece, target, sems.at[c, k]))
    for copy in copies:
        copy.start()
    for copy in copies:
        copy.wait()
    width, share = x_ref.shape[1], w_ref.shape[-1]
    part_ref[...] = matmul(x_ref[...], w_ref[...].reshape(width, share)).astype(BF16)


def project(at, x, near, far):
    layers = len(near)
    rows, width = x.shape
    _, lane_rows, share = near[0].shape
    return pl.pallas_call(
        functools.partial(project_kernel, layers),
        in_specs=[SMEM, VMEM] + [HBM] * (2 * layers),
        out_specs=[VMEM, VMEM],
        out_shape=[
            shape((rows, share)),
            shape((layers * SQUARE, 2, lane_rows, share)),
        ],
        scratch_shapes=[pltpu.SemaphoreType.DMA((2, layers))],
        compiler_params=params(),
        cost_estimate=pl.CostEstimate(
            flops=2 * rows * width * share, bytes_accessed=4 * width * share, transcendentals=0
        ),
        name="project",
    )(at, x, *near, *far)


def latent_kernel(at_ref, cos_ref, sin_ref, *refs):
    parts = refs[:SQUARE]
    hat_ref, low_ref, inverse_ref, kv_ref, kv_sum = refs[SQUARE:]
    corner = at_ref[1]
    rows = kv_ref.shape[0]
    rank_share, kv_share = hat_ref.shape[1] // SQUARE, 2 * HEAD // SQUARE
    for m, part in enumerate(parts):
        b = corner ^ m
        columns = pl.ds(pl.multiple_of(b * rank_share, rank_share), rank_share)
        for i in range(SQUARE):
            source = slice((i ^ m) * rows, (i ^ m) * rows + rows)
            hat_ref[i * rows : (i + 1) * rows, columns] = part[source, :rank_share].astype(F32)
        columns = pl.ds(pl.multiple_of(b * kv_share, kv_share), kv_share)
        kv_sum[:, columns] = part[m * rows : (m + 1) * rows, rank_share:].astype(F32)
    q_lat = hat_ref[...]
    inverse = inverse_rms(q_lat)
    hat = q_lat * inverse
    hat_ref[...] = hat
    low_ref[...] = hat.astype(BF16)
    inverse_ref[...] = inverse
    kv_ref[:, :HEAD] = rotate(kv_sum[:, :HEAD], cos_ref[:rows], sin_ref[:rows]).astype(BF16)
    kv_ref[:, HEAD:] = kv_sum[:, HEAD:].astype(BF16)


def latent(at, cosine, sine, parts, rank):
    count = parts[0].shape[0]
    rows = count // SQUARE
    return pl.pallas_call(
        latent_kernel,
        in_specs=[SMEM] + [VMEM] * (2 + SQUARE),
        out_specs=[VMEM] * 4,
        out_shape=[
            shape((count, rank), F32),
            shape((count, rank)),
            shape((count, 1), F32),
            shape((rows, 2 * HEAD)),
        ],
        scratch_shapes=[pltpu.VMEM((rows, 2 * HEAD), F32)],
        compiler_params=params(),
        cost_estimate=pl.CostEstimate(flops=8 * count * rank, bytes_accessed=10 * count * rank, transcendentals=0),
        name="latent",
    )(at, cosine, sine, *parts)


def head_copies(refs, wq, wo, sems):
    copies = []
    for i, target in enumerate((wq, wo)):
        size = target.shape[2]
        for c in range(2):
            source = refs[2 * i + c]
            if source.shape[1] > size:
                skipped = 0 if i == 0 else source.shape[1] - size
                source = source.at[:, pl.ds(skipped, size)]
            copies.append(pltpu.make_async_copy(source, target.at[c], sems.at[i, c]))
    return copies


def head_q(wq, c, h, pair):
    size = wq.shape[2] // (2 * pair)
    halves = [wq[c, :, (2 * h + i) * size : (2 * h + i + 1) * size, :] for i in range(2)]
    return jnp.concatenate([half.reshape(-1, HEAD // 2) for half in halves], axis=1)


def head_out(wo, c, h):
    return jnp.concatenate(
        [wo[c, tile, h * HEAD : (h + 1) * HEAD, :] for tile in range(wo.shape[1])], axis=1
    )


def attend_kernel(
    lat_ref, cos_ref, sin_ref, natural_ref, start_ref, kv_ref, keys_ref, *refs
):
    weights, (q_ref, o_ref, lse_ref, part_ref, wq, wo, sems) = refs[:4], refs[4:]

    @pl.when(pl.program_id(0) == 0)
    def _():
        copies = head_copies(weights, wq, wo, sems)
        for copy in copies:
            copy.start()
        for copy in copies:
            copy.wait()

    keys = keys_ref[...]
    allowed = (keys <= natural_ref[...]) & (keys >= start_ref[...])
    pair = wo.shape[2] // HEAD
    part = None
    for c in range(2):
        for h in range(pair):
            q_pre = matmul(lat_ref[...], head_q(wq, c, h, pair))
            q = rotate(q_pre, cos_ref[...], sin_ref[...]).astype(BF16)
            q = (q.astype(F32) * HEAD**-0.5).astype(BF16)
            scores = jnp.where(allowed, times_transposed(q, kv_ref[:, :HEAD]), MASKED)
            top = jnp.max(scores, axis=-1, keepdims=True)
            terms = jnp.exp(scores - top)
            total = jnp.sum(terms, axis=-1, keepdims=True)
            mix = matmul(terms.astype(BF16), kv_ref[:, HEAD:]) / total
            q_ref[c * pair + h] = q
            o_ref[c * pair + h] = mix
            lse_ref[c * pair + h] = top + jnp.log(total)
            share = matmul(mix.astype(BF16), head_out(wo, c, h))
            part = share if part is None else part + share
    part_ref[...] = part.astype(BF16)


def attend_specs(block, rank, count):
    row = lambda size: pl.BlockSpec((block, size), lambda i: (i, 0))
    whole = lambda dims: pl.BlockSpec(dims, lambda i: (0,) * len(dims))
    half = HEAD // 2
    return [
        row(rank),
        row(half),
        row(half),
        row(1),
        row(1),
        whole((count, 2 * HEAD)),
        whole((1, count)),
    ] + [HBM] * 4


def attend(lat, tables, kv, keys, weights, pair, block):
    places, tiles, lanes = weights[0].shape[0], weights[2].shape[0], 128
    rows, rank = lat.shape
    count = kv.shape[0]
    q_rows = 2 * pair * rank // places
    heads, width = 2 * pair, tiles * lanes
    by_head = lambda size: pl.BlockSpec((heads, block, size), lambda i: (0, i, 0))
    return pl.pallas_call(
        attend_kernel,
        grid=(rows // block,),
        in_specs=attend_specs(block, rank, count),
        out_specs=[
            by_head(HEAD),
            by_head(HEAD),
            by_head(1),
            pl.BlockSpec((block, width), lambda i: (i, 0)),
        ],
        out_shape=[
            shape((heads, rows, HEAD)),
            shape((heads, rows, HEAD), F32),
            shape((heads, rows, 1), F32),
            shape((rows, width)),
        ],
        scratch_shapes=[
            pltpu.VMEM((2, places, q_rows, HEAD // 2), BF16),
            pltpu.VMEM((2, tiles, pair * HEAD, lanes), BF16),
            pltpu.SemaphoreType.DMA((2, 2)),
        ],
        compiler_params=params(),
        cost_estimate=pl.CostEstimate(
            flops=2 * rows * heads * HEAD * (2 * count + rank + width),
            bytes_accessed=4 * count * HEAD + 2 * heads * HEAD * (rank + width),
            transcendentals=rows * heads * count,
        ),
        name="attend",
    )(lat, *tables, kv, keys, *weights)


def attend_back_kernel(
    at_ref, lat_ref, cos_ref, sin_ref, natural_ref, start_ref, kv_ref, keys_ref, *refs
):
    weights, refs = refs[:4], refs[4:]
    q_ref, o_ref, lse_ref, d_attn_ref = refs[:4]
    grads_q, refs = refs[4:6], refs[6:]
    d_lat_ref, near_ref, far_ref, wq, wo, sems, d_kv_sum, d_lat_sum = refs[:8]
    sums = refs[8:]
    q_rows = wq.shape[2]
    pair = wo.shape[2] // HEAD
    step, steps = pl.program_id(0), pl.num_programs(0)
    corner = at_ref[1]

    @pl.when(step == 0)
    def _():
        copies = head_copies(weights, wq, wo, sems)
        for copy in copies:
            copy.start()
        d_kv_sum[...] = jnp.zeros_like(d_kv_sum)
        for total in sums:
            total[...] = jnp.zeros_like(total)
        for copy in copies:
            copy.wait()

    def store(c, h, grad_q):
        size = q_rows // (2 * pair)
        for i in range(2):
            here = slice((2 * h + i) * size, (2 * h + i + 1) * size)
            tile = grad_q[:, i * 128 : (i + 1) * 128].astype(BF16)
            grads_q[c][:, here, :] = tile.reshape(-1, size, 128)

    keys = keys_ref[...]
    allowed = (keys <= natural_ref[...]) & (keys >= start_ref[...])
    d_attn, lat = d_attn_ref[...], lat_ref[...]
    d_lat = None
    for c in range(2):
        for h in range(pair):
            q, mix, lse = q_ref[c * pair + h], o_ref[c * pair + h], lse_ref[c * pair + h]
            w_q, w_out = head_q(wq, c, h, pair), head_out(wo, c, h)
            d_o = times_transposed(d_attn, w_out).astype(BF16)
            delta = jnp.sum(d_o.astype(F32) * mix, axis=-1, keepdims=True)
            scores = times_transposed(q, kv_ref[:, :HEAD])
            probs = jnp.exp(jnp.where(allowed, scores - lse, MASKED))
            d_probs = times_transposed(d_o, kv_ref[:, HEAD:])
            d_scores = (probs * (d_probs - delta)).astype(BF16)
            d_query = matmul(d_scores, kv_ref[:, :HEAD]) * HEAD**-0.5
            probs_low = probs.astype(BF16)
            for some in range(0, d_kv_sum.shape[0], 2048):
                these = slice(some, some + 2048)
                d_kv_sum[these, :HEAD] += contract_rows(d_scores[:, these], q)
                d_kv_sum[these, HEAD:] += contract_rows(probs_low[:, these], d_o)
            d_qpre = unrotate(d_query, cos_ref[...], sin_ref[...]).astype(BF16)
            grad_q = contract_rows(lat, d_qpre)
            share = times_transposed(d_qpre, w_q)
            d_lat = share if d_lat is None else d_lat + share
            if sums:
                sums[0][c, h] += grad_q
            else:
                store(c, h, grad_q)
    if sums:

        @pl.when(step == steps - 1)
        def _():
            for c in range(2):
                for h in range(pair):
                    store(c, h, sums[0][c, h])

    d_lat_sum[...] = d_lat
    share = d_lat.shape[1] // SQUARE
    dot = jnp.sum(d_lat * lat.astype(F32), axis=-1, keepdims=True)
    for m in range(SQUARE):
        b = corner ^ m
        columns = pl.ds(pl.multiple_of(b * share, share), share)
        d_lat_ref[m, :, :share] = d_lat_sum[:, columns].astype(BF16)
        d_lat_ref[m, :, share:] = jnp.broadcast_to(dot, (d_lat.shape[0], 128)).astype(BF16)

    @pl.when(step == steps - 1)
    def _():
        size = near_ref.shape[0]
        near_ref[...] = d_kv_sum[:size, :].astype(near_ref.dtype)
        far_ref[...] = d_kv_sum[size:, :].astype(BF16)


def attend_back(at, lat, tables, kv, keys, weights, q, o, lse, d_attn, pair, block):
    places, tiles, lanes = weights[0].shape[0], weights[2].shape[0], 128
    rows, rank = lat.shape
    count = kv.shape[0]
    q_rows = 2 * pair * rank // places
    heads, width = 2 * pair, tiles * lanes
    by_head = lambda size: pl.BlockSpec((heads, block, size), lambda i: (0, i, 0))
    whole = lambda dims: pl.BlockSpec(dims, lambda i: (0,) * len(dims))
    grad_dims = [(places, q_rows, HEAD // 2)] * 2
    d_lat_dims = (SQUARE, rows, rank // SQUARE + 128)
    sums = []
    if rows != block:
        sums = [pltpu.VMEM((2, pair, rank, HEAD), F32)]
    return pl.pallas_call(
        attend_back_kernel,
        grid=(rows // block,),
        in_specs=[SMEM]
        + attend_specs(block, rank, count)
        + [by_head(HEAD), by_head(HEAD), by_head(1), pl.BlockSpec((block, width), lambda i: (i, 0))],
        out_specs=[
            *[whole(dims) for dims in grad_dims],
            pl.BlockSpec((SQUARE, block, d_lat_dims[2]), lambda i: (0, i, 0)),
            whole((count // 2, 2 * HEAD)),
            whole((count // 2, 2 * HEAD)),
        ],
        out_shape=[
            *[shape(dims) for dims in grad_dims],
            shape(d_lat_dims),
            shape((count // 2, 2 * HEAD), BF16 if sums else F32),
            shape((count // 2, 2 * HEAD)),
        ],
        scratch_shapes=[
            pltpu.VMEM((2, places, q_rows, HEAD // 2), BF16),
            pltpu.VMEM((2, tiles, pair * HEAD, lanes), BF16),
            pltpu.SemaphoreType.DMA((2, 2)),
            pltpu.VMEM((count, 2 * HEAD), F32),
            pltpu.VMEM((block, rank), F32),
        ]
        + sums,
        compiler_params=params(VMEM_LIMIT + len(sums) * 2**22),
        cost_estimate=pl.CostEstimate(
            flops=2 * rows * heads * HEAD * (5 * count + 2 * rank + 2 * width),
            bytes_accessed=12 * count * HEAD + 4 * heads * HEAD * (rank + width),
            transcendentals=rows * heads * count,
        ),
        name="attend_back",
    )(at, lat, *tables, kv, keys, *weights, q, o, lse, d_attn)


def out_grads_kernel(mix_ref, d_attn_ref, near_ref, far_ref):
    d_attn = d_attn_ref[...]
    pair = mix_ref.shape[0] // 2
    for c, out_ref in enumerate((near_ref, far_ref)):
        for h in range(pair):
            grad = contract_rows(mix_ref[c * pair + h], d_attn)
            for tile in range(out_ref.shape[0]):
                out_ref[tile, h * HEAD : (h + 1) * HEAD, :] = grad[
                    :, tile * 128 : (tile + 1) * 128
                ].astype(BF16)


def out_grads(mix, d_attn, pair):
    rows, width = d_attn.shape
    dims = (width // 128, pair * HEAD, 128)
    return pl.pallas_call(
        out_grads_kernel,
        in_specs=[VMEM, VMEM],
        out_specs=[VMEM, VMEM],
        out_shape=[shape(dims), shape(dims)],
        compiler_params=params(),
        cost_estimate=pl.CostEstimate(
            flops=4 * rows * pair * HEAD * width, bytes_accessed=8 * pair * HEAD * width, transcendentals=0
        ),
        name="out_grads",
    )(mix, d_attn)


def latent_back_kernel(layers, at_ref, hat_ref, inverse_ref, d_kv_ref, x_ref, w_ref, *refs):
    parts = refs[:SQUARE]
    d_x_ref, near_ref, far_ref, d_sum = refs[SQUARE:]
    layer, corner, core = at_ref[0], at_ref[1], at_ref[2]
    count, width = x_ref.shape
    rows = count // SQUARE
    share = w_ref.shape[-1]
    rank_share = hat_ref.shape[1] // SQUARE
    for i in range(SQUARE):
        d_sum[i * rows : (i + 1) * rows] = sum(
            part[(i ^ m) * rows : (i ^ m) * rows + rows].astype(F32) for m, part in enumerate(parts)
        )
    columns = pl.ds(pl.multiple_of(corner * rank_share, rank_share), rank_share)
    dot = d_sum[:, rank_share : rank_share + 1] * (1.0 / hat_ref.shape[1])
    d_lat = inverse_ref[...] * (d_sum[:, :rank_share] - hat_ref[:, columns] * dot)
    d_down = jnp.concatenate([d_lat.astype(BF16), d_kv_ref[...]], axis=1)
    weight = w_ref[...].reshape(width, share)
    d_x_ref[...] = times_transposed(d_down, weight).astype(BF16)
    grad = contract_rows(x_ref[...], d_down)
    grad = grad.reshape(layers, SQUARE, 2, near_ref.shape[2], share)
    low, high = grad[:, :, 0], grad[:, :, 1]
    near = jnp.where(core == 0, low, high)
    far = jnp.where(core == 0, high, low).astype(BF16)
    for z in range(layers):
        k = lax.rem(layer + layers - z, layers)
        near_ref[k] = near[z]
        far_ref[k] = far[z]


def latent_back(at, hat, inverse, d_kv, x, weight, parts):
    count, width = x.shape
    places, _, lane_rows, share = weight.shape
    layers = places // SQUARE
    dims = (layers, SQUARE, lane_rows, share)
    return pl.pallas_call(
        functools.partial(latent_back_kernel, layers),
        in_specs=[SMEM] + [VMEM] * (5 + SQUARE),
        out_specs=[VMEM] * 3,
        out_shape=[shape((count, width)), shape(dims, F32), shape(dims)],
        scratch_shapes=[pltpu.VMEM(parts[0].shape, F32)],
        compiler_params=params(),
        cost_estimate=pl.CostEstimate(
            flops=4 * count * width * share, bytes_accessed=10 * width * share, transcendentals=0
        ),
        name="latent_back",
    )(at, hat, inverse, d_kv, x, weight, *parts)


def chunk(ref, q, tiles):
    columns = [(t * SQUARE + q) * 128 for t in range(tiles)]
    return jnp.concatenate([ref[:, c : c + 128] for c in columns], axis=1)


def mlp_kernel(h_ref, cot_ref, *refs):
    d_h_ref, out_ref, act_near_ref, act_far_ref, weights, sems = refs[2:]
    tiles, units = weights.shape[3:5]
    copies = [
        [
            pltpu.make_async_copy(
                refs[c].at[:, :, pl.ds(kind * units, units)], weights.at[c, kind], sems.at[c, kind]
            )
            for kind in range(3)
        ]
        for c in range(2)
    ]
    for one in copies:
        for copy in one:
            copy.start()

    def weight(c, kind, q):
        return jnp.concatenate([weights[c, kind, q, t] for t in range(tiles)], axis=1)

    sides = (act_near_ref, act_far_ref)
    for c, acts in enumerate(sides):

        def product(value_ref, kind):
            copies[c][kind].wait()
            return sum(
                times_transposed(chunk(value_ref, q, tiles), weight(c, kind, q)) for q in range(SQUARE)
            )

        gate_act, up_proj, d_act = product(h_ref, 0), product(h_ref, 1), product(cot_ref, 2)
        sigmoid_gate = 1.0 / (1.0 + jnp.exp(-gate_act))
        silu_gate = gate_act * sigmoid_gate
        d_gate = d_act * up_proj * sigmoid_gate * (1.0 + gate_act * (1.0 - sigmoid_gate))
        acts[0] = d_gate.astype(BF16)
        acts[1] = (d_act * silu_gate).astype(BF16)
        acts[2] = (silu_gate * up_proj).astype(BF16)
    for q in range(SQUARE):
        d_h = sum(
            matmul(acts[kind], weight(c, kind, q)) for c, acts in enumerate(sides) for kind in range(2)
        )
        out = sum(matmul(acts[2], weight(c, 2, q)) for c, acts in enumerate(sides))
        for t in range(tiles):
            here = slice((t * SQUARE + q) * 128, (t * SQUARE + q + 1) * 128)
            d_h_ref[:, here] = d_h[:, t * 128 : (t + 1) * 128].astype(BF16)
            out_ref[:, here] = out[:, t * 128 : (t + 1) * 128].astype(BF16)


def mlp(h, cot, near, far):
    rows, width = h.shape
    _, tiles, units, lanes = near.shape
    units = units // 3
    low = shape((rows, width))
    acts = shape((3, rows, units))
    return pl.pallas_call(
        mlp_kernel,
        in_specs=[VMEM, VMEM, HBM, HBM],
        out_specs=[VMEM] * 4,
        out_shape=[low, low, acts, acts],
        scratch_shapes=[
            pltpu.VMEM((2, 3, SQUARE, tiles, units, lanes), BF16),
            pltpu.SemaphoreType.DMA((2, 3)),
        ],
        compiler_params=params(),
        cost_estimate=pl.CostEstimate(
            flops=24 * rows * width * units,
            bytes_accessed=12 * width * units + 8 * rows * width,
            transcendentals=2 * rows * units,
        ),
        name="mlp",
    )(h, cot, near, far)


def unit_grads_kernel(acts_ref, value_ref, *refs):
    more, out_ref = refs[:-1], refs[-1]
    acts = acts_ref[0]
    tiles = out_ref.shape[1]
    for q in range(SQUARE):
        grad = contract_rows(acts, chunk(value_ref, q, tiles))
        for t in range(tiles):
            tile = grad[:, t * 128 : (t + 1) * 128]
            if more:
                tile = tile + more[0][q, t].astype(F32)
            out_ref[q, t] = tile.astype(BF16)


def unit_grads(acts, kind, value, received=None, kinds=None):
    rows, width = value.shape
    units = acts.shape[2]
    tiles = width // SQUARE // 128
    whole = lambda dims: pl.BlockSpec(dims, lambda i: (0,) * len(dims))
    dims = (SQUARE, tiles, units, 128)
    in_specs = [pl.BlockSpec((1, rows, units), lambda i: (kind, 0, 0)), whole((rows, width))]
    args, aliases, body = [acts, value], {}, unit_grads_kernel
    out_specs, out_dims = whole(dims), dims
    if received is not None:
        args.append(received)
        in_specs.append(whole(dims))
        out_specs = pl.BlockSpec(dims, lambda i: (0, 0, kind, 0))
        out_dims = (SQUARE, tiles, 3 * units, 128)
    if kinds is not None:
        args.append(kinds)
        in_specs.append(HBM)
        aliases = {3: 0}
        body = lambda a, v, r, k, o: unit_grads_kernel(a, v, r, o)
    return pl.pallas_call(
        body,
        grid=(1,),
        in_specs=in_specs,
        out_specs=out_specs,
        out_shape=shape(out_dims),
        input_output_aliases=aliases,
        compiler_params=params(),
        cost_estimate=pl.CostEstimate(
            flops=2 * rows * width * units, bytes_accessed=4 * width * units, transcendentals=0
        ),
        name="unit_grads",
    )(*args)


def local(
    chips,
    tokens,
    attn_gain,
    q_gain,
    w_qdown,
    w_qup,
    w_kv,
    w_out,
    mlp_gain,
    w_gate,
    w_up,
    w_down,
    cotangent,
    seq_lengths,
    block_slots,
):
    layers = chips // SQUARE
    rows, width = tokens.shape[0] // 2, tokens.shape[1]
    lanes = width // chips
    rank = w_qdown.shape[1]
    rank_rows = w_qup.shape[0]
    pair = w_qup.shape[1] // HEAD // SQUARE
    units = w_gate.shape[1] // layers
    half = HEAD // 2
    place = lax.axis_index("seq")
    core = lax.axis_index("tp")
    layer, corner = place // SQUARE, place % SQUARE
    at = jnp.stack([layer, corner, core]).astype(jnp.int32)
    first = core == 0
    lines = [[z * SQUARE + c for z in range(layers)] for c in range(SQUARE)]
    square_groups = [[z * SQUARE + c for c in range(SQUARE)] for z in range(layers)]

    def across(value):
        return lax.ppermute(value, "tp", [(0, 1), (1, 0)])

    def along(value, step):
        pairs = [
            (z * SQUARE + c, (z + step) % layers * SQUARE + c)
            for z in range(layers)
            for c in range(SQUARE)
        ]
        return lax.ppermute(value, "seq", pairs)

    def within(value, flip):
        return lax.ppermute(value, "seq", [(i, i ^ flip) for i in range(chips)])

    def line_exchange(value):
        return lax.all_to_all(value, "seq", 0, 0, axis_index_groups=lines, tiled=True)

    def square_exchange(value):
        return lax.all_to_all(value, "seq", 0, 0, axis_index_groups=square_groups, tiled=True)

    def line_pieces(value):
        return [value] + [along(value, k) for k in range(1, layers)]

    def line_sum(blocks):
        return blocks[0].astype(F32) + sum(
            along(blocks[k], -k).astype(F32) for k in range(1, layers)
        )

    def by_layer(value):
        blocks = value.reshape(layers, rows, -1)
        return jnp.concatenate(
            [
                lax.dynamic_index_in_dim(blocks, (layer - z) % layers, 0, keepdims=False)
                for z in range(layers)
            ]
        )

    def square_pieces(value):
        return [value] + [within(value, m) for m in range(1, SQUARE)]

    def square_sum(blocks):
        return blocks[0].astype(F32) + sum(
            within(blocks[m], m).astype(F32) for m in range(1, SQUARE)
        )

    def after(value, *earlier):
        return lax.optimization_barrier((value,) + earlier)[0]

    def together(*values):
        return lax.optimization_barrier(values)

    def own(pair_value):
        return lax.dynamic_slice_in_dim(pair_value, core * rows, rows, 0)

    def both(mine, theirs, axis=0):
        return jnp.concatenate(
            [jnp.where(first, mine, theirs), jnp.where(first, theirs, mine)], axis=axis
        )

    def tiled(value):
        if lanes == 128:
            return value
        count, size, _ = value.shape
        value = jnp.swapaxes(value, 0, 1).reshape(size, count * lanes // 128, 128)
        return jnp.swapaxes(value, 0, 1)

    def untiled(value):
        if lanes == 128:
            return value
        count, size, _ = value.shape
        value = jnp.swapaxes(value, 0, 1).reshape(size, count * 128 // lanes, lanes)
        return jnp.swapaxes(value, 0, 1)

    def arranged(value):
        if lanes == 128:
            return value
        shaped = value.reshape(value.shape[0], -1, 128 // lanes, SQUARE, lanes)
        return jnp.swapaxes(shaped, 2, 3).reshape(value.shape)

    def unarranged(value):
        if lanes == 128:
            return value
        shaped = value.reshape(value.shape[0], -1, SQUARE, 128 // lanes, lanes)
        return jnp.swapaxes(shaped, 2, 3).reshape(value.shape)

    inputs = own(tokens).astype(F32)
    x_inverse = inverse_rms(inputs)
    x_hat = inputs * x_inverse
    x_all = jnp.concatenate(square_pieces(x_hat.astype(BF16)))

    gain_rows = attn_gain.astype(F32)[:, None]
    down = jnp.concatenate([w_qdown, w_kv], axis=1)
    rank_share, kv_share = rank // SQUARE, 2 * HEAD // SQUARE

    def shares(value):
        return jnp.stack(
            [
                jnp.concatenate(
                    [
                        value[:, b * rank_share : (b + 1) * rank_share],
                        value[:, rank + b * kv_share : rank + (b + 1) * kv_share],
                    ],
                    axis=1,
                )
                for b in range(SQUARE)
            ]
        )

    def unshares(value):
        return jnp.concatenate(
            [value[b, :, :rank_share] for b in range(SQUARE)]
            + [value[b, :, rank_share:] for b in range(SQUARE)],
            axis=1,
        )

    down_scaled = (down.astype(F32) * gain_rows).astype(BF16)
    down_half = lax.dynamic_slice_in_dim(down_scaled, core * (lanes // 2), lanes // 2, 0)
    cot_own = own(cotangent)
    down_own = square_exchange(shares(down_half))
    cot_pieces = line_pieces(arranged(cot_own))
    cot_all = by_layer(jnp.concatenate(cot_pieces))
    down_near = line_pieces(after(down_own, *cot_pieces[1:]))
    down_far = [across(piece) for piece in down_near]

    q_gain_rows = q_gain.astype(F32)[:, None]
    qup_scaled = (w_qup.astype(F32) * q_gain_rows).astype(BF16)
    qup_send = qup_scaled.reshape(rank_rows, SQUARE, 2 * pair, half)
    qup_send = jnp.transpose(qup_send, (1, 2, 0, 3)).reshape(SQUARE, -1, lanes)
    qup_size = qup_send.shape[1]
    head_send = jnp.concatenate([qup_send, w_out.reshape(SQUARE, pair * HEAD, lanes)], axis=1)
    head_own = square_exchange(after(head_send, down_own))

    mlp_gain_rows = mlp_gain.astype(F32)[:, None]
    gate_send = (w_gate.astype(F32) * mlp_gain_rows).astype(BF16).T
    up_send = (w_up.astype(F32) * mlp_gain_rows).astype(BF16).T
    mlp_send = jnp.concatenate(
        [value.reshape(layers, units, lanes) for value in (gate_send, up_send, w_down)], axis=1
    )

    bounds = jnp.cumsum(seq_lengths)
    starts = bounds - seq_lengths

    def layout(blocks):
        natural = (blocks[:, None] * rows + jnp.arange(rows, dtype=jnp.int32)[None, :]).reshape(-1)
        member = (natural[:, None] >= starts[None, :]) & (natural[:, None] < bounds[None, :])
        return natural, jnp.sum(jnp.where(member, starts[None, :], 0), axis=1)

    back_steps = jnp.arange(layers, dtype=jnp.int32)
    flips = jnp.arange(SQUARE, dtype=jnp.int32)
    owners = (((layer - back_steps) % layers) * SQUARE)[None, :] + (corner ^ flips)[:, None]
    square_slots = block_slots[2 * owners[:, 0] + core]
    row_natural, row_start = layout(square_slots)
    owners = owners.reshape(-1)
    near_natural, _ = layout(block_slots[2 * owners + core])
    far_natural, _ = layout(block_slots[2 * owners + 1 - core])
    key_natural = jnp.concatenate([near_natural, far_natural])[None, :]
    cosine, sine = angles(row_natural - row_start)
    tables = (cosine, sine, row_natural[:, None], row_start[:, None])

    x_all = after(x_all, head_own)
    part, down_here = project(at, x_all, down_near, down_far)
    lat_hat, lat_low, lat_inverse, kv_own = latent(at, cosine, sine, square_pieces(part), rank)
    mlp_layer = line_exchange(after(mlp_send, *down_near[1:]))
    mlp_layer, kv_own = together(mlp_layer, kv_own)
    kv_line = jnp.concatenate(line_pieces(kv_own))
    mlp_near = lax.all_gather(tiled(mlp_layer), "seq", axis_index_groups=square_groups)

    head_near = line_exchange(jnp.tile(after(head_own, mlp_layer, kv_line), (layers, 1, 1)))
    kv_near = jnp.concatenate(square_pieces(kv_line))
    kv_all = jnp.concatenate([kv_near, across(kv_near)])
    head_near, kv_all = together(head_near, kv_all)
    head_far = across(head_near)
    if lanes == 128:
        head_weights = (head_near, head_far, head_near, head_far)
    else:
        head_weights = tuple(
            side[:, :qup_size].reshape(chips, -1, half) for side in (head_near, head_far)
        ) + tuple(tiled(side[:, qup_size:]) for side in (head_near, head_far))

    block = max(32, min(SQUARE * rows, 2**30 // kv_all.shape[0] ** 2))
    queries, attn_mix, log_total, attn_part = attend(
        lat_low, tables, kv_all, key_natural, head_weights, pair, block
    )
    mlp_near, attn_part = together(mlp_near, attn_part)
    mlp_far = across(mlp_near)
    hidden = inputs + square_sum(attn_part.reshape(SQUARE, rows, width))
    h_inverse = inverse_rms(hidden)
    h_hat = hidden * h_inverse
    h_low = h_hat.astype(BF16)
    h_all = jnp.concatenate(line_pieces(arranged(h_low)))
    h_all = by_layer(h_all)

    d_h_part, mlp_part, acts_near, acts_far = mlp(h_all, cot_all, mlp_near, mlp_far)
    def line_blocks(value):
        return line_exchange(value.reshape(layers, rows, width))

    def line_total(blocks):
        return unarranged(jnp.sum(blocks.astype(F32), axis=0))

    kinds = ((0, h_all), (1, h_all), (2, cot_all))
    far_grads = [unit_grads(acts_far, kind, value) for kind, value in kinds]
    d_h_lines = line_blocks(d_h_part)
    d_h_lines, acts_near, *far_grads = together(d_h_lines, acts_near, *far_grads)
    d_hscaled = line_total(d_h_lines)
    d_hidden = cot_own.astype(F32) + norm_back(d_hscaled, h_hat, h_inverse)
    mlp_grads = None
    for kind, value in kinds:
        mlp_grads = unit_grads(acts_near, kind, value, across(far_grads[kind]), mlp_grads)
    mlp_lines = line_blocks(after(mlp_part, d_hscaled))
    d_attn_pieces = square_pieces(d_hidden.astype(BF16))
    mlp_lines, mlp_grads, *d_attn_pieces = together(mlp_lines, mlp_grads, *d_attn_pieces)
    d_attn_all = jnp.concatenate(d_attn_pieces)
    mlp_sum = lax.psum_scatter(mlp_grads, "seq", axis_index_groups=square_groups)

    mix_low = attn_mix.astype(BF16)
    grad_out_near, grad_out_far = out_grads(mix_low, d_attn_all, pair)
    grad_out_total = grad_out_near.astype(F32) + across(grad_out_far).astype(F32)
    grad_out_total = untiled(grad_out_total.astype(BF16))
    head_out_lines = line_exchange(grad_out_total)
    layer_out_own = (hidden + line_total(mlp_lines)).astype(BF16)
    layer_out = both(layer_out_own, across(layer_out_own))
    grad_q_near, grad_q_far, d_lat_parts, d_kv_near, d_kv_far = attend_back(
        at,
        lat_low,
        tables,
        kv_all,
        key_natural,
        head_weights,
        queries,
        attn_mix,
        log_total,
        d_attn_all,
        pair,
        block,
    )
    d_kv_low = (d_kv_near.astype(F32) + across(d_kv_far).astype(F32)).astype(BF16)
    d_kv_line = square_sum(d_kv_low.reshape(SQUARE, layers * rows, 2 * HEAD)).astype(BF16)
    head_out_lines, d_kv_line = together(head_out_lines, d_kv_line)
    grad_q_total = (grad_q_near.astype(F32) + across(grad_q_far).astype(F32)).astype(BF16)
    d_kv_own = line_sum(d_kv_line.reshape(layers, rows, 2 * HEAD))
    d_kv_own = jnp.concatenate(
        [unrotate(d_kv_own[:, :HEAD], cosine[:rows], sine[:rows]), d_kv_own[:, HEAD:]], axis=1
    ).astype(BF16)
    head_q = line_exchange(after(grad_q_total, d_kv_own).reshape(chips, -1, lanes))
    kv_share_of = lambda m: lax.dynamic_slice_in_dim(d_kv_own, (corner ^ m) * kv_share, kv_share, 1)
    d_kv_share = jnp.concatenate(
        [kv_share_of(0)] + [within(kv_share_of(m), m) for m in range(1, SQUARE)]
    )
    d_lat_received = [d_lat_parts[0]] + [within(d_lat_parts[m], m) for m in range(1, SQUARE)]
    head_q, *d_lat_received = together(head_q, *d_lat_received)

    d_x_part, down_grad_near, down_grad_far = latent_back(
        at, lat_hat, lat_inverse, d_kv_share, x_all, down_here, d_lat_received
    )
    d_x_blocks = d_x_part.reshape(SQUARE, rows, width)
    d_x_received = [within(d_x_blocks[m], m) for m in range(1, SQUARE)]
    down_sum = (down_grad_near + across(down_grad_far).astype(F32)).astype(BF16)

    def square_send(value):
        blocks = [
            lax.dynamic_index_in_dim(value, corner ^ m, 0, keepdims=False) for m in range(SQUARE)
        ]
        return [blocks[0]] + [within(blocks[m], m) for m in range(1, SQUARE)]

    def by_corner(pieces):
        pieces = jnp.stack(pieces)
        return jnp.stack(
            [
                lax.dynamic_index_in_dim(pieces, corner ^ q, 0, keepdims=False)
                for q in range(SQUARE)
            ]
        )

    mlp_sum = untiled(mlp_sum)
    gate_up_back = line_exchange(after(mlp_sum[:, : 2 * units], head_q))
    head_sum = jnp.concatenate(
        [
            jnp.sum(blocks.reshape(layers, SQUARE, -1, lanes).astype(F32), axis=0).astype(BF16)
            for blocks in (head_q, head_out_lines)
        ],
        axis=1,
    )
    head_pieces = square_send(head_sum)
    gate_up_back, *received = together(gate_up_back, *d_x_received, *head_pieces)
    d_x_received, head_pieces = received[: SQUARE - 1], received[SQUARE - 1 :]
    d_xscaled = d_x_blocks[0].astype(F32) + sum(block.astype(F32) for block in d_x_received)
    token_own = (d_hidden + norm_back(d_xscaled, x_hat, x_inverse)).astype(BF16)
    token_grad = both(token_own, across(token_own))
    down_sum = after(down_sum, gate_up_back)
    down_pieces = [along(down_sum[k], -k) for k in range(1, layers)]
    unit_back = line_exchange(after(mlp_sum[:, 2 * units :], *down_pieces))
    down_line = down_sum[0].astype(F32) + sum(piece.astype(F32) for piece in down_pieces)
    down_pieces = square_send(down_line.astype(BF16))
    unit_back, *down_pieces = together(unit_back, *down_pieces)
    head_sum = by_corner(head_pieces)
    down_back = unshares(by_corner(down_pieces)).astype(F32)
    down_back = both(down_back, across(down_back))
    attn_gain_part = jnp.sum(down_back * down.astype(F32), axis=1)
    down_grad = down_back * gain_rows
    qdown_part, kv_part = down_grad[:, :rank], down_grad[:, rank:]

    gate_back, up_back, down_part = (
        value.reshape(layers * units, lanes).astype(F32)
        for value in (gate_up_back[:, :units], gate_up_back[:, units:], unit_back)
    )
    gate_back, up_back = gate_back.T, up_back.T
    gate_part, up_part = gate_back * mlp_gain_rows, up_back * mlp_gain_rows
    mlp_gain_part = jnp.sum(gate_back * w_gate.astype(F32) + up_back * w_up.astype(F32), axis=1)

    qup_back = head_sum[:, :qup_size].reshape(SQUARE, 2 * pair, rank_rows, half)
    qup_back = jnp.transpose(qup_back, (2, 0, 1, 3)).reshape(rank_rows, -1).astype(F32)
    out_part = head_sum[:, qup_size:].reshape(-1, lanes).astype(F32)
    qup_part = qup_back * q_gain_rows
    q_gain_half = jnp.sum(qup_back * w_qup.astype(F32), axis=1)
    gain_parts = jnp.concatenate([q_gain_half, mlp_gain_part])
    gain_parts = gain_parts + across(gain_parts)
    q_gain_part, mlp_gain_part = gain_parts[:rank_rows], gain_parts[rank_rows:]
    return (
        layer_out,
        token_grad,
        attn_gain_part,
        q_gain_part,
        qdown_part,
        qup_part,
        kv_part,
        out_part,
        mlp_gain_part,
        gate_part,
        up_part,
        down_part,
    )


def solution(mesh):
    in_specs = (
        P("seq", None),
        P("seq"),
        P("seq"),
        P("seq", None),
        P("seq", "tp"),
        P("seq", None),
        P("tp", "seq"),
        P("seq"),
        P("seq", "tp"),
        P("seq", "tp"),
        P("tp", "seq"),
        P("seq", None),
        P(),
        P(),
    )
    out_specs = (
        P("seq", None),
        P("seq", None),
        P("seq"),
        P("seq"),
        P("seq", None),
        P("seq", "tp"),
        P("seq", None),
        P("tp", "seq"),
        P("seq"),
        P("seq", "tp"),
        P("seq", "tp"),
        P("tp", "seq"),
    )
    body = functools.partial(local, mesh.shape["seq"])
    return jax.shard_map(body, mesh=mesh, in_specs=in_specs, out_specs=out_specs, check_vma=False)
```

```python
import functools
import math

import jax
import jax.numpy as jnp
from jax import lax
from jax.experimental import pallas as pl
from jax.experimental.pallas import tpu as pltpu
from jax.sharding import PartitionSpec as P

EPSILON = 1e-06
ROPE_BASE = 10000.0
MASKED = -1e30
HEAD = 256
SQUARE = 4
VMEM_LIMIT = 56 * 1024 * 1024
MLP_LIMIT = 26 * 1024 * 1024
ATTEND_LIMIT = 32 * 1024 * 1024
GRADS_LIMIT = 16 * 1024 * 1024
BF16 = jnp.bfloat16
F32 = jnp.float32


def matmul(left, right):
    return jnp.dot(left, right, preferred_element_type=F32)


def contract_rows(left, right):
    return lax.dot_general(left, right, (((0,), (0,)), ((), ())), preferred_element_type=F32)


def times_transposed(left, right):
    return lax.dot_general(left, right, (((1,), (1,)), ((), ())), preferred_element_type=F32)


def inverse_rms(vector):
    return lax.rsqrt(jnp.mean(vector * vector, axis=-1, keepdims=True) + EPSILON)


def norm_back(scaled_grad, normed, inverse):
    return inverse * (scaled_grad - normed * jnp.mean(scaled_grad * normed, axis=-1, keepdims=True))


def angles(position):
    half = HEAD // 2
    frequency = jnp.exp(jnp.arange(half, dtype=F32) * (-math.log(ROPE_BASE) / half))
    phase = position.astype(F32)[:, None] * frequency[None, :]
    return jnp.cos(phase), jnp.sin(phase)


def rotate(vector, cosine, sine):
    half = HEAD // 2
    front, back = vector[:, :half], vector[:, half:]
    return jnp.concatenate([front * cosine - back * sine, back * cosine + front * sine], axis=1)


def unrotate(vector, cosine, sine):
    return rotate(vector, cosine, -sine)


def params(limit=VMEM_LIMIT):
    return pltpu.CompilerParams(vmem_limit_bytes=limit)


VMEM = pl.BlockSpec(memory_space=pltpu.VMEM)
SMEM = pl.BlockSpec(memory_space=pltpu.SMEM)
HBM = pl.BlockSpec(memory_space=pl.ANY)
FAR = pl.BlockSpec(memory_space=pltpu.HBM)


def shape(dims, dtype=BF16):
    return jax.ShapeDtypeStruct(tuple(dims), dtype)


def project_kernel(layers, at_ref, x_ref, *refs):
    near, far = refs[:layers], refs[layers : 2 * layers]
    part_ref, w_ref, sems = refs[2 * layers :]
    layer, core = at_ref[0], at_ref[2]
    copies = []
    for c, pieces in enumerate((near, far)):
        side = core if c == 0 else 1 - core
        for k, piece in enumerate(pieces):
            first = lax.rem(layer + layers - k, layers) * SQUARE
            target = w_ref.at[pl.ds(first, SQUARE), side]
            copies.append(pltpu.make_async_copy(piece, target, sems.at[c, k]))
    for copy in copies:
        copy.start()
    for copy in copies:
        copy.wait()
    width, share = x_ref.shape[1], w_ref.shape[-1]
    part_ref[...] = matmul(x_ref[...], w_ref[...].reshape(width, share)).astype(BF16)


def project(at, x, near, far):
    layers = len(near)
    rows, width = x.shape
    _, lane_rows, share = near[0].shape
    return pl.pallas_call(
        functools.partial(project_kernel, layers),
        in_specs=[SMEM, VMEM] + [HBM] * (2 * layers),
        out_specs=[VMEM, VMEM],
        out_shape=[
            shape((rows, share)),
            shape((layers * SQUARE, 2, lane_rows, share)),
        ],
        scratch_shapes=[pltpu.SemaphoreType.DMA((2, layers))],
        compiler_params=params(),
        cost_estimate=pl.CostEstimate(
            flops=2 * rows * width * share, bytes_accessed=4 * width * share, transcendentals=0
        ),
        name="project",
    )(at, x, *near, *far)


def latent_kernel(at_ref, cos_ref, sin_ref, *refs):
    parts = refs[:SQUARE]
    hat_ref, low_ref, inverse_ref, kv_ref, kv_sum = refs[SQUARE:]
    corner = at_ref[1]
    rows = kv_ref.shape[0]
    rank_share, kv_share = hat_ref.shape[1] // SQUARE, 2 * HEAD // SQUARE
    own = pl.ds(pl.multiple_of(corner * rows, rows), rows)
    for m, part in enumerate(parts):
        b = corner ^ m
        columns = pl.ds(pl.multiple_of(b * rank_share, rank_share), rank_share)
        hat_ref[:, columns] = part[:, :rank_share].astype(F32)
        columns = pl.ds(pl.multiple_of(b * kv_share, kv_share), kv_share)
        kv_sum[:, columns] = part[own, rank_share:].astype(F32)
    q_lat = hat_ref[...]
    inverse = inverse_rms(q_lat)
    hat = q_lat * inverse
    hat_ref[...] = hat
    low_ref[...] = hat.astype(BF16)
    inverse_ref[...] = inverse
    kv_ref[:, :HEAD] = rotate(kv_sum[:, :HEAD], cos_ref[own, :], sin_ref[own, :]).astype(BF16)
    kv_ref[:, HEAD:] = kv_sum[:, HEAD:].astype(BF16)


def latent(at, cosine, sine, parts, rank):
    count = parts[0].shape[0]
    rows = count // SQUARE
    return pl.pallas_call(
        latent_kernel,
        in_specs=[SMEM] + [VMEM] * (2 + SQUARE),
        out_specs=[VMEM] * 4,
        out_shape=[
            shape((count, rank), F32),
            shape((count, rank)),
            shape((count, 1), F32),
            shape((rows, 2 * HEAD)),
        ],
        scratch_shapes=[pltpu.VMEM((rows, 2 * HEAD), F32)],
        compiler_params=params(),
        cost_estimate=pl.CostEstimate(flops=8 * count * rank, bytes_accessed=10 * count * rank, transcendentals=0),
        name="latent",
    )(at, cosine, sine, *parts)


def head_q(weights, c, h, pair):
    ref = weights[c]
    size = (ref.shape[1] if len(weights) == 4 else ref.shape[1] - pair * HEAD) // (2 * pair)
    halves = [ref[:, (2 * h + i) * size : (2 * h + i + 1) * size, :] for i in range(2)]
    return jnp.concatenate([half.reshape(-1, HEAD // 2) for half in halves], axis=1)


def head_out(weights, c, h, pair):
    ref = weights[len(weights) - 2 + c]
    first = ref.shape[1] - pair * HEAD + h * HEAD
    return jnp.concatenate(
        [ref[tile, first : first + HEAD, :] for tile in range(ref.shape[0])], axis=1
    )


def attend_kernel(pair, count, lat_ref, cos_ref, sin_ref, places_ref, kv_ref, keys_ref, *refs):
    weights, (saved_ref, part_ref, kept, sems) = refs[:count], refs[count:]
    keys = keys_ref[...]
    rows = part_ref.shape[0]
    here = pl.ds(pl.program_id(0) * rows, rows)
    allowed = (keys <= places_ref[:, 0:1]) & (keys >= places_ref[:, 1:2])
    part, copies = None, []
    for c in range(2):
        for h in range(pair):
            head = c * pair + h
            q_pre = matmul(lat_ref[...], head_q(weights, c, h, pair))
            q = rotate(q_pre, cos_ref[...], sin_ref[...]).astype(BF16)
            q = (q.astype(F32) * HEAD**-0.5).astype(BF16)
            scores = jnp.where(allowed, times_transposed(q, kv_ref[:, :HEAD]), MASKED)
            top = jnp.max(scores, axis=-1, keepdims=True)
            terms = jnp.exp(scores - top)
            total = jnp.sum(terms, axis=-1, keepdims=True)
            mix = (matmul(terms.astype(BF16), kv_ref[:, HEAD:]) / total).astype(BF16)
            kept[head, :, :HEAD] = q
            kept[head, :, HEAD:] = mix
            copy = pltpu.make_async_copy(kept.at[head], saved_ref.at[head, here], sems.at[head])
            copy.start()
            copies.append(copy)
            share = matmul(mix, head_out(weights, c, h, pair))
            part = share if part is None else part + share
    part_ref[...] = part.astype(BF16)
    for copy in copies:
        copy.wait()


def attend_specs(block, rank, count, weights):
    row = lambda size: pl.BlockSpec((block, size), lambda i: (i, 0))
    whole = lambda dims: pl.BlockSpec(dims, lambda i: (0,) * len(dims))
    half = HEAD // 2
    return [
        row(rank),
        row(half),
        row(half),
        row(128),
        whole((count, 2 * HEAD)),
        whole((1, count)),
    ] + [whole(weight.shape) for weight in weights]


def attend(lat, tables, kv, keys, weights, pair, block):
    rows, rank = lat.shape
    count = kv.shape[0]
    heads, width = 2 * pair, weights[-1].shape[0] * 128
    return pl.pallas_call(
        functools.partial(attend_kernel, pair, len(weights)),
        grid=(rows // block,),
        in_specs=attend_specs(block, rank, count, weights),
        out_specs=[FAR, pl.BlockSpec((block, width), lambda i: (i, 0))],
        out_shape=[shape((heads, rows, 2 * HEAD)), shape((rows, width))],
        scratch_shapes=[
            pltpu.VMEM((heads, block, 2 * HEAD), BF16),
            pltpu.SemaphoreType.DMA((heads,)),
        ],
        compiler_params=params(ATTEND_LIMIT if rows == block else VMEM_LIMIT),
        cost_estimate=pl.CostEstimate(
            flops=2 * rows * heads * HEAD * (2 * count + rank + width),
            bytes_accessed=4 * count * HEAD + 2 * heads * HEAD * (rank + width),
            transcendentals=rows * heads * count,
        ),
        name="attend",
    )(lat, *tables, kv, keys, *weights)


def attend_back_kernel(
    pair, count, at_ref, lat_ref, cos_ref, sin_ref, places_ref, kv_ref, keys_ref, *refs
):
    weights, refs = refs[:count], refs[count:]
    saved_ref, d_attn_ref = refs[:2]
    grads_q, d_lat_refs, (near_ref, far_ref, d_kv_sum, d_lat_sum) = refs[2:4], refs[4:8], refs[8:12]
    sums = refs[12:]
    step, steps = pl.program_id(0), pl.num_programs(0)
    corner = at_ref[1]

    @pl.when(step == 0)
    def _():
        d_kv_sum[...] = jnp.zeros_like(d_kv_sum)
        for total in sums:
            total[...] = jnp.zeros_like(total)

    def store(c, h, grad_q):
        size = grads_q[c].shape[1] // (2 * pair)
        for i in range(2):
            here = slice((2 * h + i) * size, (2 * h + i + 1) * size)
            tile = grad_q[:, i * 128 : (i + 1) * 128].astype(BF16)
            grads_q[c][:, here, :] = tile.reshape(-1, size, 128)

    keys = keys_ref[...]
    allowed = (keys <= places_ref[:, 0:1]) & (keys >= places_ref[:, 1:2])
    d_attn, lat = d_attn_ref[...], lat_ref[...]
    d_lat = None
    for c in range(2):
        for h in range(pair):
            q, mix = saved_ref[c * pair + h, :, :HEAD], saved_ref[c * pair + h, :, HEAD:]
            w_q, w_out = head_q(weights, c, h, pair), head_out(weights, c, h, pair)
            d_o = times_transposed(d_attn, w_out).astype(BF16)
            delta = jnp.sum(d_o.astype(F32) * mix.astype(F32), axis=-1, keepdims=True)
            scores = jnp.where(allowed, times_transposed(q, kv_ref[:, :HEAD]), MASKED)
            terms = jnp.exp(scores - jnp.max(scores, axis=-1, keepdims=True))
            probs = terms * (1.0 / jnp.sum(terms, axis=-1, keepdims=True))
            d_probs = times_transposed(d_o, kv_ref[:, HEAD:])
            d_scores = (probs * (d_probs - delta)).astype(BF16)
            d_query = matmul(d_scores, kv_ref[:, :HEAD]) * HEAD**-0.5
            probs_low = probs.astype(BF16)
            for some in range(0, d_kv_sum.shape[0], 2048):
                these = slice(some, some + 2048)
                d_kv_sum[these, :HEAD] += contract_rows(d_scores[:, these], q)
                d_kv_sum[these, HEAD:] += contract_rows(probs_low[:, these], d_o)
            d_qpre = unrotate(d_query, cos_ref[...], sin_ref[...]).astype(BF16)
            grad_q = contract_rows(lat, d_qpre)
            share = times_transposed(d_qpre, w_q)
            d_lat = share if d_lat is None else d_lat + share
            if sums:
                sums[0][c, h] += grad_q
            else:
                store(c, h, grad_q)
    if sums:

        @pl.when(step == steps - 1)
        def _():
            for c in range(2):
                for h in range(pair):
                    store(c, h, sums[0][c, h])

    d_lat_sum[...] = d_lat
    share = d_lat.shape[1] // SQUARE
    dot = jnp.sum(d_lat * lat.astype(F32), axis=-1, keepdims=True)
    for m, d_lat_ref in enumerate(d_lat_refs):
        columns = pl.ds(pl.multiple_of((corner ^ m) * share, share), share)
        d_lat_ref[:, :share] = d_lat_sum[:, columns].astype(BF16)
        d_lat_ref[:, share:] = jnp.broadcast_to(dot, (d_lat.shape[0], 128)).astype(BF16)

    @pl.when(step == steps - 1)
    def _():
        size = near_ref.shape[0]
        near_ref[...] = d_kv_sum[:size, :].astype(near_ref.dtype)
        far_ref[...] = d_kv_sum[size:, :].astype(BF16)


def attend_back(at, lat, tables, kv, keys, weights, saved, d_attn, pair, block):
    rows, rank = lat.shape
    count = kv.shape[0]
    heads, width = 2 * pair, weights[-1].shape[0] * 128
    places = weights[0].shape[0]
    row = lambda size: pl.BlockSpec((block, size), lambda i: (i, 0))
    whole = lambda dims: pl.BlockSpec(dims, lambda i: (0,) * len(dims))
    grad_dims = (places, 2 * pair * rank // places, HEAD // 2)
    d_lat_size = rank // SQUARE + 128
    kv_dims = (count // 2, 2 * HEAD)
    sums = [pltpu.VMEM((2, pair, rank, HEAD), F32)] if rows != block else []
    return pl.pallas_call(
        functools.partial(attend_back_kernel, pair, len(weights)),
        grid=(rows // block,),
        in_specs=[SMEM]
        + attend_specs(block, rank, count, weights)
        + [pl.BlockSpec((heads, block, 2 * HEAD), lambda i: (0, i, 0)), row(width)],
        out_specs=[whole(grad_dims)] * 2 + [row(d_lat_size)] * SQUARE + [whole(kv_dims)] * 2,
        out_shape=[shape(grad_dims)] * 2
        + [shape((rows, d_lat_size))] * SQUARE
        + [shape(kv_dims, BF16 if sums else F32), shape(kv_dims)],
        scratch_shapes=[
            pltpu.VMEM((count, 2 * HEAD), F32),
            pltpu.VMEM((block, rank), F32),
        ]
        + sums,
        compiler_params=params(VMEM_LIMIT + len(sums) * 2**22),
        cost_estimate=pl.CostEstimate(
            flops=2 * rows * heads * HEAD * (5 * count + 2 * rank + width),
            bytes_accessed=12 * count * HEAD + 4 * heads * HEAD * (rank + width),
            transcendentals=rows * heads * count,
        ),
        name="attend_back",
    )(at, lat, *tables, kv, keys, *weights, saved, d_attn)


def out_grads_kernel(mix_ref, d_attn_ref, *refs):
    more, out_ref = refs[:-1], refs[-1]
    for h in range(mix_ref.shape[0]):
        grad = contract_rows(mix_ref[h], d_attn_ref[...])
        here = slice(h * HEAD, (h + 1) * HEAD)
        for tile in range(out_ref.shape[0]):
            value = grad[:, tile * 128 : (tile + 1) * 128]
            if more:
                value = value + more[0][tile, here, :].astype(F32)
            out_ref[tile, here, :] = value.astype(BF16)


def out_grads(saved, side, d_attn, *received):
    rows, width = d_attn.shape
    pair = saved.shape[0] // 2
    dims = (width // 128, pair * HEAD, 128)
    whole = lambda dims: pl.BlockSpec(dims, lambda i: (0,) * len(dims))
    return pl.pallas_call(
        out_grads_kernel,
        grid=(1,),
        in_specs=[pl.BlockSpec((pair, rows, HEAD), lambda i: (side, 0, 1)), whole((rows, width))]
        + [whole(dims)] * len(received),
        out_specs=whole(dims),
        out_shape=shape(dims),
        compiler_params=params(GRADS_LIMIT),
        cost_estimate=pl.CostEstimate(
            flops=2 * rows * pair * HEAD * width, bytes_accessed=4 * pair * HEAD * width, transcendentals=0
        ),
        name="out_grads",
    )(saved, d_attn, *received)


def latent_back_kernel(layers, at_ref, hat_ref, inverse_ref, x_ref, w_ref, *refs):
    parts, d_kv_refs, d_x_refs = (refs[i * SQUARE : (i + 1) * SQUARE] for i in range(3))
    near_ref, far_ref, d_sum, d_kv_sum, d_x_sum = refs[3 * SQUARE :]
    layer, corner, core = at_ref[0], at_ref[1], at_ref[2]
    count, width = x_ref.shape
    rows = count // SQUARE
    share = w_ref.shape[-1]
    rank_share = hat_ref.shape[1] // SQUARE
    places = [pl.ds(pl.multiple_of((corner ^ m) * rows, rows), rows) for m in range(SQUARE)]
    d_sum[...] = sum(part[...].astype(F32) for part in parts)
    for place, d_kv_ref in zip(places, d_kv_refs):
        d_kv_sum[place, :] = d_kv_ref[...]
    columns = pl.ds(pl.multiple_of(corner * rank_share, rank_share), rank_share)
    dot = d_sum[:, rank_share : rank_share + 1] * (1.0 / hat_ref.shape[1])
    d_lat = inverse_ref[...] * (d_sum[:, :rank_share] - hat_ref[:, columns] * dot)
    d_down = jnp.concatenate([d_lat.astype(BF16), d_kv_sum[...]], axis=1)
    weight = w_ref[...].reshape(width, share)
    d_x_sum[...] = times_transposed(d_down, weight).astype(BF16)
    for place, d_x_ref in zip(places, d_x_refs):
        d_x_ref[...] = d_x_sum[place, :]
    grad = contract_rows(x_ref[...], d_down)
    grad = grad.reshape(layers, SQUARE, 2, near_ref.shape[2], share)
    low, high = grad[:, :, 0], grad[:, :, 1]
    near = jnp.where(core == 0, low, high)
    far = jnp.where(core == 0, high, low).astype(BF16)
    for z in range(layers):
        k = lax.rem(layer + layers - z, layers)
        near_ref[k] = near[z]
        far_ref[k] = far[z]


def latent_back(at, hat, inverse, d_kv, x, weight, parts):
    count, width = x.shape
    places, _, lane_rows, share = weight.shape
    layers = places // SQUARE
    dims = (layers, SQUARE, lane_rows, share)
    return pl.pallas_call(
        functools.partial(latent_back_kernel, layers),
        in_specs=[SMEM] + [VMEM] * (4 + 2 * SQUARE),
        out_specs=[VMEM] * (SQUARE + 2),
        out_shape=[shape((count // SQUARE, width))] * SQUARE + [shape(dims, F32), shape(dims)],
        scratch_shapes=[
            pltpu.VMEM(parts[0].shape, F32),
            pltpu.VMEM((count, d_kv[0].shape[1]), BF16),
            pltpu.VMEM((count, width), BF16),
        ],
        compiler_params=params(),
        cost_estimate=pl.CostEstimate(
            flops=4 * count * width * share, bytes_accessed=10 * width * share, transcendentals=0
        ),
        name="latent_back",
    )(at, hat, inverse, x, weight, *parts, *d_kv)


def chunk(ref, q, tiles):
    columns = [(t * SQUARE + q) * 128 for t in range(tiles)]
    return jnp.concatenate([ref[:, c : c + 128] for c in columns], axis=1)


def mlp_kernel(
    h_ref,
    cot_ref,
    near_ref,
    far_ref,
    d_h_hbm,
    out_hbm,
    act_near_ref,
    act_far_ref,
    turned,
    d_h_ref,
    out_ref,
    sems,
):
    tiles = near_ref.shape[1]
    units = act_near_ref.shape[1]
    for q in range(SQUARE):
        turned[0, q] = chunk(h_ref, q, tiles).T
        turned[1, q] = chunk(cot_ref, q, tiles).T

    def weight(side, kind, q):
        here = slice(kind * units, (kind + 1) * units)
        return jnp.concatenate([side[q, t, here, :] for t in range(tiles)], axis=1)

    sides = ((near_ref, act_near_ref), (far_ref, act_far_ref))
    for side, acts in sides:

        def product(which, kind):
            return sum(matmul(weight(side, kind, q), turned[which, q]) for q in range(SQUARE))

        gate_act, up_proj, d_act = product(0, 0), product(0, 1), product(1, 2)
        sigmoid_gate = 1.0 / (1.0 + jnp.exp(-gate_act))
        silu_gate = gate_act * sigmoid_gate
        d_gate = d_act * up_proj * sigmoid_gate * (1.0 + gate_act * (1.0 - sigmoid_gate))
        acts[0] = d_gate.astype(BF16)
        acts[1] = (d_act * silu_gate).astype(BF16)
        acts[2] = (silu_gate * up_proj).astype(BF16)
    straight = [[acts[kind].T for kind in range(3)] for _, acts in sides]
    copies = []
    for i, (first, count, value_ref, hbm) in enumerate(
        ((0, 2, d_h_ref, d_h_hbm), (2, 1, out_ref, out_hbm))
    ):
        for q in range(SQUARE):
            value = sum(
                matmul(straight[c][kind], weight(sides[c][0], kind, q))
                for c in range(2)
                for kind in range(first, first + count)
            )
            for t in range(tiles):
                here = slice((t * SQUARE + q) * 128, (t * SQUARE + q + 1) * 128)
                value_ref[:, here] = value[:, t * 128 : (t + 1) * 128].astype(BF16)
        copies.append(pltpu.make_async_copy(value_ref, hbm, sems.at[i]))
        copies[-1].start()
    for copy in copies:
        copy.wait()


def mlp(h, cot, near, far):
    rows, width = h.shape
    units = near.shape[2] // 3
    low, acts = shape((rows, width)), shape((3, units, rows))
    return pl.pallas_call(
        mlp_kernel,
        in_specs=[VMEM] * 4,
        out_specs=[FAR, FAR, VMEM, VMEM],
        out_shape=[low, low, acts, acts],
        scratch_shapes=[
            pltpu.VMEM((2, SQUARE, width // SQUARE, rows), BF16),
            pltpu.VMEM((rows, width), BF16),
            pltpu.VMEM((rows, width), BF16),
            pltpu.SemaphoreType.DMA((2,)),
        ],
        compiler_params=params(MLP_LIMIT if rows <= 256 else VMEM_LIMIT),
        cost_estimate=pl.CostEstimate(
            flops=24 * rows * width * units,
            bytes_accessed=12 * width * units + 8 * rows * width,
            transcendentals=2 * rows * units,
        ),
        name="mlp",
    )(h, cot, near, far)


def unit_grads_kernel(acts_ref, value_ref, *refs):
    more, out_ref = refs[:-1], refs[-1]
    acts = acts_ref[0]
    tiles = out_ref.shape[1]
    for q in range(SQUARE):
        grad = matmul(acts, chunk(value_ref, q, tiles))
        for t in range(tiles):
            tile = grad[:, t * 128 : (t + 1) * 128]
            if more:
                tile = tile + more[0][q, t].astype(F32)
            out_ref[q, t] = tile.astype(BF16)


def unit_grads(acts, kind, value, received=None, kinds=None):
    rows, width = value.shape
    units = acts.shape[1]
    tiles = width // SQUARE // 128
    whole = lambda dims: pl.BlockSpec(dims, lambda i: (0,) * len(dims))
    dims = (SQUARE, tiles, units, 128)
    in_specs = [pl.BlockSpec((1, units, rows), lambda i: (kind, 0, 0)), whole((rows, width))]
    args, aliases, body = [acts, value], {}, unit_grads_kernel
    out_specs, out_dims = whole(dims), dims
    if received is not None:
        args.append(received)
        in_specs.append(whole(dims))
        if kind < 2:
            out_specs = pl.BlockSpec(dims, lambda i: (0, 0, kind, 0))
            out_dims = (SQUARE, tiles, 2 * units, 128)
    if kinds is not None:
        args.append(kinds)
        in_specs.append(HBM)
        aliases = {3: 0}
        body = lambda a, v, r, k, o: unit_grads_kernel(a, v, r, o)
    return pl.pallas_call(
        body,
        grid=(1,),
        in_specs=in_specs,
        out_specs=out_specs,
        out_shape=shape(out_dims),
        input_output_aliases=aliases,
        compiler_params=params(GRADS_LIMIT),
        cost_estimate=pl.CostEstimate(
            flops=2 * rows * width * units, bytes_accessed=4 * width * units, transcendentals=0
        ),
        name="unit_grads",
    )(*args)


def local(
    chips,
    tokens,
    attn_gain,
    q_gain,
    w_qdown,
    w_qup,
    w_kv,
    w_out,
    mlp_gain,
    w_gate,
    w_up,
    w_down,
    cotangent,
    seq_lengths,
    block_slots,
):
    layers = chips // SQUARE
    rows, width = tokens.shape[0] // 2, tokens.shape[1]
    lanes = width // chips
    rank = w_qdown.shape[1]
    rank_rows = w_qup.shape[0]
    pair = w_qup.shape[1] // HEAD // SQUARE
    units = w_gate.shape[1] // layers
    half = HEAD // 2
    place = lax.axis_index("seq")
    core = lax.axis_index("tp")
    layer, corner = place // SQUARE, place % SQUARE
    at = jnp.stack([layer, corner, core]).astype(jnp.int32)
    first = core == 0
    lines = [[z * SQUARE + c for z in range(layers)] for c in range(SQUARE)]
    square_groups = [[z * SQUARE + c for c in range(SQUARE)] for z in range(layers)]

    def across(value):
        return lax.ppermute(value, "tp", [(0, 1), (1, 0)])

    def along(value, step):
        pairs = [
            (z * SQUARE + c, (z + step) % layers * SQUARE + c)
            for z in range(layers)
            for c in range(SQUARE)
        ]
        return lax.ppermute(value, "seq", pairs)

    def within(value, flip):
        return lax.ppermute(value, "seq", [(i, i ^ flip) for i in range(chips)])

    def line_exchange(value):
        return lax.all_to_all(value, "seq", 0, 0, axis_index_groups=lines, tiled=True)

    def square_exchange(value):
        return lax.all_to_all(value, "seq", 0, 0, axis_index_groups=square_groups, tiled=True)

    def line_pieces(value):
        return [value] + [along(value, k) for k in range(1, layers)]

    def line_sum(blocks):
        return blocks[0].astype(F32) + sum(
            along(blocks[k], -k).astype(F32) for k in range(1, layers)
        )

    def by_layer(value):
        blocks = value.reshape(layers, rows, -1)
        return jnp.concatenate(
            [
                lax.dynamic_index_in_dim(blocks, (layer - z) % layers, 0, keepdims=False)
                for z in range(layers)
            ]
        )

    def square_pieces(value):
        return [value] + [within(value, m) for m in range(1, SQUARE)]

    def square_sum(blocks):
        return blocks[0].astype(F32) + sum(
            within(blocks[m], m).astype(F32) for m in range(1, SQUARE)
        )

    def after(value, *earlier):
        return lax.optimization_barrier((value,) + earlier)[0]

    def together(*values):
        return lax.optimization_barrier(values)

    def own(pair_value):
        return lax.dynamic_slice_in_dim(pair_value, core * rows, rows, 0)

    def both(mine, theirs, axis=0):
        return jnp.concatenate(
            [jnp.where(first, mine, theirs), jnp.where(first, theirs, mine)], axis=axis
        )

    def tiled(value):
        if lanes == 128:
            return value
        count, size, _ = value.shape
        value = jnp.swapaxes(value, 0, 1).reshape(size, count * lanes // 128, 128)
        return jnp.swapaxes(value, 0, 1)

    def untiled(value):
        if lanes == 128:
            return value
        count, size, _ = value.shape
        value = jnp.swapaxes(value, 0, 1).reshape(size, count * 128 // lanes, lanes)
        return jnp.swapaxes(value, 0, 1)

    def arranged(value):
        if lanes == 128:
            return value
        shaped = value.reshape(value.shape[0], -1, 128 // lanes, SQUARE, lanes)
        return jnp.swapaxes(shaped, 2, 3).reshape(value.shape)

    def unarranged(value):
        if lanes == 128:
            return value
        shaped = value.reshape(value.shape[0], -1, SQUARE, 128 // lanes, lanes)
        return jnp.swapaxes(shaped, 2, 3).reshape(value.shape)

    inputs = own(tokens).astype(F32)
    x_inverse = inverse_rms(inputs)
    x_hat = inputs * x_inverse
    def by_corner(pieces):
        pieces = jnp.stack(pieces)
        return jnp.stack(
            [
                lax.dynamic_index_in_dim(pieces, corner ^ q, 0, keepdims=False)
                for q in range(SQUARE)
            ]
        )

    x_all = by_corner(square_pieces(x_hat.astype(BF16))).reshape(-1, width)

    gain_rows = attn_gain.astype(F32)[:, None]
    down = jnp.concatenate([w_qdown, w_kv], axis=1)
    rank_share, kv_share = rank // SQUARE, 2 * HEAD // SQUARE

    def shares(value):
        return jnp.stack(
            [
                jnp.concatenate(
                    [
                        value[:, b * rank_share : (b + 1) * rank_share],
                        value[:, rank + b * kv_share : rank + (b + 1) * kv_share],
                    ],
                    axis=1,
                )
                for b in range(SQUARE)
            ]
        )

    def unshares(value):
        return jnp.concatenate(
            [value[b, :, :rank_share] for b in range(SQUARE)]
            + [value[b, :, rank_share:] for b in range(SQUARE)],
            axis=1,
        )

    down_scaled = (down.astype(F32) * gain_rows).astype(BF16)
    down_half = lax.dynamic_slice_in_dim(down_scaled, core * (lanes // 2), lanes // 2, 0)
    cot_own = own(cotangent)
    down_own = square_exchange(shares(down_half))
    cot_pieces = line_pieces(arranged(cot_own))
    cot_all = by_layer(jnp.concatenate(cot_pieces))
    down_near = line_pieces(after(down_own, *cot_pieces[1:]))
    down_far = [across(piece) for piece in down_near]

    q_gain_rows = q_gain.astype(F32)[:, None]
    qup_scaled = (w_qup.astype(F32) * q_gain_rows).astype(BF16)
    qup_send = qup_scaled.reshape(rank_rows, SQUARE, 2 * pair, half)
    qup_send = jnp.transpose(qup_send, (1, 2, 0, 3)).reshape(SQUARE, -1, lanes)
    qup_size = qup_send.shape[1]
    head_send = jnp.concatenate([qup_send, w_out.reshape(SQUARE, pair * HEAD, lanes)], axis=1)
    head_own = square_exchange(after(head_send, down_own))

    mlp_gain_rows = mlp_gain.astype(F32)[:, None]
    gate_send = (w_gate.astype(F32) * mlp_gain_rows).astype(BF16).T
    up_send = (w_up.astype(F32) * mlp_gain_rows).astype(BF16).T
    mlp_send = jnp.concatenate(
        [value.reshape(layers, units, lanes) for value in (gate_send, up_send, w_down)], axis=1
    )

    bounds = jnp.cumsum(seq_lengths)
    starts = bounds - seq_lengths

    def layout(blocks):
        natural = (blocks[:, None] * rows + jnp.arange(rows, dtype=jnp.int32)[None, :]).reshape(-1)
        member = (natural[:, None] >= starts[None, :]) & (natural[:, None] < bounds[None, :])
        return natural, jnp.sum(jnp.where(member, starts[None, :], 0), axis=1)

    back_steps = jnp.arange(layers, dtype=jnp.int32)
    flips = jnp.arange(SQUARE, dtype=jnp.int32)
    owners = (((layer - back_steps) % layers) * SQUARE)[None, :] + (corner ^ flips)[:, None]
    square_slots = block_slots[2 * (layer * SQUARE + flips) + core]
    row_natural, row_start = layout(square_slots)
    owners = owners.reshape(-1)
    near_natural, _ = layout(block_slots[2 * owners + core])
    far_natural, _ = layout(block_slots[2 * owners + 1 - core])
    key_natural = jnp.concatenate([near_natural, far_natural])[None, :]
    cosine, sine = angles(row_natural - row_start)
    lane = jnp.arange(128, dtype=jnp.int32)[None, :]
    tables = (cosine, sine, jnp.where(lane == 0, row_natural[:, None], row_start[:, None]))

    x_all = after(x_all, head_own)
    part, down_here = project(at, x_all, down_near, down_far)
    lat_hat, lat_low, lat_inverse, kv_own = latent(at, cosine, sine, square_pieces(part), rank)
    mlp_layer = line_exchange(after(mlp_send, *down_near[1:]))
    head_copies = jnp.tile(head_own, (layers, 1, 1))
    mlp_layer, kv_own, head_copies = together(mlp_layer, kv_own, head_copies)
    kv_line = jnp.concatenate(line_pieces(kv_own))
    mlp_near = lax.all_gather(tiled(mlp_layer), "seq", axis_index_groups=square_groups)

    head_near = line_exchange(after(head_copies, kv_line))
    kv_near = jnp.concatenate(square_pieces(kv_line))
    kv_all = jnp.concatenate([kv_near, across(kv_near)])
    head_near, kv_all = together(head_near, kv_all)
    head_far = across(head_near)
    if lanes == 128:
        head_weights = (head_near, head_far)
    else:
        head_weights = tuple(
            side[:, :qup_size].reshape(chips, -1, half) for side in (head_near, head_far)
        ) + tuple(tiled(side[:, qup_size:]) for side in (head_near, head_far))

    block = max(32, min(SQUARE * rows, 2**30 // kv_all.shape[0] ** 2))
    saved, attn_part = attend(
        lat_low, tables, kv_all, key_natural, head_weights, pair, block
    )
    mlp_near, attn_part = together(mlp_near, attn_part)
    mlp_far = across(mlp_near)
    attn_blocks = square_exchange(attn_part.reshape(SQUARE, rows, width))
    hidden = inputs + jnp.sum(attn_blocks.astype(F32), axis=0)
    h_inverse = inverse_rms(hidden)
    h_hat = hidden * h_inverse
    h_low = h_hat.astype(BF16)
    h_all = jnp.concatenate(line_pieces(arranged(h_low)))
    h_all = by_layer(h_all)

    d_h_part, mlp_part, acts_near, acts_far = mlp(h_all, cot_all, mlp_near, mlp_far)
    def line_blocks(value):
        return line_exchange(value.reshape(layers, rows, -1))

    def line_total(blocks):
        return unarranged(jnp.sum(blocks.astype(F32), axis=0))

    kinds = ((0, h_all), (1, h_all), (2, cot_all))
    far_grads = [unit_grads(acts_far, kind, value) for kind, value in kinds]
    d_h_lines = line_blocks(d_h_part)
    d_h_lines, acts_near, *far_grads = together(d_h_lines, acts_near, *far_grads)
    d_hscaled = line_total(d_h_lines)
    d_hidden = cot_own.astype(F32) + norm_back(d_hscaled, h_hat, h_inverse)
    mlp_grads = None
    for kind, value in kinds[:2]:
        mlp_grads = unit_grads(acts_near, kind, value, across(far_grads[kind]), mlp_grads)
    unit_sum = unit_grads(acts_near, 2, cot_all, across(far_grads[2]))
    mlp_blocks = after(mlp_part, d_hscaled).reshape(layers, rows, width)
    mlp_pieces = []
    for k in range(layers):
        block_out = lax.dynamic_index_in_dim(mlp_blocks, (layer - k) % layers, 0, keepdims=False)
        mlp_pieces.append(along(block_out, -k) if k else block_out)
    d_attn_all = square_exchange(jnp.tile(d_hidden.astype(BF16)[None], (SQUARE, 1, 1)))
    mlp_grads, unit_sum, d_attn_all, *mlp_pieces = together(
        mlp_grads, unit_sum, d_attn_all, *mlp_pieces
    )
    d_attn_all = d_attn_all.reshape(-1, width)
    gate_up_sum = lax.psum_scatter(mlp_grads, "seq", axis_index_groups=square_groups)
    unit_sum = lax.psum_scatter(unit_sum, "seq", axis_index_groups=square_groups)

    received = across(out_grads(saved, 1, d_attn_all))
    grad_out_total = untiled(out_grads(saved, 0, d_attn_all, received))
    head_out_lines = line_exchange(grad_out_total)
    mlp_own = unarranged(sum(piece.astype(F32) for piece in mlp_pieces))
    layer_out_own = (hidden + mlp_own).astype(BF16)
    layer_out = both(layer_out_own, across(layer_out_own))
    grad_q_near, grad_q_far, *d_lat_parts, d_kv_near, d_kv_far = attend_back(
        at,
        lat_low,
        tables,
        kv_all,
        key_natural,
        head_weights,
        saved,
        d_attn_all,
        pair,
        block,
    )
    d_kv_low = (d_kv_near.astype(F32) + across(d_kv_far).astype(F32)).astype(BF16)
    d_kv_line = square_sum(d_kv_low.reshape(SQUARE, layers * rows, 2 * HEAD)).astype(BF16)
    grad_q_total = (grad_q_near.astype(F32) + across(grad_q_far).astype(F32)).astype(BF16)
    grad_q_total = grad_q_total.reshape(chips, -1, lanes)
    head_out_lines, d_kv_line, grad_q_total = together(head_out_lines, d_kv_line, grad_q_total)
    d_kv_own = line_sum(d_kv_line.reshape(layers, rows, 2 * HEAD))
    own_cosine = lax.dynamic_slice_in_dim(cosine, corner * rows, rows, 0)
    own_sine = lax.dynamic_slice_in_dim(sine, corner * rows, rows, 0)
    d_kv_own = jnp.concatenate(
        [unrotate(d_kv_own[:, :HEAD], own_cosine, own_sine), d_kv_own[:, HEAD:]], axis=1
    ).astype(BF16)
    head_q = line_exchange(after(grad_q_total, d_kv_own))
    kv_share_of = lambda m: lax.dynamic_slice_in_dim(d_kv_own, (corner ^ m) * kv_share, kv_share, 1)
    d_kv_share = [kv_share_of(0)] + [within(kv_share_of(m), m) for m in range(1, SQUARE)]
    d_lat_received = [d_lat_parts[0]] + [within(d_lat_parts[m], m) for m in range(1, SQUARE)]
    head_q, *d_lat_received = together(head_q, *d_lat_received)

    *d_x_blocks, down_grad_near, down_grad_far = latent_back(
        at, lat_hat, lat_inverse, d_kv_share, x_all, down_here, d_lat_received
    )
    d_x_received = [within(d_x_blocks[m], m) for m in range(1, SQUARE)]
    down_sum = (down_grad_near + across(down_grad_far).astype(F32)).astype(BF16)

    def square_send(value):
        blocks = [
            lax.dynamic_index_in_dim(value, corner ^ m, 0, keepdims=False) for m in range(SQUARE)
        ]
        return [blocks[0]] + [within(blocks[m], m) for m in range(1, SQUARE)]

    gate_up_back = line_exchange(untiled(after(gate_up_sum, head_q)))
    head_sum = jnp.concatenate(
        [
            jnp.sum(blocks.reshape(layers, SQUARE, -1, lanes).astype(F32), axis=0).astype(BF16)
            for blocks in (head_q, head_out_lines)
        ],
        axis=1,
    )
    head_pieces = square_send(head_sum)
    down_blocks = [down_sum[k] for k in range(layers)]
    gate_up_back, *received = together(gate_up_back, *d_x_received, *down_blocks)
    d_x_received, down_blocks = received[: SQUARE - 1], received[SQUARE - 1 :]
    d_xscaled = d_x_blocks[0].astype(F32) + sum(block.astype(F32) for block in d_x_received)
    token_own = (d_hidden + norm_back(d_xscaled, x_hat, x_inverse)).astype(BF16)
    token_grad = both(token_own, across(token_own))
    down_pieces = [along(down_blocks[k], -k) for k in range(1, layers)]
    unit_back = line_exchange(untiled(after(unit_sum, *down_pieces)))
    down_line = down_blocks[0].astype(F32) + sum(piece.astype(F32) for piece in down_pieces)
    down_pieces = square_send(down_line.astype(BF16))
    unit_back, *received = together(unit_back, *down_pieces, *head_pieces)
    down_pieces, head_pieces = received[:SQUARE], received[SQUARE:]
    head_sum = by_corner(head_pieces)
    down_back = unshares(by_corner(down_pieces)).astype(F32)
    down_back = both(down_back, across(down_back))
    attn_gain_part = jnp.sum(down_back * down.astype(F32), axis=1)
    down_grad = down_back * gain_rows
    qdown_part, kv_part = down_grad[:, :rank], down_grad[:, rank:]

    gate_back, up_back, down_part = (
        value.reshape(layers * units, lanes).astype(F32)
        for value in (gate_up_back[:, :units], gate_up_back[:, units:], unit_back)
    )
    gate_back, up_back = gate_back.T, up_back.T
    gate_part, up_part = gate_back * mlp_gain_rows, up_back * mlp_gain_rows
    mlp_gain_part = jnp.sum(gate_back * w_gate.astype(F32) + up_back * w_up.astype(F32), axis=1)

    qup_back = head_sum[:, :qup_size].reshape(SQUARE, 2 * pair, rank_rows, half)
    qup_back = jnp.transpose(qup_back, (2, 0, 1, 3)).reshape(rank_rows, -1).astype(F32)
    out_part = head_sum[:, qup_size:].reshape(-1, lanes).astype(F32)
    qup_part = qup_back * q_gain_rows
    q_gain_half = jnp.sum(qup_back * w_qup.astype(F32), axis=1)
    gain_parts = jnp.concatenate([q_gain_half, mlp_gain_part])
    gain_parts = gain_parts + across(gain_parts)
    q_gain_part, mlp_gain_part = gain_parts[:rank_rows], gain_parts[rank_rows:]
    return (
        layer_out,
        token_grad,
        attn_gain_part,
        q_gain_part,
        qdown_part,
        qup_part,
        kv_part,
        out_part,
        mlp_gain_part,
        gate_part,
        up_part,
        down_part,
    )


def solution(mesh):
    in_specs = (
        P("seq", None),
        P("seq"),
        P("seq"),
        P("seq", None),
        P("seq", "tp"),
        P("seq", None),
        P("tp", "seq"),
        P("seq"),
        P("seq", "tp"),
        P("seq", "tp"),
        P("tp", "seq"),
        P("seq", None),
        P(),
        P(),
    )
    out_specs = (
        P("seq", None),
        P("seq", None),
        P("seq"),
        P("seq"),
        P("seq", None),
        P("seq", "tp"),
        P("seq", None),
        P("tp", "seq"),
        P("seq"),
        P("seq", "tp"),
        P("seq", "tp"),
        P("tp", "seq"),
    )
    body = functools.partial(local, mesh.shape["seq"])
    return jax.shard_map(body, mesh=mesh, in_specs=in_specs, out_specs=out_specs, check_vma=False)
```

```python
import functools
import math

import jax
import jax.numpy as jnp
from jax import lax
from jax.experimental import pallas as pl
from jax.experimental.pallas import tpu as pltpu
from jax.sharding import PartitionSpec as P

EPSILON = 1e-06
ROPE_BASE = 10000.0
MASKED = -1e30
HEAD = 256
SQUARE = 4
VMEM_LIMIT = 56 * 1024 * 1024
MLP_LIMIT = 26 * 1024 * 1024
ATTEND_LIMIT = 22 * 1024 * 1024
GRADS_LIMIT = 16 * 1024 * 1024
BF16 = jnp.bfloat16
F32 = jnp.float32


def matmul(left, right):
    return jnp.dot(left, right, preferred_element_type=F32)


def contract_rows(left, right):
    return lax.dot_general(left, right, (((0,), (0,)), ((), ())), preferred_element_type=F32)


def times_transposed(left, right):
    return lax.dot_general(left, right, (((1,), (1,)), ((), ())), preferred_element_type=F32)


def inverse_rms(vector):
    return lax.rsqrt(jnp.mean(vector * vector, axis=-1, keepdims=True) + EPSILON)


def norm_back(scaled_grad, normed, inverse):
    return inverse * (scaled_grad - normed * jnp.mean(scaled_grad * normed, axis=-1, keepdims=True))


def angles(position):
    half = HEAD // 2
    frequency = jnp.exp(jnp.arange(half, dtype=F32) * (-math.log(ROPE_BASE) / half))
    phase = position.astype(F32)[:, None] * frequency[None, :]
    return jnp.cos(phase), jnp.sin(phase)


def rotate(vector, cosine, sine):
    half = HEAD // 2
    front, back = vector[:, :half], vector[:, half:]
    return jnp.concatenate([front * cosine - back * sine, back * cosine + front * sine], axis=1)


def unrotate(vector, cosine, sine):
    return rotate(vector, cosine, -sine)


def params(limit=VMEM_LIMIT):
    return pltpu.CompilerParams(vmem_limit_bytes=limit)


VMEM = pl.BlockSpec(memory_space=pltpu.VMEM)
SMEM = pl.BlockSpec(memory_space=pltpu.SMEM)
HBM = pl.BlockSpec(memory_space=pl.ANY)
FAR = pl.BlockSpec(memory_space=pltpu.HBM)


def shape(dims, dtype=BF16):
    return jax.ShapeDtypeStruct(tuple(dims), dtype)


def project_kernel(layers, at_ref, x_ref, *refs):
    near, far = refs[:layers], refs[layers : 2 * layers]
    part_ref, w_ref, sems = refs[2 * layers :]
    layer, core = at_ref[0], at_ref[2]
    copies = []
    for c, pieces in enumerate((near, far)):
        side = core if c == 0 else 1 - core
        for k, piece in enumerate(pieces):
            first = lax.rem(layer + layers - k, layers) * SQUARE
            target = w_ref.at[pl.ds(first, SQUARE), side]
            copies.append(pltpu.make_async_copy(piece, target, sems.at[c, k]))
    for copy in copies:
        copy.start()
    for copy in copies:
        copy.wait()
    width, share = x_ref.shape[1], w_ref.shape[-1]
    part_ref[...] = matmul(x_ref[...], w_ref[...].reshape(width, share)).astype(BF16)


def project(at, x, near, far):
    layers = len(near)
    rows, width = x.shape
    _, lane_rows, share = near[0].shape
    return pl.pallas_call(
        functools.partial(project_kernel, layers),
        in_specs=[SMEM, VMEM] + [HBM] * (2 * layers),
        out_specs=[VMEM, VMEM],
        out_shape=[
            shape((rows, share)),
            shape((layers * SQUARE, 2, lane_rows, share)),
        ],
        scratch_shapes=[pltpu.SemaphoreType.DMA((2, layers))],
        compiler_params=params(),
        cost_estimate=pl.CostEstimate(
            flops=2 * rows * width * share, bytes_accessed=4 * width * share, transcendentals=0
        ),
        name="project",
    )(at, x, *near, *far)


def latent_kernel(at_ref, cos_ref, sin_ref, *refs):
    parts = refs[:SQUARE]
    hat_ref, low_ref, inverse_ref, kv_ref, kv_sum = refs[SQUARE:]
    corner = at_ref[1]
    rows = kv_ref.shape[0]
    rank_share, kv_share = hat_ref.shape[1] // SQUARE, 2 * HEAD // SQUARE
    own = pl.ds(pl.multiple_of(corner * rows, rows), rows)
    for m, part in enumerate(parts):
        b = corner ^ m
        columns = pl.ds(pl.multiple_of(b * rank_share, rank_share), rank_share)
        hat_ref[:, columns] = part[:, :rank_share].astype(F32)
        columns = pl.ds(pl.multiple_of(b * kv_share, kv_share), kv_share)
        kv_sum[:, columns] = part[own, rank_share:].astype(F32)
    q_lat = hat_ref[...]
    inverse = inverse_rms(q_lat)
    hat = q_lat * inverse
    hat_ref[...] = hat
    low_ref[...] = hat.astype(BF16)
    inverse_ref[...] = inverse
    kv_ref[:, :HEAD] = rotate(kv_sum[:, :HEAD], cos_ref[own, :], sin_ref[own, :]).astype(BF16)
    kv_ref[:, HEAD:] = kv_sum[:, HEAD:].astype(BF16)


def latent(at, cosine, sine, parts, rank):
    count = parts[0].shape[0]
    rows = count // SQUARE
    return pl.pallas_call(
        latent_kernel,
        in_specs=[SMEM] + [VMEM] * (2 + SQUARE),
        out_specs=[VMEM] * 4,
        out_shape=[
            shape((count, rank), F32),
            shape((count, rank)),
            shape((count, 1), F32),
            shape((rows, 2 * HEAD)),
        ],
        scratch_shapes=[pltpu.VMEM((rows, 2 * HEAD), F32)],
        compiler_params=params(),
        cost_estimate=pl.CostEstimate(flops=8 * count * rank, bytes_accessed=10 * count * rank, transcendentals=0),
        name="latent",
    )(at, cosine, sine, *parts)


def head_q(weights, c, h, pair):
    ref = weights[c]
    size = (ref.shape[1] if len(weights) == 4 else ref.shape[1] - pair * HEAD) // (2 * pair)
    halves = [ref[:, (2 * h + i) * size : (2 * h + i + 1) * size, :] for i in range(2)]
    return jnp.concatenate([half.reshape(-1, HEAD // 2) for half in halves], axis=1)


def head_out(weights, c, h, pair):
    ref = weights[len(weights) - 2 + c]
    first = ref.shape[1] - pair * HEAD + h * HEAD
    return jnp.concatenate(
        [ref[tile, first : first + HEAD, :] for tile in range(ref.shape[0])], axis=1
    )


def attend_kernel(pair, count, lat_ref, cos_ref, sin_ref, places_ref, kv_ref, keys_ref, *refs):
    weights, (saved_ref, part_ref, kept, sems) = refs[:count], refs[count:]
    keys = keys_ref[...]
    rows = part_ref.shape[0]
    here = pl.ds(pl.program_id(0) * rows, rows)
    allowed = (keys <= places_ref[:, 0:1]) & (keys >= places_ref[:, 1:2])
    part, copies = None, []
    for c in range(2):
        for h in range(pair):
            head = c * pair + h
            q_pre = matmul(lat_ref[...], head_q(weights, c, h, pair))
            q = rotate(q_pre, cos_ref[...], sin_ref[...]).astype(BF16)
            q = (q.astype(F32) * HEAD**-0.5).astype(BF16)
            scores = jnp.where(allowed, times_transposed(q, kv_ref[:, :HEAD]), MASKED)
            top = jnp.max(scores, axis=-1, keepdims=True)
            terms = jnp.exp(scores - top)
            total = jnp.sum(terms, axis=-1, keepdims=True)
            mix = (matmul(terms.astype(BF16), kv_ref[:, HEAD:]) / total).astype(BF16)
            kept[head, :, :HEAD] = q
            kept[head, :, HEAD:] = mix
            copy = pltpu.make_async_copy(kept.at[head], saved_ref.at[head, here], sems.at[head])
            copy.start()
            copies.append(copy)
            share = matmul(mix, head_out(weights, c, h, pair))
            part = share if part is None else part + share
    part_ref[...] = part.astype(BF16)
    for copy in copies:
        copy.wait()


def attend_specs(block, rank, count, weights):
    row = lambda size: pl.BlockSpec((block, size), lambda i: (i, 0))
    whole = lambda dims: pl.BlockSpec(dims, lambda i: (0,) * len(dims))
    half = HEAD // 2
    return [
        row(rank),
        row(half),
        row(half),
        row(128),
        whole((count, 2 * HEAD)),
        whole((1, count)),
    ] + [whole(weight.shape) for weight in weights]


def attend(lat, tables, kv, keys, weights, pair, block):
    rows, rank = lat.shape
    count = kv.shape[0]
    heads, width = 2 * pair, weights[-1].shape[0] * 128
    return pl.pallas_call(
        functools.partial(attend_kernel, pair, len(weights)),
        grid=(rows // block,),
        in_specs=attend_specs(block, rank, count, weights),
        out_specs=[FAR, pl.BlockSpec((block, width), lambda i: (i, 0))],
        out_shape=[shape((heads, rows, 2 * HEAD)), shape((rows, width))],
        scratch_shapes=[
            pltpu.VMEM((heads, block, 2 * HEAD), BF16),
            pltpu.SemaphoreType.DMA((heads,)),
        ],
        compiler_params=params(ATTEND_LIMIT if rows == block else VMEM_LIMIT),
        cost_estimate=pl.CostEstimate(
            flops=2 * rows * heads * HEAD * (2 * count + rank + width),
            bytes_accessed=4 * count * HEAD + 2 * heads * HEAD * (rank + width),
            transcendentals=rows * heads * count,
        ),
        name="attend",
    )(lat, *tables, kv, keys, *weights)


def attend_back_kernel(
    pair, count, at_ref, lat_ref, cos_ref, sin_ref, places_ref, kv_ref, keys_ref, *refs
):
    weights, refs = refs[:count], refs[count:]
    saved_ref, d_attn_ref = refs[:2]
    grads_q, d_lat_refs, (near_ref, far_ref, d_kv_sum, d_lat_sum) = refs[2:4], refs[4:8], refs[8:12]
    sums = refs[12:]
    step, steps = pl.program_id(0), pl.num_programs(0)
    corner = at_ref[1]

    @pl.when(step == 0)
    def _():
        d_kv_sum[...] = jnp.zeros_like(d_kv_sum)
        for total in sums:
            total[...] = jnp.zeros_like(total)

    def store(c, h, grad_q):
        size = grads_q[c].shape[1] // (2 * pair)
        for i in range(2):
            here = slice((2 * h + i) * size, (2 * h + i + 1) * size)
            tile = grad_q[:, i * 128 : (i + 1) * 128].astype(BF16)
            grads_q[c][:, here, :] = tile.reshape(-1, size, 128)

    keys = keys_ref[...]
    allowed = (keys <= places_ref[:, 0:1]) & (keys >= places_ref[:, 1:2])
    d_attn, lat = d_attn_ref[...], lat_ref[...]
    d_lat = None
    for c in range(2):
        for h in range(pair):
            q, mix = saved_ref[c * pair + h, :, :HEAD], saved_ref[c * pair + h, :, HEAD:]
            w_q, w_out = head_q(weights, c, h, pair), head_out(weights, c, h, pair)
            d_o = times_transposed(d_attn, w_out).astype(BF16)
            delta = jnp.sum(d_o.astype(F32) * mix.astype(F32), axis=-1, keepdims=True)
            scores = jnp.where(allowed, times_transposed(q, kv_ref[:, :HEAD]), MASKED)
            terms = jnp.exp(scores - jnp.max(scores, axis=-1, keepdims=True))
            probs = terms * (1.0 / jnp.sum(terms, axis=-1, keepdims=True))
            d_probs = times_transposed(d_o, kv_ref[:, HEAD:])
            d_scores = (probs * (d_probs - delta)).astype(BF16)
            d_query = matmul(d_scores, kv_ref[:, :HEAD]) * HEAD**-0.5
            probs_low = probs.astype(BF16)
            for some in range(0, d_kv_sum.shape[0], 2048):
                these = slice(some, some + 2048)
                d_kv_sum[these, :HEAD] += contract_rows(d_scores[:, these], q)
                d_kv_sum[these, HEAD:] += contract_rows(probs_low[:, these], d_o)
            d_qpre = unrotate(d_query, cos_ref[...], sin_ref[...]).astype(BF16)
            grad_q = contract_rows(lat, d_qpre)
            share = times_transposed(d_qpre, w_q)
            d_lat = share if d_lat is None else d_lat + share
            if sums:
                sums[0][c, h] += grad_q
            else:
                store(c, h, grad_q)
    if sums:

        @pl.when(step == steps - 1)
        def _():
            for c in range(2):
                for h in range(pair):
                    store(c, h, sums[0][c, h])

    d_lat_sum[...] = d_lat
    share = d_lat.shape[1] // SQUARE
    dot = jnp.sum(d_lat * lat.astype(F32), axis=-1, keepdims=True)
    for m, d_lat_ref in enumerate(d_lat_refs):
        columns = pl.ds(pl.multiple_of((corner ^ m) * share, share), share)
        d_lat_ref[:, :share] = d_lat_sum[:, columns].astype(BF16)
        d_lat_ref[:, share:] = jnp.broadcast_to(dot, (d_lat.shape[0], 128)).astype(BF16)

    @pl.when(step == steps - 1)
    def _():
        size = near_ref.shape[0]
        near_ref[...] = d_kv_sum[:size, :].astype(near_ref.dtype)
        far_ref[...] = d_kv_sum[size:, :].astype(BF16)


def attend_back(at, lat, tables, kv, keys, weights, saved, d_attn, pair, block):
    rows, rank = lat.shape
    count = kv.shape[0]
    heads, width = 2 * pair, weights[-1].shape[0] * 128
    places = weights[0].shape[0]
    row = lambda size: pl.BlockSpec((block, size), lambda i: (i, 0))
    whole = lambda dims: pl.BlockSpec(dims, lambda i: (0,) * len(dims))
    grad_dims = (places, 2 * pair * rank // places, HEAD // 2)
    d_lat_size = rank // SQUARE + 128
    kv_dims = (count // 2, 2 * HEAD)
    sums = [pltpu.VMEM((2, pair, rank, HEAD), F32)] if rows != block else []
    return pl.pallas_call(
        functools.partial(attend_back_kernel, pair, len(weights)),
        grid=(rows // block,),
        in_specs=[SMEM]
        + attend_specs(block, rank, count, weights)
        + [pl.BlockSpec((heads, block, 2 * HEAD), lambda i: (0, i, 0)), row(width)],
        out_specs=[whole(grad_dims)] * 2 + [row(d_lat_size)] * SQUARE + [whole(kv_dims)] * 2,
        out_shape=[shape(grad_dims)] * 2
        + [shape((rows, d_lat_size))] * SQUARE
        + [shape(kv_dims, BF16 if sums else F32), shape(kv_dims)],
        scratch_shapes=[
            pltpu.VMEM((count, 2 * HEAD), F32),
            pltpu.VMEM((block, rank), F32),
        ]
        + sums,
        compiler_params=params(VMEM_LIMIT + len(sums) * 2**22),
        cost_estimate=pl.CostEstimate(
            flops=2 * rows * heads * HEAD * (5 * count + 2 * rank + width),
            bytes_accessed=12 * count * HEAD + 4 * heads * HEAD * (rank + width),
            transcendentals=rows * heads * count,
        ),
        name="attend_back",
    )(at, lat, *tables, kv, keys, *weights, saved, d_attn)


def out_grads_kernel(mix_ref, d_attn_ref, *refs):
    more, out_ref = refs[:-1], refs[-1]
    for h in range(mix_ref.shape[0]):
        grad = contract_rows(mix_ref[h], d_attn_ref[...])
        here = slice(h * HEAD, (h + 1) * HEAD)
        for tile in range(out_ref.shape[0]):
            value = grad[:, tile * 128 : (tile + 1) * 128]
            if more:
                value = value + more[0][tile, here, :].astype(F32)
            out_ref[tile, here, :] = value.astype(BF16)


def out_grads(saved, side, d_attn, *received):
    rows, width = d_attn.shape
    pair = saved.shape[0] // 2
    dims = (width // 128, pair * HEAD, 128)
    whole = lambda dims: pl.BlockSpec(dims, lambda i: (0,) * len(dims))
    return pl.pallas_call(
        out_grads_kernel,
        grid=(1,),
        in_specs=[pl.BlockSpec((pair, rows, HEAD), lambda i: (side, 0, 1)), whole((rows, width))]
        + [whole(dims)] * len(received),
        out_specs=whole(dims),
        out_shape=shape(dims),
        compiler_params=params(GRADS_LIMIT),
        cost_estimate=pl.CostEstimate(
            flops=2 * rows * pair * HEAD * width, bytes_accessed=4 * pair * HEAD * width, transcendentals=0
        ),
        name="out_grads",
    )(saved, d_attn, *received)


def latent_back_kernel(layers, at_ref, hat_ref, inverse_ref, x_ref, w_ref, *refs):
    parts, d_kv_refs, d_x_refs = (refs[i * SQUARE : (i + 1) * SQUARE] for i in range(3))
    near_ref, far_ref, d_sum, d_kv_sum, d_x_sum = refs[3 * SQUARE :]
    layer, corner, core = at_ref[0], at_ref[1], at_ref[2]
    count, width = x_ref.shape
    rows = count // SQUARE
    share = w_ref.shape[-1]
    rank_share = hat_ref.shape[1] // SQUARE
    places = [pl.ds(pl.multiple_of((corner ^ m) * rows, rows), rows) for m in range(SQUARE)]
    d_sum[...] = sum(part[...].astype(F32) for part in parts)
    for place, d_kv_ref in zip(places, d_kv_refs):
        d_kv_sum[place, :] = d_kv_ref[...]
    columns = pl.ds(pl.multiple_of(corner * rank_share, rank_share), rank_share)
    dot = d_sum[:, rank_share : rank_share + 1] * (1.0 / hat_ref.shape[1])
    d_lat = inverse_ref[...] * (d_sum[:, :rank_share] - hat_ref[:, columns] * dot)
    d_down = jnp.concatenate([d_lat.astype(BF16), d_kv_sum[...]], axis=1)
    weight = w_ref[...].reshape(width, share)
    d_x_sum[...] = times_transposed(d_down, weight).astype(BF16)
    for place, d_x_ref in zip(places, d_x_refs):
        d_x_ref[...] = d_x_sum[place, :]
    grad = contract_rows(x_ref[...], d_down)
    grad = grad.reshape(layers, SQUARE, 2, near_ref.shape[2], share)
    low, high = grad[:, :, 0], grad[:, :, 1]
    near = jnp.where(core == 0, low, high)
    far = jnp.where(core == 0, high, low).astype(BF16)
    for z in range(layers):
        k = lax.rem(layer + layers - z, layers)
        near_ref[k] = near[z]
        far_ref[k] = far[z]


def latent_back(at, hat, inverse, d_kv, x, weight, parts):
    count, width = x.shape
    places, _, lane_rows, share = weight.shape
    layers = places // SQUARE
    dims = (layers, SQUARE, lane_rows, share)
    return pl.pallas_call(
        functools.partial(latent_back_kernel, layers),
        in_specs=[SMEM] + [VMEM] * (4 + 2 * SQUARE),
        out_specs=[VMEM] * (SQUARE + 2),
        out_shape=[shape((count // SQUARE, width))] * SQUARE + [shape(dims, F32), shape(dims)],
        scratch_shapes=[
            pltpu.VMEM(parts[0].shape, F32),
            pltpu.VMEM((count, d_kv[0].shape[1]), BF16),
            pltpu.VMEM((count, width), BF16),
        ],
        compiler_params=params(),
        cost_estimate=pl.CostEstimate(
            flops=4 * count * width * share, bytes_accessed=10 * width * share, transcendentals=0
        ),
        name="latent_back",
    )(at, hat, inverse, x, weight, *parts, *d_kv)


def chunk(ref, q, tiles):
    columns = [(t * SQUARE + q) * 128 for t in range(tiles)]
    return jnp.concatenate([ref[:, c : c + 128] for c in columns], axis=1)


def mlp_kernel(
    h_ref,
    cot_ref,
    near_ref,
    far_ref,
    d_h_ref,
    act_near_ref,
    act_far_ref,
    turned,
):
    tiles = near_ref.shape[1]
    units = act_near_ref.shape[1]
    for q in range(SQUARE):
        turned[0, q] = chunk(h_ref, q, tiles).T
        turned[1, q] = chunk(cot_ref, q, tiles).T

    def weight(side, kind, q):
        here = slice(kind * units, (kind + 1) * units)
        return jnp.concatenate([side[q, t, here, :] for t in range(tiles)], axis=1)

    sides = ((near_ref, act_near_ref), (far_ref, act_far_ref))
    for side, acts in sides:

        def product(which, kind):
            return sum(matmul(weight(side, kind, q), turned[which, q]) for q in range(SQUARE))

        gate_act, up_proj, d_act = product(0, 0), product(0, 1), product(1, 2)
        sigmoid_gate = 1.0 / (1.0 + jnp.exp(-gate_act))
        silu_gate = gate_act * sigmoid_gate
        d_gate = d_act * up_proj * sigmoid_gate * (1.0 + gate_act * (1.0 - sigmoid_gate))
        acts[0] = d_gate.astype(BF16)
        acts[1] = (d_act * silu_gate).astype(BF16)
        acts[2] = (silu_gate * up_proj).astype(BF16)
    straight = [[acts[kind].T for kind in range(3)] for _, acts in sides]
    for q in range(SQUARE):
        value = sum(
            matmul(straight[c][kind], weight(sides[c][0], kind, q)) for c in range(2) for kind in range(2)
        )
        for t in range(tiles):
            here = slice((t * SQUARE + q) * 128, (t * SQUARE + q + 1) * 128)
            d_h_ref[:, here] = value[:, t * 128 : (t + 1) * 128].astype(BF16)


def mlp_out_kernel(near_ref, far_ref, act_near_ref, act_far_ref, out_ref):
    tiles, units = near_ref.shape[1], act_near_ref.shape[1]
    sides = ((near_ref, act_near_ref[0].T), (far_ref, act_far_ref[0].T))
    for q in range(SQUARE):
        value = sum(
            matmul(act, jnp.concatenate([side[q, t] for t in range(tiles)], axis=1))
            for side, act in sides
        )
        for t in range(tiles):
            here = slice((t * SQUARE + q) * 128, (t * SQUARE + q + 1) * 128)
            out_ref[:, here] = value[:, t * 128 : (t + 1) * 128].astype(BF16)


def mlp_out(near, far, act_near, act_far):
    _, units, rows = act_near.shape
    tiles = near.shape[1]
    width = SQUARE * tiles * 128
    weights = pl.BlockSpec((SQUARE, tiles, units, 128), lambda i: (0, 0, 2, 0))
    acts = pl.BlockSpec((1, units, rows), lambda i: (2, 0, 0))
    return pl.pallas_call(
        mlp_out_kernel,
        grid=(1,),
        in_specs=[weights, weights, acts, acts],
        out_specs=pl.BlockSpec((rows, width), lambda i: (0, 0)),
        out_shape=shape((rows, width)),
        compiler_params=params(GRADS_LIMIT if rows <= 256 else VMEM_LIMIT),
        cost_estimate=pl.CostEstimate(
            flops=4 * rows * width * units, bytes_accessed=4 * width * units, transcendentals=0
        ),
        name="mlp_out",
    )(near, far, act_near, act_far)


def mlp(h, cot, near, far):
    rows, width = h.shape
    units = near.shape[2] // 3
    low, acts = shape((rows, width)), shape((3, units, rows))
    return pl.pallas_call(
        mlp_kernel,
        in_specs=[VMEM] * 4,
        out_specs=[VMEM] * 3,
        out_shape=[low, acts, acts],
        scratch_shapes=[pltpu.VMEM((2, SQUARE, width // SQUARE, rows), BF16)],
        compiler_params=params(MLP_LIMIT if rows <= 256 else VMEM_LIMIT),
        cost_estimate=pl.CostEstimate(
            flops=20 * rows * width * units,
            bytes_accessed=12 * width * units + 6 * rows * width,
            transcendentals=2 * rows * units,
        ),
        name="mlp",
    )(h, cot, near, far)


def unit_grads_kernel(acts_ref, value_ref, *refs):
    more, out_ref = refs[:-1], refs[-1]
    acts = acts_ref[0]
    tiles = out_ref.shape[1]
    for q in range(SQUARE):
        grad = matmul(acts, chunk(value_ref, q, tiles))
        for t in range(tiles):
            tile = grad[:, t * 128 : (t + 1) * 128]
            if more:
                tile = tile + more[0][q, t].astype(F32)
            out_ref[q, t] = tile.astype(BF16)


def unit_grads(acts, kind, value, received=None, kinds=None):
    rows, width = value.shape
    units = acts.shape[1]
    tiles = width // SQUARE // 128
    whole = lambda dims: pl.BlockSpec(dims, lambda i: (0,) * len(dims))
    dims = (SQUARE, tiles, units, 128)
    in_specs = [pl.BlockSpec((1, units, rows), lambda i: (kind, 0, 0)), whole((rows, width))]
    args, aliases, body = [acts, value], {}, unit_grads_kernel
    out_specs, out_dims = whole(dims), dims
    if received is not None:
        args.append(received)
        in_specs.append(whole(dims))
        if kind < 2:
            out_specs = pl.BlockSpec(dims, lambda i: (0, 0, kind, 0))
            out_dims = (SQUARE, tiles, 2 * units, 128)
    if kinds is not None:
        args.append(kinds)
        in_specs.append(HBM)
        aliases = {3: 0}
        body = lambda a, v, r, k, o: unit_grads_kernel(a, v, r, o)
    return pl.pallas_call(
        body,
        grid=(1,),
        in_specs=in_specs,
        out_specs=out_specs,
        out_shape=shape(out_dims),
        input_output_aliases=aliases,
        compiler_params=params(GRADS_LIMIT),
        cost_estimate=pl.CostEstimate(flops=1000, bytes_accessed=1000, transcendentals=0),
        name="unit_grads",
    )(*args)


def local(
    chips,
    tokens,
    attn_gain,
    q_gain,
    w_qdown,
    w_qup,
    w_kv,
    w_out,
    mlp_gain,
    w_gate,
    w_up,
    w_down,
    cotangent,
    seq_lengths,
    block_slots,
):
    layers = chips // SQUARE
    rows, width = tokens.shape[0] // 2, tokens.shape[1]
    lanes = width // chips
    rank = w_qdown.shape[1]
    rank_rows = w_qup.shape[0]
    pair = w_qup.shape[1] // HEAD // SQUARE
    units = w_gate.shape[1] // layers
    half = HEAD // 2
    place = lax.axis_index("seq")
    core = lax.axis_index("tp")
    layer, corner = place // SQUARE, place % SQUARE
    at = jnp.stack([layer, corner, core]).astype(jnp.int32)
    first = core == 0
    lines = [[z * SQUARE + c for z in range(layers)] for c in range(SQUARE)]
    square_groups = [[z * SQUARE + c for c in range(SQUARE)] for z in range(layers)]

    def across(value):
        return lax.ppermute(value, "tp", [(0, 1), (1, 0)])

    def along(value, step):
        pairs = [
            (z * SQUARE + c, (z + step) % layers * SQUARE + c)
            for z in range(layers)
            for c in range(SQUARE)
        ]
        return lax.ppermute(value, "seq", pairs)

    def within(value, flip):
        return lax.ppermute(value, "seq", [(i, i ^ flip) for i in range(chips)])

    def line_exchange(value):
        return lax.all_to_all(value, "seq", 0, 0, axis_index_groups=lines, tiled=True)

    def square_exchange(value):
        return lax.all_to_all(value, "seq", 0, 0, axis_index_groups=square_groups, tiled=True)

    def line_pieces(value):
        return [value] + [along(value, k) for k in range(1, layers)]

    def line_sum(blocks):
        return blocks[0].astype(F32) + sum(
            along(blocks[k], -k).astype(F32) for k in range(1, layers)
        )

    def by_layer(value):
        blocks = value.reshape(layers, rows, -1)
        return jnp.concatenate(
            [
                lax.dynamic_index_in_dim(blocks, (layer - z) % layers, 0, keepdims=False)
                for z in range(layers)
            ]
        )

    def square_pieces(value):
        return [value] + [within(value, m) for m in range(1, SQUARE)]

    def square_sum(blocks):
        return blocks[0].astype(F32) + sum(
            within(blocks[m], m).astype(F32) for m in range(1, SQUARE)
        )

    def after(value, *earlier):
        return lax.optimization_barrier((value,) + earlier)[0]

    def together(*values):
        return lax.optimization_barrier(values)

    def own(pair_value):
        return lax.dynamic_slice_in_dim(pair_value, core * rows, rows, 0)

    def both(mine, theirs, axis=0):
        return jnp.concatenate(
            [jnp.where(first, mine, theirs), jnp.where(first, theirs, mine)], axis=axis
        )

    def tiled(value):
        if lanes == 128:
            return value
        count, size, _ = value.shape
        value = jnp.swapaxes(value, 0, 1).reshape(size, count * lanes // 128, 128)
        return jnp.swapaxes(value, 0, 1)

    def untiled(value):
        if lanes == 128:
            return value
        count, size, _ = value.shape
        value = jnp.swapaxes(value, 0, 1).reshape(size, count * 128 // lanes, lanes)
        return jnp.swapaxes(value, 0, 1)

    def arranged(value):
        if lanes == 128:
            return value
        shaped = value.reshape(value.shape[0], -1, 128 // lanes, SQUARE, lanes)
        return jnp.swapaxes(shaped, 2, 3).reshape(value.shape)

    def unarranged(value):
        if lanes == 128:
            return value
        shaped = value.reshape(value.shape[0], -1, SQUARE, 128 // lanes, lanes)
        return jnp.swapaxes(shaped, 2, 3).reshape(value.shape)

    inputs = own(tokens).astype(F32)
    x_inverse = inverse_rms(inputs)
    x_hat = inputs * x_inverse
    def square_send(value):
        blocks = [
            lax.dynamic_index_in_dim(value, corner ^ m, 0, keepdims=False) for m in range(SQUARE)
        ]
        return [blocks[0]] + [within(blocks[m], m) for m in range(1, SQUARE)]

    def by_corner(pieces):
        pieces = jnp.stack(pieces)
        return jnp.stack(
            [
                lax.dynamic_index_in_dim(pieces, corner ^ q, 0, keepdims=False)
                for q in range(SQUARE)
            ]
        )

    x_low = x_hat.astype(BF16)

    gain_rows = attn_gain.astype(F32)[:, None]
    down = jnp.concatenate([w_qdown, w_kv], axis=1)
    rank_share, kv_share = rank // SQUARE, 2 * HEAD // SQUARE

    def shares(value):
        return jnp.stack(
            [
                jnp.concatenate(
                    [
                        value[:, b * rank_share : (b + 1) * rank_share],
                        value[:, rank + b * kv_share : rank + (b + 1) * kv_share],
                    ],
                    axis=1,
                )
                for b in range(SQUARE)
            ]
        )

    def unshares(value):
        return jnp.concatenate(
            [value[b, :, :rank_share] for b in range(SQUARE)]
            + [value[b, :, rank_share:] for b in range(SQUARE)],
            axis=1,
        )

    down_scaled = (down.astype(F32) * gain_rows).astype(BF16)
    down_half = lax.dynamic_slice_in_dim(down_scaled, core * (lanes // 2), lanes // 2, 0)
    cot_own = own(cotangent)
    down_own = square_exchange(shares(down_half))
    down_near = line_pieces(down_own)
    x_pieces = square_pieces(after(x_low, down_own))
    x_all = by_corner(x_pieces).reshape(-1, width)
    down_far = [across(piece) for piece in down_near]

    q_gain_rows = q_gain.astype(F32)[:, None]
    qup_scaled = (w_qup.astype(F32) * q_gain_rows).astype(BF16)
    qup_send = qup_scaled.reshape(rank_rows, SQUARE, 2 * pair, half)
    qup_send = jnp.transpose(qup_send, (1, 2, 0, 3)).reshape(SQUARE, -1, lanes)
    qup_size = qup_send.shape[1]
    head_send = jnp.concatenate([qup_send, w_out.reshape(SQUARE, pair * HEAD, lanes)], axis=1)
    head_own = by_corner(square_send(after(head_send, x_pieces[1])))

    mlp_gain_rows = mlp_gain.astype(F32)[:, None]
    gate_send = (w_gate.astype(F32) * mlp_gain_rows).astype(BF16).T
    up_send = (w_up.astype(F32) * mlp_gain_rows).astype(BF16).T
    mlp_send = jnp.concatenate(
        [value.reshape(layers, units, lanes) for value in (gate_send, up_send, w_down)], axis=1
    )

    bounds = jnp.cumsum(seq_lengths)
    starts = bounds - seq_lengths

    def layout(blocks):
        natural = (blocks[:, None] * rows + jnp.arange(rows, dtype=jnp.int32)[None, :]).reshape(-1)
        member = (natural[:, None] >= starts[None, :]) & (natural[:, None] < bounds[None, :])
        return natural, jnp.sum(jnp.where(member, starts[None, :], 0), axis=1)

    back_steps = jnp.arange(layers, dtype=jnp.int32)
    flips = jnp.arange(SQUARE, dtype=jnp.int32)
    owners = (((layer - back_steps) % layers) * SQUARE)[None, :] + (corner ^ flips)[:, None]
    square_slots = block_slots[2 * (layer * SQUARE + flips) + core]
    row_natural, row_start = layout(square_slots)
    owners = owners.reshape(-1)
    near_natural, _ = layout(block_slots[2 * owners + core])
    far_natural, _ = layout(block_slots[2 * owners + 1 - core])
    key_natural = jnp.concatenate([near_natural, far_natural])[None, :]
    cosine, sine = angles(row_natural - row_start)
    lane = jnp.arange(128, dtype=jnp.int32)[None, :]
    tables = (cosine, sine, jnp.where(lane == 0, row_natural[:, None], row_start[:, None]))

    cot_copies = jnp.tile(arranged(cot_own), (layers, 1))
    head_copies = jnp.tile(head_own, (layers, 1, 1))
    part, down_here = project(at, x_all, down_near, down_far)
    head_copies, cot_copies, *part_pieces = together(head_copies, cot_copies, *square_pieces(part))
    lat_hat, lat_low, lat_inverse, kv_own = latent(at, cosine, sine, part_pieces, rank)
    mlp_layer = line_exchange(after(mlp_send, *down_near[1:]))
    mlp_layer, head_copies, *kv_pieces = together(mlp_layer, head_copies, *line_pieces(kv_own))
    kv_line = jnp.concatenate(kv_pieces)
    mlp_near = lax.all_gather(tiled(mlp_layer), "seq", axis_index_groups=square_groups)

    head_near = line_exchange(head_copies)
    kv_near = jnp.concatenate(square_pieces(kv_line))
    kv_all = jnp.concatenate([kv_near, across(kv_near)])
    head_near, kv_all = together(head_near, kv_all)
    head_far = across(head_near)
    if lanes == 128:
        head_weights = (head_near, head_far)
    else:
        head_weights = tuple(
            side[:, :qup_size].reshape(chips, -1, half) for side in (head_near, head_far)
        ) + tuple(tiled(side[:, qup_size:]) for side in (head_near, head_far))

    block = max(32, min(SQUARE * rows, 2**30 // kv_all.shape[0] ** 2))
    saved, attn_part = attend(
        lat_low, tables, kv_all, key_natural, head_weights, pair, block
    )
    cot_lines = line_exchange(after(cot_copies, head_near))
    attn_pieces = square_send(attn_part.reshape(SQUARE, rows, width))
    mlp_near, cot_all, *attn_pieces = together(mlp_near, cot_lines, *attn_pieces)
    mlp_far = across(mlp_near)
    hidden = inputs + sum(piece.astype(F32) for piece in attn_pieces)
    h_inverse = inverse_rms(hidden)
    h_hat = hidden * h_inverse
    h_low = h_hat.astype(BF16)
    h_all = jnp.concatenate(line_pieces(arranged(h_low)))
    h_all = by_layer(h_all)

    d_h_part, acts_near, acts_far = mlp(h_all, cot_all, mlp_near, mlp_far)
    mlp_part = mlp_out(mlp_near, mlp_far, acts_near, acts_far)
    def line_blocks(value):
        return line_exchange(value.reshape(layers, rows, -1))

    def line_total(blocks):
        return unarranged(jnp.sum(blocks.astype(F32), axis=0))

    kinds = ((0, h_all), (1, h_all), (2, cot_all))
    far_grads = [unit_grads(acts_far, kind, value) for kind, value in kinds]
    d_h_lines = line_blocks(d_h_part)
    d_h_lines, acts_near, mlp_part, *far_grads = together(
        d_h_lines, acts_near, mlp_part, *far_grads
    )
    d_hscaled = line_total(d_h_lines)
    d_hidden = cot_own.astype(F32) + norm_back(d_hscaled, h_hat, h_inverse)
    mlp_grads = None
    for kind, value in kinds[:2]:
        mlp_grads = unit_grads(acts_near, kind, value, across(far_grads[kind]), mlp_grads)
    unit_sum = unit_grads(acts_near, 2, cot_all, across(far_grads[2]))
    mlp_blocks = mlp_part.reshape(layers, rows, width)
    mlp_pieces = []
    for k in range(layers):
        block_out = lax.dynamic_index_in_dim(mlp_blocks, (layer - k) % layers, 0, keepdims=False)
        mlp_pieces.append(along(after(block_out, d_h_lines), -k) if k else block_out)
    d_attn_all = square_exchange(jnp.tile(d_hidden.astype(BF16)[None], (SQUARE, 1, 1)))
    mlp_grads, unit_sum, d_attn_all, *mlp_pieces = together(
        mlp_grads, unit_sum, d_attn_all, *mlp_pieces
    )
    d_attn_all = d_attn_all.reshape(-1, width)
    gate_up_sum = lax.psum_scatter(mlp_grads, "seq", axis_index_groups=square_groups)
    unit_sum = lax.psum_scatter(unit_sum, "seq", axis_index_groups=square_groups)

    received = across(out_grads(saved, 1, d_attn_all))
    grad_out_total = untiled(out_grads(saved, 0, d_attn_all, received))
    head_out_lines = line_exchange(grad_out_total)
    mlp_own = unarranged(sum(piece.astype(F32) for piece in mlp_pieces))
    layer_out_own = (hidden + mlp_own).astype(BF16)
    layer_out = both(layer_out_own, across(layer_out_own))
    grad_q_near, grad_q_far, *d_lat_parts, d_kv_near, d_kv_far = attend_back(
        at,
        lat_low,
        tables,
        kv_all,
        key_natural,
        head_weights,
        saved,
        d_attn_all,
        pair,
        block,
    )
    d_kv_low = (d_kv_near.astype(F32) + across(d_kv_far).astype(F32)).astype(BF16)
    d_kv_line = square_sum(d_kv_low.reshape(SQUARE, layers * rows, 2 * HEAD)).astype(BF16)
    grad_q_total = (grad_q_near.astype(F32) + across(grad_q_far).astype(F32)).astype(BF16)
    grad_q_total = grad_q_total.reshape(chips, -1, lanes)
    d_kv_blocks = d_kv_line.reshape(layers, rows, 2 * HEAD)
    d_kv_blocks = [d_kv_blocks[0]] + [along(d_kv_blocks[k], -k) for k in range(1, layers)]
    head_out_lines, grad_q_total, *d_kv_blocks = together(head_out_lines, grad_q_total, *d_kv_blocks)
    d_kv_own = sum(block.astype(F32) for block in d_kv_blocks)
    own_cosine = lax.dynamic_slice_in_dim(cosine, corner * rows, rows, 0)
    own_sine = lax.dynamic_slice_in_dim(sine, corner * rows, rows, 0)
    d_kv_own = jnp.concatenate(
        [unrotate(d_kv_own[:, :HEAD], own_cosine, own_sine), d_kv_own[:, HEAD:]], axis=1
    ).astype(BF16)
    head_q = line_exchange(grad_q_total)
    kv_share_of = lambda m: lax.dynamic_slice_in_dim(d_kv_own, (corner ^ m) * kv_share, kv_share, 1)
    d_kv_share = [kv_share_of(0)] + [within(kv_share_of(m), m) for m in range(1, SQUARE)]
    d_lat_received = [d_lat_parts[0]] + [within(d_lat_parts[m], m) for m in range(1, SQUARE)]
    head_q, *d_lat_received = together(head_q, *d_lat_received)

    *d_x_blocks, down_grad_near, down_grad_far = latent_back(
        at, lat_hat, lat_inverse, d_kv_share, x_all, down_here, d_lat_received
    )
    d_x_received = [within(d_x_blocks[m], m) for m in range(1, SQUARE)]
    down_sum = (down_grad_near + across(down_grad_far).astype(F32)).astype(BF16)

    gate_up_raw = line_exchange(untiled(after(gate_up_sum, head_q)))
    head_sum = jnp.concatenate(
        [
            jnp.sum(blocks.reshape(layers, SQUARE, -1, lanes).astype(F32), axis=0).astype(BF16)
            for blocks in (head_q, head_out_lines)
        ],
        axis=1,
    )
    head_pieces = square_send(head_sum)
    down_blocks = [down_sum[k] for k in range(layers)]
    down_pieces = [down_blocks[0]] + [along(down_blocks[k], -k) for k in range(1, layers)]
    gate_up_back, *received = together(gate_up_raw, *d_x_received, *down_pieces)
    d_x_received, down_pieces = received[: SQUARE - 1], received[SQUARE - 1 :]
    d_xscaled = d_x_blocks[0].astype(F32) + sum(block.astype(F32) for block in d_x_received)
    token_own = (d_hidden + norm_back(d_xscaled, x_hat, x_inverse)).astype(BF16)
    token_grad = both(token_own, across(token_own))
    unit_back = line_exchange(untiled(after(unit_sum, gate_up_raw)))
    down_line = sum(piece.astype(F32) for piece in down_pieces)
    down_pieces = square_send(down_line.astype(BF16))
    unit_back, *received = together(unit_back, *down_pieces, *head_pieces)
    down_pieces, head_pieces = received[:SQUARE], received[SQUARE:]
    head_sum = by_corner(head_pieces)
    down_back = unshares(by_corner(down_pieces)).astype(F32)
    down_back = both(down_back, across(down_back))
    attn_gain_part = jnp.sum(down_back * down.astype(F32), axis=1)
    down_grad = down_back * gain_rows
    qdown_part, kv_part = down_grad[:, :rank], down_grad[:, rank:]

    gate_back, up_back, down_part = (
        value.reshape(layers * units, lanes).astype(F32)
        for value in (gate_up_back[:, :units], gate_up_back[:, units:], unit_back)
    )
    gate_back, up_back = gate_back.T, up_back.T
    gate_part, up_part = gate_back * mlp_gain_rows, up_back * mlp_gain_rows
    mlp_gain_part = jnp.sum(gate_back * w_gate.astype(F32) + up_back * w_up.astype(F32), axis=1)

    qup_back = head_sum[:, :qup_size].reshape(SQUARE, 2 * pair, rank_rows, half)
    qup_back = jnp.transpose(qup_back, (2, 0, 1, 3)).reshape(rank_rows, -1).astype(F32)
    out_part = head_sum[:, qup_size:].reshape(-1, lanes).astype(F32)
    qup_part = qup_back * q_gain_rows
    q_gain_half = jnp.sum(qup_back * w_qup.astype(F32), axis=1)
    gain_parts = jnp.concatenate([q_gain_half, mlp_gain_part])
    gain_parts = gain_parts + across(gain_parts)
    q_gain_part, mlp_gain_part = gain_parts[:rank_rows], gain_parts[rank_rows:]
    return (
        layer_out,
        token_grad,
        attn_gain_part,
        q_gain_part,
        qdown_part,
        qup_part,
        kv_part,
        out_part,
        mlp_gain_part,
        gate_part,
        up_part,
        down_part,
    )


def solution(mesh):
    in_specs = (
        P("seq", None),
        P("seq"),
        P("seq"),
        P("seq", None),
        P("seq", "tp"),
        P("seq", None),
        P("tp", "seq"),
        P("seq"),
        P("seq", "tp"),
        P("seq", "tp"),
        P("tp", "seq"),
        P("seq", None),
        P(),
        P(),
    )
    out_specs = (
        P("seq", None),
        P("seq", None),
        P("seq"),
        P("seq"),
        P("seq", None),
        P("seq", "tp"),
        P("seq", None),
        P("tp", "seq"),
        P("seq"),
        P("seq", "tp"),
        P("seq", "tp"),
        P("tp", "seq"),
    )
    body = functools.partial(local, mesh.shape["seq"])
    return jax.shard_map(body, mesh=mesh, in_specs=in_specs, out_specs=out_specs, check_vma=False)
```

```python
import functools
import math

import jax
import jax.numpy as jnp
from jax import lax
from jax.experimental import pallas as pl
from jax.experimental.pallas import tpu as pltpu
from jax.sharding import PartitionSpec as P

EPSILON = 1e-06
ROPE_BASE = 10000.0
MASKED = -1e30
HEAD = 256
SQUARE = 4
VMEM_LIMIT = 56 * 1024 * 1024
MLP_LIMIT = 23 * 1024 * 1024
ATTEND_LIMIT = 40 * 1024 * 1024
GRADS_LIMIT = 16 * 1024 * 1024
BF16 = jnp.bfloat16
F32 = jnp.float32


def matmul(left, right):
    return jnp.dot(left, right, preferred_element_type=F32)


def contract_rows(left, right):
    return lax.dot_general(left, right, (((0,), (0,)), ((), ())), preferred_element_type=F32)


def times_transposed(left, right):
    return lax.dot_general(left, right, (((1,), (1,)), ((), ())), preferred_element_type=F32)


def inverse_rms(vector):
    return lax.rsqrt(jnp.mean(vector * vector, axis=-1, keepdims=True) + EPSILON)


def norm_back(scaled_grad, normed, inverse):
    return inverse * (scaled_grad - normed * jnp.mean(scaled_grad * normed, axis=-1, keepdims=True))


def angles(position):
    half = HEAD // 2
    frequency = jnp.exp(jnp.arange(half, dtype=F32) * (-math.log(ROPE_BASE) / half))
    phase = position.astype(F32)[:, None] * frequency[None, :]
    return jnp.cos(phase), jnp.sin(phase)


def rotate(vector, cosine, sine):
    half = HEAD // 2
    front, back = vector[:, :half], vector[:, half:]
    return jnp.concatenate([front * cosine - back * sine, back * cosine + front * sine], axis=1)


def unrotate(vector, cosine, sine):
    return rotate(vector, cosine, -sine)


def params(limit=VMEM_LIMIT):
    return pltpu.CompilerParams(vmem_limit_bytes=limit)


VMEM = pl.BlockSpec(memory_space=pltpu.VMEM)
SMEM = pl.BlockSpec(memory_space=pltpu.SMEM)
HBM = pl.BlockSpec(memory_space=pl.ANY)
FAR = pl.BlockSpec(memory_space=pltpu.HBM)


def shape(dims, dtype=BF16):
    return jax.ShapeDtypeStruct(tuple(dims), dtype)


def project_kernel(layers, at_ref, x_ref, *refs):
    near, far = refs[:layers], refs[layers : 2 * layers]
    part_ref, w_ref, sems = refs[2 * layers :]
    layer, core = at_ref[0], at_ref[2]
    copies = []
    for c, pieces in enumerate((near, far)):
        side = core if c == 0 else 1 - core
        for k, piece in enumerate(pieces):
            first = lax.rem(layer + layers - k, layers) * SQUARE
            target = w_ref.at[pl.ds(first, SQUARE), side]
            copies.append(pltpu.make_async_copy(piece, target, sems.at[c, k]))
    for copy in copies:
        copy.start()
    for copy in copies:
        copy.wait()
    width, share = x_ref.shape[1], w_ref.shape[-1]
    part_ref[...] = matmul(x_ref[...], w_ref[...].reshape(width, share)).astype(BF16)


def project(at, x, near, far):
    layers = len(near)
    rows, width = x.shape
    _, lane_rows, share = near[0].shape
    return pl.pallas_call(
        functools.partial(project_kernel, layers),
        in_specs=[SMEM, VMEM] + [HBM] * (2 * layers),
        out_specs=[VMEM, VMEM],
        out_shape=[
            shape((rows, share)),
            shape((layers * SQUARE, 2, lane_rows, share)),
        ],
        scratch_shapes=[pltpu.SemaphoreType.DMA((2, layers))],
        compiler_params=params(),
        cost_estimate=pl.CostEstimate(
            flops=2 * rows * width * share, bytes_accessed=4 * width * share, transcendentals=0
        ),
        name="project",
    )(at, x, *near, *far)


def latent_kernel(at_ref, cos_ref, sin_ref, *refs):
    parts = refs[:SQUARE]
    hat_ref, low_ref, inverse_ref, kv_ref, kv_sum = refs[SQUARE:]
    corner = at_ref[1]
    rows = kv_ref.shape[0]
    rank_share, kv_share = hat_ref.shape[1] // SQUARE, 2 * HEAD // SQUARE
    own = pl.ds(pl.multiple_of(corner * rows, rows), rows)
    for m, part in enumerate(parts):
        b = corner ^ m
        columns = pl.ds(pl.multiple_of(b * rank_share, rank_share), rank_share)
        hat_ref[:, columns] = part[:, :rank_share].astype(F32)
        columns = pl.ds(pl.multiple_of(b * kv_share, kv_share), kv_share)
        kv_sum[:, columns] = part[own, rank_share:].astype(F32)
    q_lat = hat_ref[...]
    inverse = inverse_rms(q_lat)
    hat = q_lat * inverse
    hat_ref[...] = hat
    low_ref[...] = hat.astype(BF16)
    inverse_ref[...] = inverse
    kv_ref[:, :HEAD] = rotate(kv_sum[:, :HEAD], cos_ref[own, :], sin_ref[own, :]).astype(BF16)
    kv_ref[:, HEAD:] = kv_sum[:, HEAD:].astype(BF16)


def latent(at, cosine, sine, parts, rank):
    count = parts[0].shape[0]
    rows = count // SQUARE
    return pl.pallas_call(
        latent_kernel,
        in_specs=[SMEM] + [VMEM] * (2 + SQUARE),
        out_specs=[VMEM] * 4,
        out_shape=[
            shape((count, rank), F32),
            shape((count, rank)),
            shape((count, 1), F32),
            shape((rows, 2 * HEAD)),
        ],
        scratch_shapes=[pltpu.VMEM((rows, 2 * HEAD), F32)],
        compiler_params=params(),
        cost_estimate=pl.CostEstimate(flops=8 * count * rank, bytes_accessed=10 * count * rank, transcendentals=0),
        name="latent",
    )(at, cosine, sine, *parts)


def head_q(weights, c, h, pair):
    ref = weights[c]
    size = (ref.shape[1] if len(weights) == 4 else ref.shape[1] - pair * HEAD) // (2 * pair)
    halves = [ref[:, (2 * h + i) * size : (2 * h + i + 1) * size, :] for i in range(2)]
    return jnp.concatenate([half.reshape(-1, HEAD // 2) for half in halves], axis=1)


def head_out(weights, c, h, pair):
    ref = weights[len(weights) - 2 + c]
    first = ref.shape[1] - pair * HEAD + h * HEAD
    return jnp.concatenate(
        [ref[tile, first : first + HEAD, :] for tile in range(ref.shape[0])], axis=1
    )


def attend_kernel(pair, count, lat_ref, cos_ref, sin_ref, places_ref, kv_ref, keys_ref, *refs):
    weights, (saved_ref, part_ref, kept, sems) = refs[:count], refs[count:]
    keys = keys_ref[...]
    rows = part_ref.shape[0]
    here = pl.ds(pl.program_id(0) * rows, rows)
    allowed = (keys <= places_ref[:, 0:1]) & (keys >= places_ref[:, 1:2])
    part, copies = None, []
    for c in range(2):
        for h in range(pair):
            head = c * pair + h
            q_pre = matmul(lat_ref[...], head_q(weights, c, h, pair))
            q = rotate(q_pre, cos_ref[...], sin_ref[...]).astype(BF16)
            q = (q.astype(F32) * HEAD**-0.5).astype(BF16)
            scores = jnp.where(allowed, times_transposed(q, kv_ref[:, :HEAD]), MASKED)
            top = jnp.max(scores, axis=-1, keepdims=True)
            terms = jnp.exp(scores - top)
            total = jnp.sum(terms, axis=-1, keepdims=True)
            mix = (matmul(terms.astype(BF16), kv_ref[:, HEAD:]) / total).astype(BF16)
            kept[head, :, :HEAD] = q
            kept[head, :, HEAD:] = mix
            copy = pltpu.make_async_copy(kept.at[head], saved_ref.at[head, here], sems.at[head])
            copy.start()
            copies.append(copy)
            share = matmul(mix, head_out(weights, c, h, pair))
            part = share if part is None else part + share
    part_ref[...] = part.astype(BF16)
    for copy in copies:
        copy.wait()


def attend_specs(block, rank, count, weights):
    row = lambda size: pl.BlockSpec((block, size), lambda i: (i, 0))
    whole = lambda dims: pl.BlockSpec(dims, lambda i: (0,) * len(dims))
    half = HEAD // 2
    return [
        row(rank),
        row(half),
        row(half),
        row(128),
        whole((count, 2 * HEAD)),
        whole((1, count)),
    ] + [whole(weight.shape) for weight in weights]


def attend(lat, tables, kv, keys, weights, pair, block):
    rows, rank = lat.shape
    count = kv.shape[0]
    heads, width = 2 * pair, weights[-1].shape[0] * 128
    return pl.pallas_call(
        functools.partial(attend_kernel, pair, len(weights)),
        grid=(rows // block,),
        in_specs=attend_specs(block, rank, count, weights),
        out_specs=[FAR, pl.BlockSpec((block, width), lambda i: (i, 0))],
        out_shape=[shape((heads, rows, 2 * HEAD)), shape((rows, width))],
        scratch_shapes=[
            pltpu.VMEM((heads, block, 2 * HEAD), BF16),
            pltpu.SemaphoreType.DMA((heads,)),
        ],
        compiler_params=params(ATTEND_LIMIT if rows == block else VMEM_LIMIT),
        cost_estimate=pl.CostEstimate(
            flops=2 * rows * heads * HEAD * (2 * count + rank + width),
            bytes_accessed=4 * count * HEAD + 2 * heads * HEAD * (rank + width),
            transcendentals=rows * heads * count,
        ),
        name="attend",
    )(lat, *tables, kv, keys, *weights)


def attend_back_kernel(
    pair, count, at_ref, lat_ref, cos_ref, sin_ref, places_ref, kv_ref, keys_ref, *refs
):
    weights, refs = refs[:count], refs[count:]
    saved_ref, d_attn_ref = refs[:2]
    grads_q, d_lat_refs, (near_ref, far_ref, d_kv_sum, d_lat_sum) = refs[2:4], refs[4:8], refs[8:12]
    sums = refs[12:]
    step, steps = pl.program_id(0), pl.num_programs(0)
    corner = at_ref[1]

    @pl.when(step == 0)
    def _():
        d_kv_sum[...] = jnp.zeros_like(d_kv_sum)
        for total in sums:
            total[...] = jnp.zeros_like(total)

    def store(c, h, grad_q):
        size = grads_q[c].shape[1] // (2 * pair)
        for i in range(2):
            here = slice((2 * h + i) * size, (2 * h + i + 1) * size)
            tile = grad_q[:, i * 128 : (i + 1) * 128].astype(BF16)
            grads_q[c][:, here, :] = tile.reshape(-1, size, 128)

    keys = keys_ref[...]
    allowed = (keys <= places_ref[:, 0:1]) & (keys >= places_ref[:, 1:2])
    d_attn, lat = d_attn_ref[...], lat_ref[...]
    d_lat = None
    for c in range(2):
        for h in range(pair):
            q, mix = saved_ref[c * pair + h, :, :HEAD], saved_ref[c * pair + h, :, HEAD:]
            w_q, w_out = head_q(weights, c, h, pair), head_out(weights, c, h, pair)
            d_o = times_transposed(d_attn, w_out).astype(BF16)
            delta = jnp.sum(d_o.astype(F32) * mix.astype(F32), axis=-1, keepdims=True)
            scores = jnp.where(allowed, times_transposed(q, kv_ref[:, :HEAD]), MASKED)
            terms = jnp.exp(scores - jnp.max(scores, axis=-1, keepdims=True))
            probs = terms * (1.0 / jnp.sum(terms, axis=-1, keepdims=True))
            d_probs = times_transposed(d_o, kv_ref[:, HEAD:])
            d_scores = (probs * (d_probs - delta)).astype(BF16)
            d_query = matmul(d_scores, kv_ref[:, :HEAD]) * HEAD**-0.5
            probs_low = probs.astype(BF16)
            for some in range(0, d_kv_sum.shape[0], 2048):
                these = slice(some, some + 2048)
                d_kv_sum[these, :HEAD] += contract_rows(d_scores[:, these], q)
                d_kv_sum[these, HEAD:] += contract_rows(probs_low[:, these], d_o)
            d_qpre = unrotate(d_query, cos_ref[...], sin_ref[...]).astype(BF16)
            grad_q = contract_rows(lat, d_qpre)
            share = times_transposed(d_qpre, w_q)
            d_lat = share if d_lat is None else d_lat + share
            if sums:
                sums[0][c, h] += grad_q
            else:
                store(c, h, grad_q)
    if sums:

        @pl.when(step == steps - 1)
        def _():
            for c in range(2):
                for h in range(pair):
                    store(c, h, sums[0][c, h])

    d_lat_sum[...] = d_lat
    share = d_lat.shape[1] // SQUARE
    dot = jnp.sum(d_lat * lat.astype(F32), axis=-1, keepdims=True)
    for m, d_lat_ref in enumerate(d_lat_refs):
        columns = pl.ds(pl.multiple_of((corner ^ m) * share, share), share)
        d_lat_ref[:, :share] = d_lat_sum[:, columns].astype(BF16)
        d_lat_ref[:, share:] = jnp.broadcast_to(dot, (d_lat.shape[0], 128)).astype(BF16)

    @pl.when(step == steps - 1)
    def _():
        size = near_ref.shape[0]
        near_ref[...] = d_kv_sum[:size, :].astype(near_ref.dtype)
        far_ref[...] = d_kv_sum[size:, :].astype(BF16)


def attend_back(at, lat, tables, kv, keys, weights, saved, d_attn, pair, block):
    rows, rank = lat.shape
    count = kv.shape[0]
    heads, width = 2 * pair, weights[-1].shape[0] * 128
    places = weights[0].shape[0]
    row = lambda size: pl.BlockSpec((block, size), lambda i: (i, 0))
    whole = lambda dims: pl.BlockSpec(dims, lambda i: (0,) * len(dims))
    grad_dims = (places, 2 * pair * rank // places, HEAD // 2)
    d_lat_size = rank // SQUARE + 128
    kv_dims = (count // 2, 2 * HEAD)
    sums = [pltpu.VMEM((2, pair, rank, HEAD), F32)] if rows != block else []
    return pl.pallas_call(
        functools.partial(attend_back_kernel, pair, len(weights)),
        grid=(rows // block,),
        in_specs=[SMEM]
        + attend_specs(block, rank, count, weights)
        + [pl.BlockSpec((heads, block, 2 * HEAD), lambda i: (0, i, 0)), row(width)],
        out_specs=[whole(grad_dims)] * 2 + [row(d_lat_size)] * SQUARE + [whole(kv_dims)] * 2,
        out_shape=[shape(grad_dims)] * 2
        + [shape((rows, d_lat_size))] * SQUARE
        + [shape(kv_dims, BF16 if sums else F32), shape(kv_dims)],
        scratch_shapes=[
            pltpu.VMEM((count, 2 * HEAD), F32),
            pltpu.VMEM((block, rank), F32),
        ]
        + sums,
        compiler_params=params(VMEM_LIMIT + len(sums) * 2**22),
        cost_estimate=pl.CostEstimate(
            flops=2 * rows * heads * HEAD * (5 * count + 2 * rank + width),
            bytes_accessed=12 * count * HEAD + 4 * heads * HEAD * (rank + width),
            transcendentals=rows * heads * count,
        ),
        name="attend_back",
    )(at, lat, *tables, kv, keys, *weights, saved, d_attn)


def out_grads_kernel(mix_ref, d_attn_ref, *refs):
    more, out_ref = refs[:-1], refs[-1]
    for h in range(mix_ref.shape[0]):
        grad = contract_rows(mix_ref[h], d_attn_ref[...])
        here = slice(h * HEAD, (h + 1) * HEAD)
        for tile in range(out_ref.shape[0]):
            value = grad[:, tile * 128 : (tile + 1) * 128]
            if more:
                value = value + more[0][tile, here, :].astype(F32)
            out_ref[tile, here, :] = value.astype(BF16)


def out_grads(saved, side, d_attn, *received):
    rows, width = d_attn.shape
    pair = saved.shape[0] // 2
    dims = (width // 128, pair * HEAD, 128)
    whole = lambda dims: pl.BlockSpec(dims, lambda i: (0,) * len(dims))
    return pl.pallas_call(
        out_grads_kernel,
        grid=(1,),
        in_specs=[pl.BlockSpec((pair, rows, HEAD), lambda i: (side, 0, 1)), whole((rows, width))]
        + [whole(dims)] * len(received),
        out_specs=whole(dims),
        out_shape=shape(dims),
        compiler_params=params(GRADS_LIMIT),
        cost_estimate=pl.CostEstimate(
            flops=2 * rows * pair * HEAD * width, bytes_accessed=4 * pair * HEAD * width, transcendentals=0
        ),
        name="out_grads",
    )(saved, d_attn, *received)


def latent_back_kernel(layers, at_ref, hat_ref, inverse_ref, x_ref, w_ref, *refs):
    parts, d_kv_refs, d_x_refs = (refs[i * SQUARE : (i + 1) * SQUARE] for i in range(3))
    near_ref, far_ref, d_sum, d_kv_sum, d_x_sum = refs[3 * SQUARE :]
    layer, corner, core = at_ref[0], at_ref[1], at_ref[2]
    count, width = x_ref.shape
    rows = count // SQUARE
    share = w_ref.shape[-1]
    rank_share = hat_ref.shape[1] // SQUARE
    places = [pl.ds(pl.multiple_of((corner ^ m) * rows, rows), rows) for m in range(SQUARE)]
    d_sum[...] = sum(part[...].astype(F32) for part in parts)
    for place, d_kv_ref in zip(places, d_kv_refs):
        d_kv_sum[place, :] = d_kv_ref[...]
    columns = pl.ds(pl.multiple_of(corner * rank_share, rank_share), rank_share)
    dot = d_sum[:, rank_share : rank_share + 1] * (1.0 / hat_ref.shape[1])
    d_lat = inverse_ref[...] * (d_sum[:, :rank_share] - hat_ref[:, columns] * dot)
    d_down = jnp.concatenate([d_lat.astype(BF16), d_kv_sum[...]], axis=1)
    weight = w_ref[...].reshape(width, share)
    d_x_sum[...] = times_transposed(d_down, weight).astype(BF16)
    for place, d_x_ref in zip(places, d_x_refs):
        d_x_ref[...] = d_x_sum[place, :]
    grad = contract_rows(x_ref[...], d_down)
    grad = grad.reshape(layers, SQUARE, 2, near_ref.shape[2], share)
    low, high = grad[:, :, 0], grad[:, :, 1]
    near = jnp.where(core == 0, low, high)
    far = jnp.where(core == 0, high, low).astype(BF16)
    for z in range(layers):
        k = lax.rem(layer + layers - z, layers)
        near_ref[k] = near[z]
        far_ref[k] = far[z]


def latent_back(at, hat, inverse, d_kv, x, weight, parts):
    count, width = x.shape
    places, _, lane_rows, share = weight.shape
    layers = places // SQUARE
    dims = (layers, SQUARE, lane_rows, share)
    return pl.pallas_call(
        functools.partial(latent_back_kernel, layers),
        in_specs=[SMEM] + [VMEM] * (4 + 2 * SQUARE),
        out_specs=[VMEM] * (SQUARE + 2),
        out_shape=[shape((count // SQUARE, width))] * SQUARE + [shape(dims, F32), shape(dims)],
        scratch_shapes=[
            pltpu.VMEM(parts[0].shape, F32),
            pltpu.VMEM((count, d_kv[0].shape[1]), BF16),
            pltpu.VMEM((count, width), BF16),
        ],
        compiler_params=params(),
        cost_estimate=pl.CostEstimate(
            flops=4 * count * width * share, bytes_accessed=10 * width * share, transcendentals=0
        ),
        name="latent_back",
    )(at, hat, inverse, x, weight, *parts, *d_kv)


def chunk(ref, q, tiles):
    columns = [(t * SQUARE + q) * 128 for t in range(tiles)]
    return jnp.concatenate([ref[:, c : c + 128] for c in columns], axis=1)


def mlp_kernel(
    h_ref,
    cot_ref,
    near_ref,
    far_ref,
    d_h_ref,
    act_near_ref,
    act_far_ref,
    turned,
):
    tiles = near_ref.shape[1]
    units = act_near_ref.shape[1]
    for q in range(SQUARE):
        turned[0, q] = chunk(h_ref, q, tiles).T
        turned[1, q] = chunk(cot_ref, q, tiles).T

    def weight(side, kind, q):
        here = slice(kind * units, (kind + 1) * units)
        return jnp.concatenate([side[q, t, here, :] for t in range(tiles)], axis=1)

    sides = ((near_ref, act_near_ref), (far_ref, act_far_ref))
    for side, acts in sides:

        def product(which, kind):
            return sum(matmul(weight(side, kind, q), turned[which, q]) for q in range(SQUARE))

        gate_act, up_proj, d_act = product(0, 0), product(0, 1), product(1, 2)
        sigmoid_gate = 1.0 / (1.0 + jnp.exp(-gate_act))
        silu_gate = gate_act * sigmoid_gate
        d_gate = d_act * up_proj * sigmoid_gate * (1.0 + gate_act * (1.0 - sigmoid_gate))
        acts[0] = d_gate.astype(BF16)
        acts[1] = (d_act * silu_gate).astype(BF16)
        acts[2] = (silu_gate * up_proj).astype(BF16)
    straight = [[acts[kind].T for kind in range(3)] for _, acts in sides]
    for q in range(SQUARE):
        value = sum(
            matmul(straight[c][kind], weight(sides[c][0], kind, q)) for c in range(2) for kind in range(2)
        )
        for t in range(tiles):
            here = slice((t * SQUARE + q) * 128, (t * SQUARE + q + 1) * 128)
            d_h_ref[:, here] = value[:, t * 128 : (t + 1) * 128].astype(BF16)


def mlp_out_kernel(near_ref, far_ref, act_near_ref, act_far_ref, out_ref):
    tiles, units = near_ref.shape[1], act_near_ref.shape[1]
    sides = ((near_ref, act_near_ref[0].T), (far_ref, act_far_ref[0].T))
    for q in range(SQUARE):
        value = sum(
            matmul(act, jnp.concatenate([side[q, t] for t in range(tiles)], axis=1))
            for side, act in sides
        )
        for t in range(tiles):
            here = slice((t * SQUARE + q) * 128, (t * SQUARE + q + 1) * 128)
            out_ref[:, here] = value[:, t * 128 : (t + 1) * 128].astype(BF16)


def mlp_out(near, far, act_near, act_far):
    _, units, rows = act_near.shape
    tiles = near.shape[1]
    width = SQUARE * tiles * 128
    weights = pl.BlockSpec((SQUARE, tiles, units, 128), lambda i: (0, 0, 2, 0))
    acts = pl.BlockSpec((1, units, rows), lambda i: (2, 0, 0))
    return pl.pallas_call(
        mlp_out_kernel,
        grid=(1,),
        in_specs=[weights, weights, acts, acts],
        out_specs=pl.BlockSpec((rows, width), lambda i: (0, 0)),
        out_shape=shape((rows, width)),
        compiler_params=params(GRADS_LIMIT if rows <= 256 else VMEM_LIMIT),
        cost_estimate=pl.CostEstimate(
            flops=4 * rows * width * units, bytes_accessed=4 * width * units, transcendentals=0
        ),
        name="mlp_out",
    )(near, far, act_near, act_far)


def mlp(h, cot, near, far):
    rows, width = h.shape
    units = near.shape[2] // 3
    low, acts = shape((rows, width)), shape((3, units, rows))
    return pl.pallas_call(
        mlp_kernel,
        in_specs=[VMEM] * 4,
        out_specs=[VMEM] * 3,
        out_shape=[low, acts, acts],
        scratch_shapes=[pltpu.VMEM((2, SQUARE, width // SQUARE, rows), BF16)],
        compiler_params=params(MLP_LIMIT if rows <= 256 else VMEM_LIMIT),
        cost_estimate=pl.CostEstimate(
            flops=20 * rows * width * units,
            bytes_accessed=12 * width * units + 6 * rows * width,
            transcendentals=2 * rows * units,
        ),
        name="mlp",
    )(h, cot, near, far)


def unit_grads_kernel(acts_ref, value_ref, *refs):
    more, out_ref = refs[:-1], refs[-1]
    acts = acts_ref[0]
    tiles = out_ref.shape[1]
    for q in range(SQUARE):
        grad = matmul(acts, chunk(value_ref, q, tiles))
        for t in range(tiles):
            tile = grad[:, t * 128 : (t + 1) * 128]
            if more:
                tile = tile + more[0][q, t].astype(F32)
            out_ref[q, t] = tile.astype(BF16)


def unit_grads(acts, kind, value, received=None, kinds=None):
    rows, width = value.shape
    units = acts.shape[1]
    tiles = width // SQUARE // 128
    whole = lambda dims: pl.BlockSpec(dims, lambda i: (0,) * len(dims))
    dims = (SQUARE, tiles, units, 128)
    in_specs = [pl.BlockSpec((1, units, rows), lambda i: (kind, 0, 0)), whole((rows, width))]
    args, aliases, body = [acts, value], {}, unit_grads_kernel
    out_specs, out_dims = whole(dims), dims
    if received is not None:
        args.append(received)
        in_specs.append(whole(dims))
        if kind < 2:
            out_specs = pl.BlockSpec(dims, lambda i: (0, 0, kind, 0))
            out_dims = (SQUARE, tiles, 2 * units, 128)
    if kinds is not None:
        args.append(kinds)
        in_specs.append(HBM)
        aliases = {3: 0}
        body = lambda a, v, r, k, o: unit_grads_kernel(a, v, r, o)
    return pl.pallas_call(
        body,
        grid=(1,),
        in_specs=in_specs,
        out_specs=out_specs,
        out_shape=shape(out_dims),
        input_output_aliases=aliases,
        compiler_params=params(GRADS_LIMIT),
        cost_estimate=pl.CostEstimate(flops=1000, bytes_accessed=1000, transcendentals=0),
        name="unit_grads",
    )(*args)


def local(
    chips,
    tokens,
    attn_gain,
    q_gain,
    w_qdown,
    w_qup,
    w_kv,
    w_out,
    mlp_gain,
    w_gate,
    w_up,
    w_down,
    cotangent,
    seq_lengths,
    block_slots,
):
    layers = chips // SQUARE
    rows, width = tokens.shape[0] // 2, tokens.shape[1]
    lanes = width // chips
    rank = w_qdown.shape[1]
    rank_rows = w_qup.shape[0]
    pair = w_qup.shape[1] // HEAD // SQUARE
    units = w_gate.shape[1] // layers
    half = HEAD // 2
    place = lax.axis_index("seq")
    core = lax.axis_index("tp")
    layer, corner = place // SQUARE, place % SQUARE
    at = jnp.stack([layer, corner, core]).astype(jnp.int32)
    first = core == 0
    lines = [[z * SQUARE + c for z in range(layers)] for c in range(SQUARE)]
    square_groups = [[z * SQUARE + c for c in range(SQUARE)] for z in range(layers)]

    def across(value):
        return lax.ppermute(value, "tp", [(0, 1), (1, 0)])

    def along(value, step):
        pairs = [
            (z * SQUARE + c, (z + step) % layers * SQUARE + c)
            for z in range(layers)
            for c in range(SQUARE)
        ]
        return lax.ppermute(value, "seq", pairs)

    def within(value, flip):
        return lax.ppermute(value, "seq", [(i, i ^ flip) for i in range(chips)])

    def line_exchange(value):
        return lax.all_to_all(value, "seq", 0, 0, axis_index_groups=lines, tiled=True)

    def square_exchange(value):
        return lax.all_to_all(value, "seq", 0, 0, axis_index_groups=square_groups, tiled=True)

    def line_pieces(value):
        return [value] + [along(value, k) for k in range(1, layers)]

    def line_sum(blocks):
        return blocks[0].astype(F32) + sum(
            along(blocks[k], -k).astype(F32) for k in range(1, layers)
        )

    def by_layer(value):
        blocks = value.reshape(layers, rows, -1)
        return jnp.concatenate(
            [
                lax.dynamic_index_in_dim(blocks, (layer - z) % layers, 0, keepdims=False)
                for z in range(layers)
            ]
        )

    def square_pieces(value):
        return [value] + [within(value, m) for m in range(1, SQUARE)]

    def square_sum(blocks):
        return blocks[0].astype(F32) + sum(
            within(blocks[m], m).astype(F32) for m in range(1, SQUARE)
        )

    def after(value, *earlier):
        return lax.optimization_barrier((value,) + earlier)[0]

    def together(*values):
        return lax.optimization_barrier(values)

    def own(pair_value):
        return lax.dynamic_slice_in_dim(pair_value, core * rows, rows, 0)

    def both(mine, theirs, axis=0):
        return jnp.concatenate(
            [jnp.where(first, mine, theirs), jnp.where(first, theirs, mine)], axis=axis
        )

    def tiled(value):
        if lanes == 128:
            return value
        count, size, _ = value.shape
        value = jnp.swapaxes(value, 0, 1).reshape(size, count * lanes // 128, 128)
        return jnp.swapaxes(value, 0, 1)

    def untiled(value):
        if lanes == 128:
            return value
        count, size, _ = value.shape
        value = jnp.swapaxes(value, 0, 1).reshape(size, count * 128 // lanes, lanes)
        return jnp.swapaxes(value, 0, 1)

    def arranged(value):
        if lanes == 128:
            return value
        shaped = value.reshape(value.shape[0], -1, 128 // lanes, SQUARE, lanes)
        return jnp.swapaxes(shaped, 2, 3).reshape(value.shape)

    def unarranged(value):
        if lanes == 128:
            return value
        shaped = value.reshape(value.shape[0], -1, SQUARE, 128 // lanes, lanes)
        return jnp.swapaxes(shaped, 2, 3).reshape(value.shape)

    inputs = own(tokens).astype(F32)
    x_inverse = inverse_rms(inputs)
    x_hat = inputs * x_inverse
    def square_send(value):
        blocks = [
            lax.dynamic_index_in_dim(value, corner ^ m, 0, keepdims=False) for m in range(SQUARE)
        ]
        return [blocks[0]] + [within(blocks[m], m) for m in range(1, SQUARE)]

    def by_corner(pieces):
        pieces = jnp.stack(pieces)
        return jnp.stack(
            [
                lax.dynamic_index_in_dim(pieces, corner ^ q, 0, keepdims=False)
                for q in range(SQUARE)
            ]
        )

    x_low = x_hat.astype(BF16)

    gain_rows = attn_gain.astype(F32)[:, None]
    down = jnp.concatenate([w_qdown, w_kv], axis=1)
    rank_share, kv_share = rank // SQUARE, 2 * HEAD // SQUARE

    def shares(value):
        return jnp.stack(
            [
                jnp.concatenate(
                    [
                        value[:, b * rank_share : (b + 1) * rank_share],
                        value[:, rank + b * kv_share : rank + (b + 1) * kv_share],
                    ],
                    axis=1,
                )
                for b in range(SQUARE)
            ]
        )

    def unshares(value):
        return jnp.concatenate(
            [value[b, :, :rank_share] for b in range(SQUARE)]
            + [value[b, :, rank_share:] for b in range(SQUARE)],
            axis=1,
        )

    down_scaled = (down.astype(F32) * gain_rows).astype(BF16)
    down_half = lax.dynamic_slice_in_dim(down_scaled, core * (lanes // 2), lanes // 2, 0)
    cot_own = own(cotangent)
    down_own = square_exchange(shares(down_half))
    down_near = line_pieces(down_own)
    x_pieces = square_pieces(after(x_low, down_own))
    x_all = by_corner(x_pieces).reshape(-1, width)
    down_far = [across(piece) for piece in down_near]

    q_gain_rows = q_gain.astype(F32)[:, None]
    qup_scaled = (w_qup.astype(F32) * q_gain_rows).astype(BF16)
    qup_send = qup_scaled.reshape(rank_rows, SQUARE, 2 * pair, half)
    qup_send = jnp.transpose(qup_send, (1, 2, 0, 3)).reshape(SQUARE, -1, lanes)
    qup_size = qup_send.shape[1]
    head_send = jnp.concatenate([qup_send, w_out.reshape(SQUARE, pair * HEAD, lanes)], axis=1)
    head_own = by_corner(square_send(after(head_send, x_pieces[1])))

    mlp_gain_rows = mlp_gain.astype(F32)[:, None]
    gate_send = (w_gate.astype(F32) * mlp_gain_rows).astype(BF16).T
    up_send = (w_up.astype(F32) * mlp_gain_rows).astype(BF16).T
    mlp_send = jnp.concatenate(
        [value.reshape(layers, units, lanes) for value in (gate_send, up_send, w_down)], axis=1
    )

    bounds = jnp.cumsum(seq_lengths)
    starts = bounds - seq_lengths

    def layout(blocks):
        natural = (blocks[:, None] * rows + jnp.arange(rows, dtype=jnp.int32)[None, :]).reshape(-1)
        member = (natural[:, None] >= starts[None, :]) & (natural[:, None] < bounds[None, :])
        return natural, jnp.sum(jnp.where(member, starts[None, :], 0), axis=1)

    back_steps = jnp.arange(layers, dtype=jnp.int32)
    flips = jnp.arange(SQUARE, dtype=jnp.int32)
    owners = (((layer - back_steps) % layers) * SQUARE)[None, :] + (corner ^ flips)[:, None]
    square_slots = block_slots[2 * (layer * SQUARE + flips) + core]
    row_natural, row_start = layout(square_slots)
    owners = owners.reshape(-1)
    near_natural, _ = layout(block_slots[2 * owners + core])
    far_natural, _ = layout(block_slots[2 * owners + 1 - core])
    key_natural = jnp.concatenate([near_natural, far_natural])[None, :]
    cosine, sine = angles(row_natural - row_start)
    lane = jnp.arange(128, dtype=jnp.int32)[None, :]
    tables = (cosine, sine, jnp.where(lane == 0, row_natural[:, None], row_start[:, None]))

    cot_copies = jnp.tile(arranged(cot_own), (layers, 1))
    head_copies = jnp.tile(head_own, (layers, 1, 1))
    part, down_here = project(at, x_all, down_near, down_far)
    head_copies, cot_copies, *part_pieces = together(head_copies, cot_copies, *square_pieces(part))
    lat_hat, lat_low, lat_inverse, kv_own = latent(at, cosine, sine, part_pieces, rank)
    mlp_layer = line_exchange(after(mlp_send, *down_near[1:]))
    mlp_layer, head_copies, *kv_pieces = together(mlp_layer, head_copies, *line_pieces(kv_own))
    kv_line = jnp.concatenate(kv_pieces)
    mlp_near = lax.all_gather(tiled(mlp_layer), "seq", axis_index_groups=square_groups)

    head_near = line_exchange(head_copies)
    kv_near = jnp.concatenate(square_pieces(kv_line))
    kv_all = jnp.concatenate([kv_near, across(kv_near)])
    head_near, kv_all = together(head_near, kv_all)
    head_far = across(head_near)
    if lanes == 128:
        head_weights = (head_near, head_far)
    else:
        head_weights = tuple(
            side[:, :qup_size].reshape(chips, -1, half) for side in (head_near, head_far)
        ) + tuple(tiled(side[:, qup_size:]) for side in (head_near, head_far))

    block = max(32, min(SQUARE * rows, 2**30 // kv_all.shape[0] ** 2))
    saved, attn_part = attend(
        lat_low, tables, kv_all, key_natural, head_weights, pair, block
    )
    cot_lines = line_exchange(after(cot_copies, head_near))
    attn_pieces = square_send(attn_part.reshape(SQUARE, rows, width))
    mlp_near, cot_all, *attn_pieces = together(mlp_near, cot_lines, *attn_pieces)
    mlp_far = across(mlp_near)
    hidden = inputs + sum(piece.astype(F32) for piece in attn_pieces)
    h_inverse = inverse_rms(hidden)
    h_hat = hidden * h_inverse
    h_low = h_hat.astype(BF16)
    h_all = jnp.concatenate(line_pieces(arranged(h_low)))
    h_all = by_layer(h_all)

    d_h_part, acts_near, acts_far = mlp(h_all, cot_all, mlp_near, mlp_far)
    mlp_part = mlp_out(mlp_near, mlp_far, acts_near, acts_far)
    def line_blocks(value):
        return line_exchange(value.reshape(layers, rows, -1))

    def line_total(blocks):
        return unarranged(jnp.sum(blocks.astype(F32), axis=0))

    kinds = ((0, h_all), (1, h_all), (2, cot_all))
    far_grads = [unit_grads(acts_far, kind, value) for kind, value in kinds]
    d_h_lines = line_blocks(d_h_part)
    d_h_lines, acts_near, mlp_part, *far_grads = together(
        d_h_lines, acts_near, mlp_part, *far_grads
    )
    d_hscaled = line_total(d_h_lines)
    d_hidden = cot_own.astype(F32) + norm_back(d_hscaled, h_hat, h_inverse)
    mlp_grads = None
    for kind, value in kinds[:2]:
        mlp_grads = unit_grads(acts_near, kind, value, across(far_grads[kind]), mlp_grads)
    unit_sum = unit_grads(acts_near, 2, cot_all, across(far_grads[2]))
    mlp_blocks = mlp_part.reshape(layers, rows, width)
    mlp_pieces = []
    for k in range(layers):
        block_out = lax.dynamic_index_in_dim(mlp_blocks, (layer - k) % layers, 0, keepdims=False)
        mlp_pieces.append(along(after(block_out, d_h_lines), -k) if k else block_out)
    d_attn_all = square_exchange(jnp.tile(d_hidden.astype(BF16)[None], (SQUARE, 1, 1)))
    mlp_grads, unit_sum, d_attn_all, *mlp_pieces = together(
        mlp_grads, unit_sum, d_attn_all, *mlp_pieces
    )
    d_attn_all = d_attn_all.reshape(-1, width)
    gate_up_sum = lax.psum_scatter(mlp_grads, "seq", axis_index_groups=square_groups)
    unit_sum = lax.psum_scatter(unit_sum, "seq", axis_index_groups=square_groups)

    received = across(out_grads(saved, 1, d_attn_all))
    grad_out_total = untiled(out_grads(saved, 0, d_attn_all, received))
    head_out_lines = line_exchange(grad_out_total)
    mlp_own = unarranged(sum(piece.astype(F32) for piece in mlp_pieces))
    layer_out_own = (hidden + mlp_own).astype(BF16)
    layer_out = both(layer_out_own, across(layer_out_own))
    grad_q_near, grad_q_far, *d_lat_parts, d_kv_near, d_kv_far = attend_back(
        at,
        lat_low,
        tables,
        kv_all,
        key_natural,
        head_weights,
        saved,
        d_attn_all,
        pair,
        block,
    )
    d_kv_low = (d_kv_near.astype(F32) + across(d_kv_far).astype(F32)).astype(BF16)
    d_kv_line = square_sum(d_kv_low.reshape(SQUARE, layers * rows, 2 * HEAD)).astype(BF16)
    grad_q_total = (grad_q_near.astype(F32) + across(grad_q_far).astype(F32)).astype(BF16)
    grad_q_total = grad_q_total.reshape(chips, -1, lanes)
    d_kv_blocks = d_kv_line.reshape(layers, rows, 2 * HEAD)
    d_kv_blocks = [d_kv_blocks[0]] + [along(d_kv_blocks[k], -k) for k in range(1, layers)]
    head_out_lines, grad_q_total, *d_kv_blocks = together(head_out_lines, grad_q_total, *d_kv_blocks)
    d_kv_own = sum(block.astype(F32) for block in d_kv_blocks)
    own_cosine = lax.dynamic_slice_in_dim(cosine, corner * rows, rows, 0)
    own_sine = lax.dynamic_slice_in_dim(sine, corner * rows, rows, 0)
    d_kv_own = jnp.concatenate(
        [unrotate(d_kv_own[:, :HEAD], own_cosine, own_sine), d_kv_own[:, HEAD:]], axis=1
    ).astype(BF16)
    head_q = line_exchange(grad_q_total)
    kv_share_of = lambda m: lax.dynamic_slice_in_dim(d_kv_own, (corner ^ m) * kv_share, kv_share, 1)
    d_kv_share = [kv_share_of(0)] + [within(kv_share_of(m), m) for m in range(1, SQUARE)]
    d_lat_received = [d_lat_parts[0]] + [within(d_lat_parts[m], m) for m in range(1, SQUARE)]
    head_q, *d_lat_received = together(head_q, *d_lat_received)

    *d_x_blocks, down_grad_near, down_grad_far = latent_back(
        at, lat_hat, lat_inverse, d_kv_share, x_all, down_here, d_lat_received
    )
    d_x_received = [within(d_x_blocks[m], m) for m in range(1, SQUARE)]
    down_sum = (down_grad_near + across(down_grad_far).astype(F32)).astype(BF16)

    gate_up_raw = line_exchange(untiled(after(gate_up_sum, head_q)))
    head_sum = jnp.concatenate(
        [
            jnp.sum(blocks.reshape(layers, SQUARE, -1, lanes).astype(F32), axis=0).astype(BF16)
            for blocks in (head_q, head_out_lines)
        ],
        axis=1,
    )
    head_pieces = square_send(head_sum)
    down_blocks = [down_sum[k] for k in range(layers)]
    down_pieces = [down_blocks[0]] + [along(down_blocks[k], -k) for k in range(1, layers)]
    gate_up_back, *received = together(gate_up_raw, *d_x_received, *down_pieces)
    d_x_received, down_pieces = received[: SQUARE - 1], received[SQUARE - 1 :]
    d_xscaled = d_x_blocks[0].astype(F32) + sum(block.astype(F32) for block in d_x_received)
    token_own = (d_hidden + norm_back(d_xscaled, x_hat, x_inverse)).astype(BF16)
    token_grad = both(token_own, across(token_own))
    unit_back = line_exchange(untiled(after(unit_sum, gate_up_raw)))
    down_line = sum(piece.astype(F32) for piece in down_pieces)
    down_pieces = square_send(down_line.astype(BF16))
    unit_back, *received = together(unit_back, *down_pieces, *head_pieces)
    down_pieces, head_pieces = received[:SQUARE], received[SQUARE:]
    head_sum = by_corner(head_pieces)
    down_back = unshares(by_corner(down_pieces)).astype(F32)
    down_back = both(down_back, across(down_back))
    attn_gain_part = jnp.sum(down_back * down.astype(F32), axis=1)
    down_grad = down_back * gain_rows
    qdown_part, kv_part = down_grad[:, :rank], down_grad[:, rank:]

    gate_back, up_back, down_part = (
        value.reshape(layers * units, lanes).astype(F32)
        for value in (gate_up_back[:, :units], gate_up_back[:, units:], unit_back)
    )
    gate_back, up_back = gate_back.T, up_back.T
    gate_part, up_part = gate_back * mlp_gain_rows, up_back * mlp_gain_rows
    mlp_gain_part = jnp.sum(gate_back * w_gate.astype(F32) + up_back * w_up.astype(F32), axis=1)

    qup_back = head_sum[:, :qup_size].reshape(SQUARE, 2 * pair, rank_rows, half)
    qup_back = jnp.transpose(qup_back, (2, 0, 1, 3)).reshape(rank_rows, -1).astype(F32)
    out_part = head_sum[:, qup_size:].reshape(-1, lanes).astype(F32)
    qup_part = qup_back * q_gain_rows
    q_gain_half = jnp.sum(qup_back * w_qup.astype(F32), axis=1)
    gain_parts = jnp.concatenate([q_gain_half, mlp_gain_part])
    gain_parts = gain_parts + across(gain_parts)
    q_gain_part, mlp_gain_part = gain_parts[:rank_rows], gain_parts[rank_rows:]
    return (
        layer_out,
        token_grad,
        attn_gain_part,
        q_gain_part,
        qdown_part,
        qup_part,
        kv_part,
        out_part,
        mlp_gain_part,
        gate_part,
        up_part,
        down_part,
    )


def solution(mesh):
    in_specs = (
        P("seq", None),
        P("seq"),
        P("seq"),
        P("seq", None),
        P("seq", "tp"),
        P("seq", None),
        P("tp", "seq"),
        P("seq"),
        P("seq", "tp"),
        P("seq", "tp"),
        P("tp", "seq"),
        P("seq", None),
        P(),
        P(),
    )
    out_specs = (
        P("seq", None),
        P("seq", None),
        P("seq"),
        P("seq"),
        P("seq", None),
        P("seq", "tp"),
        P("seq", None),
        P("tp", "seq"),
        P("seq"),
        P("seq", "tp"),
        P("seq", "tp"),
        P("tp", "seq"),
    )
    body = functools.partial(local, mesh.shape["seq"])
    return jax.shard_map(body, mesh=mesh, in_specs=in_specs, out_specs=out_specs, check_vma=False)
```
